128 devices in a mesh: rows: 32 (over z, x_hi, y), tp: 4 (over x_lo, core).
Axes of the slice: x: 4 (x_hi: 2, x_lo: 2; x = x_hi * 2 + x_lo), y: 4, z: 4, core: 2. Of those that a mesh axis runs over, the one named last changes fastest.
Arguments:
- tokens: int32 [4, 128], P(None, 'rows'), may hold values from 0 to 76031
- lengths: int32 [128], P('rows'), may hold values from 256 to 1024, as said below
- embedding: bfloat16 [76032, 32, 256], P(None, 'rows', 'tp')
- attn_gain: bfloat16 [8192], P('tp'), may hold values from 0.099609375 to 1.8984375
- key_weight: bfloat16 [8192, 1024], P('tp')
- value_weight: bfloat16 [8192, 1024], P('tp'), may hold values from -0.0625 to 0.0625
- policy_keys: bfloat16 [128, 1024, 1024], P('rows', None, 'tp')
- policy_values: bfloat16 [128, 1024, 1024], P('rows', None, 'tp'), may hold values from -6 to 6
- critic_lengths: int32 [128], P('rows'), may hold values from 256 to 1024, as said below
- critic_gain: bfloat16 [8192], P('tp'), may hold values from 0.099609375 to 1.8984375
- critic_keys: bfloat16 [128, 1024, 1024], P('rows', None, 'tp')
- critic_values: bfloat16 [128, 1024, 1024], P('rows', None, 'tp'), may hold values from -6 to 6
- value_gain: bfloat16 [8192], P('tp'), may hold values from 0.099609375 to 1.8984375
- value_head: bfloat16 [8192, 51], P('tp')
Outputs:
- policy_hidden: bfloat16 [4, 128, 8192], P(None, 'rows', 'tp')
- values: float32 [4, 128], P(None, 'rows')
The draws below stay inside these ranges and needn't reach their ends.
Inputs may be any that keep to these rules, and one draw needn't show every extreme that they name: `lengths`: positions at or past a row's length are unused; the first row of each block of 4 rows has length 1024. `critic_lengths`: positions at or past a row's length are unused; the first row of each block of 4 rows has length 1024.
All inputs are finite; a program needn't handle non-finite values.
Results may differ from the reference program's by a relative error of at most 0.038.
Values may be sent and summed in bfloat16 or wider, within the bound.
No kernel may reach another device: no remote copies, remote signals or barrier semaphores. Data moves between devices by JAX's collectives and lax.ppermute only.
A program may use at most 128 MiB of HBM per device.

```python
import math
import jax
import jax.numpy as jnp
from jax import lax

D = 8192
HEADS = 64
KV_HEADS = 8
HEAD_DIM = 128
VOCAB = 76032
ATOMS = 51
STEPS = 4
ROWS_DEV = 4
CACHE_LEN = 1024
ROWS = 128
EMB_COLS = 256
N_ROWS = 32
N_TP = 4


def ragged(key):
    drawn = jax.random.randint(key, (ROWS,), CACHE_LEN // 4, CACHE_LEN + 1)
    leaders = jnp.arange(ROWS) % ROWS_DEV == 0
    return jnp.where(leaders, CACHE_LEN, drawn).astype(jnp.int32)


def rising(columns, rise):
    block_width = max(columns // N_TP, 1)
    block = (lax.broadcasted_iota(jnp.int32, (columns,), 0) // block_width).astype(jnp.float32)
    return jnp.exp(math.log(rise) * block / max(N_TP - 1, 1))


def token_quarters(key, spread):
    quarter_width = max(EMB_COLS // N_TP, 1)
    levels = jax.random.uniform(key, (VOCAB, N_TP), jnp.float32, -spread, spread)
    return jnp.repeat(jnp.exp(levels), quarter_width, axis=1)


def draw_lengths(key, part):
    key = jax.random.fold_in(key, 5)
    return ragged(key)


def draw_critic_lengths(key, part):
    key = jax.random.fold_in(key, 7)
    return ragged(key)


def draw_embedding(key, part):
    key = jax.random.fold_in(key, 19)
    base = jax.random.normal(jax.random.fold_in(key, 1), (VOCAB, N_ROWS, EMB_COLS), jnp.float32)
    base = jnp.clip(base, -6.0, 6.0)
    factors = rising(EMB_COLS, 3.0)
    per_token = token_quarters(jax.random.fold_in(key, 2), 1.0)
    return (base * factors[None, None, :] * per_token[:, None, :]).astype(jnp.bfloat16)


def draw_key_weight(key, part):
    key = jax.random.fold_in(key, 23)
    width = KV_HEADS * HEAD_DIM
    group_size = HEADS // KV_HEADS
    base = jax.random.normal(jax.random.fold_in(key, 1), (D, width), jnp.float32) / math.sqrt(D)
    feature = lax.broadcasted_iota(jnp.int32, (D, width), 0)
    column = lax.broadcasted_iota(jnp.int32, (D, width), 1)
    target = feature // HEAD_DIM // group_size * HEAD_DIM + feature % HEAD_DIM
    linked = 5.0 / math.sqrt(HEAD_DIM)
    return jnp.where(column == target, base + linked, base).astype(jnp.bfloat16)


def draw_policy_keys(key, part):
    key = jax.random.fold_in(key, 11)
    base = jax.random.normal(jax.random.fold_in(key, 1), (ROWS, CACHE_LEN, KV_HEADS * HEAD_DIM), jnp.float32)
    return base.astype(jnp.bfloat16)


def draw_critic_keys(key, part):
    key = jax.random.fold_in(key, 13)
    base = 3.0 * jax.random.normal(jax.random.fold_in(key, 1), (ROWS, CACHE_LEN, KV_HEADS * HEAD_DIM), jnp.float32)
    return base.astype(jnp.bfloat16)


def draw_value_head(key, part):
    key = jax.random.fold_in(key, 17)
    weights = jax.random.normal(jax.random.fold_in(key, 1), (D, ATOMS), jnp.float32) * (3.0 / math.sqrt(D))
    return weights.astype(jnp.bfloat16)


def set_ends(values, rng, smallest, largest):
    extent = values.shape
    place = [jax.random.randint(jax.random.fold_in(rng, axis), (), 0, extent[axis]) for axis in range(len(extent))]
    values = values.at[tuple(place)].set(smallest)
    longest = extent.index(max(extent))
    place[longest] = (place[longest] + 1) % extent[longest]
    return values.at[tuple(place)].set(largest)


def steps_of(own_key, extent, shards, low, high):
    loudness = 1.0
    for axis_at, blocks in shards:
        steps = jax.random.uniform(jax.random.fold_in(jax.random.fold_in(own_key, 6), axis_at), (blocks,), jnp.float32, low / len(shards), high / len(shards))
        loudness = loudness * jnp.repeat(jnp.exp(steps), extent[axis_at] // blocks).reshape((-1,) + (1,) * (len(extent) - 1 - axis_at))
    return loudness


def centred(stream_key, dims, scale, reach, cuts=(), kind=jnp.bfloat16):
    factor_of = steps_of(stream_key, dims, cuts, -0.22, 0.18) if cuts else 1.0
    values = jax.random.normal(stream_key, dims, jnp.float32) * scale * factor_of
    return jnp.minimum(jnp.maximum(values, -reach), reach).astype(kind)


def setup_inputs(seed: int = 0) -> dict:
    seeds = jax.random.split(jax.random.key(seed), 15)
    return {
        "tokens": set_ends(jax.random.randint(seeds[0], (STEPS, ROWS), 0, VOCAB), jax.random.fold_in(seeds[0], 1), 0, VOCAB - 1).astype(jnp.int32),
        "lengths": draw_lengths(jax.random.fold_in(seeds[14], 71), 0),
        "embedding": draw_embedding(jax.random.fold_in(seeds[14], 71), 0),
        "attn_gain": jnp.clip(1.0 + 0.18 * jax.random.normal(seeds[3], (D,), jnp.float32), 0.099609375, 1.8984375).astype(jnp.bfloat16),
        "key_weight": draw_key_weight(jax.random.fold_in(seeds[14], 71), 0),
        "value_weight": centred(seeds[5], (D, KV_HEADS * HEAD_DIM), D ** -0.5, 0.0625, ((0, 4),)),
        "policy_keys": draw_policy_keys(jax.random.fold_in(seeds[14], 71), 0),
        "policy_values": centred(seeds[7], (ROWS, CACHE_LEN, KV_HEADS * HEAD_DIM), 1.0, 6.0, ((0, 32), (2, 4))),
        "critic_lengths": draw_critic_lengths(jax.random.fold_in(seeds[14], 71), 0),
        "critic_gain": jnp.clip(1.0 + 0.18 * jax.random.normal(seeds[9], (D,), jnp.float32), 0.099609375, 1.8984375).astype(jnp.bfloat16),
        "critic_keys": draw_critic_keys(jax.random.fold_in(seeds[14], 71), 0),
        "critic_values": centred(seeds[11], (ROWS, CACHE_LEN, KV_HEADS * HEAD_DIM), 1.0, 6.0, ((0, 32), (2, 4))),
        "value_gain": jnp.clip(1.0 + 0.18 * jax.random.normal(seeds[12], (D,), jnp.float32), 0.099609375, 1.8984375).astype(jnp.bfloat16),
        "value_head": draw_value_head(jax.random.fold_in(seeds[14], 71), 0),
    }


norm_eps = 1e-06
atom_span = 10.0

def attend(query, keys, values, lengths, extra_keys, extra_values):
    row_count = query.shape[0]
    cache_size = keys.shape[1]
    kv_count = keys.shape[2] // HEAD_DIM
    group_size = query.shape[1] // HEAD_DIM // kv_count
    scale = 1.0 / math.sqrt(HEAD_DIM)
    grouped = query.reshape(row_count, kv_count, group_size, HEAD_DIM).astype(jnp.float32)
    cache_keys = keys.reshape(row_count, cache_size, kv_count, HEAD_DIM).astype(jnp.float32)
    scores = jnp.einsum('rkgd,rtkd->rkgt', grouped, cache_keys) * scale
    visible = lax.broadcasted_iota(jnp.int32, (row_count, cache_size), 1) < lengths[:, None].astype(jnp.int32)
    scores = jnp.where(visible[:, None, None, :], scores, -1e+30)
    highest = lax.optimization_barrier(jnp.max(scores, axis=-1))
    if extra_keys is not None:
        count = extra_keys.shape[1]
        fresh_keys = extra_keys.reshape(row_count, count, kv_count, HEAD_DIM).astype(jnp.float32)
        extra_scores = jnp.einsum('rkgd,rtkd->rkgt', grouped, fresh_keys) * scale
        highest = jnp.maximum(highest, lax.optimization_barrier(jnp.max(extra_scores, axis=-1)))
    weights = jnp.exp(scores - highest[..., None])
    totals = lax.optimization_barrier(jnp.sum(weights, axis=-1))
    if extra_keys is not None:
        extra_weights = jnp.exp(extra_scores - highest[..., None])
        totals = totals + lax.optimization_barrier(jnp.sum(extra_weights, axis=-1))
    inverse = 1.0 / totals
    probs = (weights * inverse[..., None]).astype(jnp.bfloat16)
    cache_values = values.reshape(row_count, cache_size, kv_count, HEAD_DIM).astype(jnp.float32)
    attended = jnp.einsum('rkgt,rtkd->rkgd', probs.astype(jnp.float32), cache_values)
    if extra_keys is not None:
        extra_probs = (extra_weights * inverse[..., None]).astype(jnp.bfloat16)
        fresh_values = extra_values.reshape(row_count, count, kv_count, HEAD_DIM).astype(jnp.float32)
        attended = attended + jnp.einsum('rkgt,rtkd->rkgd', extra_probs.astype(jnp.float32), fresh_values)
    return attended.reshape(row_count, -1)

def reference(tokens, lengths, embedding, attn_gain, key_weight, value_weight, policy_keys, policy_values, critic_lengths, critic_gain, critic_keys, critic_values, value_gain, value_head):
    row_count = tokens.shape[1]
    block_cols = D // (N_ROWS * N_TP)
    atom_index = lax.broadcasted_iota(jnp.int32, (ATOMS,), 0).astype(jnp.float32)
    atom_values = -atom_span + 2.0 * atom_span * atom_index / (ATOMS - 1)
    fresh_keys = []
    fresh_values = []
    hiddens = []
    results = []
    for decode_step in range(STEPS):
        blocked = jnp.take(embedding, tokens[decode_step].astype(jnp.int32), axis=0)
        blocked = blocked.reshape(row_count, N_ROWS, N_TP, block_cols)
        picked = jnp.transpose(blocked, (0, 2, 1, 3)).reshape(row_count, D)
        picked_f = picked.astype(jnp.float32)
        inv = lax.rsqrt(lax.optimization_barrier(jnp.mean(picked_f * picked_f, axis=-1, keepdims=True)) + norm_eps)
        gained = (picked_f * attn_gain.astype(jnp.float32)).astype(jnp.bfloat16)
        new_key = (inv * jnp.dot(gained, key_weight, preferred_element_type=jnp.float32)).astype(jnp.bfloat16)
        new_value = (inv * jnp.dot(gained, value_weight, preferred_element_type=jnp.float32)).astype(jnp.bfloat16)
        query = (gained.astype(jnp.float32) * inv).astype(jnp.bfloat16)
        fresh_keys.append(new_key)
        fresh_values.append(new_value)
        attended = attend(query, policy_keys, policy_values, lengths, jnp.stack(fresh_keys, axis=1), jnp.stack(fresh_values, axis=1))
        hidden = (picked_f + attended).astype(jnp.bfloat16)
        hiddens.append(hidden)
        critic_rows = jnp.roll(hidden, -(row_count // 2), axis=0).astype(jnp.float32)
        inv_h = lax.rsqrt(lax.optimization_barrier(jnp.mean(critic_rows * critic_rows, axis=-1, keepdims=True)) + norm_eps)
        critic_query = (critic_rows * critic_gain.astype(jnp.float32) * inv_h).astype(jnp.bfloat16)
        critic_out = attend(critic_query, critic_keys, critic_values, critic_lengths, None, None)
        combined = critic_rows + critic_out
        inv_c = lax.rsqrt(lax.optimization_barrier(jnp.mean(combined * combined, axis=-1, keepdims=True)) + norm_eps)
        scaled = (combined * value_gain.astype(jnp.float32)).astype(jnp.bfloat16)
        logits = inv_c * jnp.dot(scaled, value_head, preferred_element_type=jnp.float32)
        probs = jax.nn.softmax(logits, axis=-1)
        results.append(lax.optimization_barrier(jnp.sum(probs * atom_values[None, :], axis=-1)))
    return (jnp.stack(hiddens, axis=0), jnp.stack(results, axis=0))
```

```python
import math

import jax
import jax.numpy as jnp
from jax import lax
from jax.experimental import pallas as pl
from jax.experimental.pallas import tpu as pltpu
from jax.sharding import PartitionSpec as P

D = 8192
HEAD_DIM = 128
ATOMS = 51
LANES = 128

norm_eps = 1e-06
atom_span = 10.0


def pick_rows_kernel(token_ref, table_ref, out_ref):
    width = table_ref.shape[0]
    groups = out_ref.shape[0] // LANES
    lane = lax.broadcasted_iota(jnp.int32, (width, LANES), 1)

    def column(token, place):
        block = pl.multiple_of((token // LANES) * LANES, LANES)
        tile = table_ref[:, pl.ds(block, LANES)].astype(jnp.float32)
        shift = jnp.bitwise_and(place - token + LANES * LANES * 8, LANES - 1)
        return pltpu.roll(tile, shift, 1)

    for group in range(groups):

        def step(place, carry):
            first, second = carry
            base = (group * (LANES // 8) + place // 8) * 16 + place % 8
            here = lane == place
            first = jnp.where(here, column(token_ref[base], place), first)
            second = jnp.where(here, column(token_ref[base + 8], place), second)
            return first, second

        empty = jnp.zeros((width, LANES), jnp.float32)
        first, second = lax.fori_loop(0, LANES, step, (empty, empty), unroll=4)
        both = jnp.concatenate([first, second], axis=0)
        out_ref[pl.ds(group * LANES, LANES), :] = both.T.astype(out_ref.dtype)


def pick_rows(tokens, table):
    width = table.shape[0]
    rows = tokens.shape[0] * width // LANES
    return pl.pallas_call(
        pick_rows_kernel,
        out_shape=jax.ShapeDtypeStruct((rows, LANES), table.dtype),
        in_specs=[
            pl.BlockSpec(memory_space=pltpu.SMEM),
            pl.BlockSpec(memory_space=pltpu.VMEM),
        ],
        out_specs=pl.BlockSpec(memory_space=pltpu.VMEM),
        compiler_params=pltpu.CompilerParams(vmem_limit_bytes=16 * 1024 * 1024),
        name="pick_rows",
    )(tokens, table)


def swapped(shard, by):
    peers = lax.axis_size("tp")
    return lax.ppermute(shard, "tp", [(i, i ^ by) for i in range(peers)])


def passed_along(shard, axis, by):
    peers = lax.axis_size(axis)
    return lax.ppermute(shard, axis, [(i, (i + by) % peers) for i in range(peers)])


def summed(shard):
    peers = lax.axis_size("tp")
    arrived = [swapped(shard, by) for by in range(1, peers)]
    return shard + (arrived[0] + (arrived[1] + arrived[2]))


def grouped_heads(rows, row_count):
    kv_count = rows.shape[1] // (8 * HEAD_DIM)
    split = rows.reshape(row_count, -1, kv_count, 8, HEAD_DIM)
    return split.transpose(0, 2, 1, 3, 4).reshape(row_count, kv_count, -1, HEAD_DIM)


def raw_scores(grouped, keys):
    row_count, cache_size = keys.shape[:2]
    cache_keys = keys.reshape(row_count, cache_size, -1, HEAD_DIM)
    return jnp.einsum("rkgd,rtkd->rkgt", grouped, cache_keys, preferred_element_type=jnp.float32)


def on_device(
    tokens,
    lengths,
    embedding,
    attn_gain,
    key_weight,
    value_weight,
    policy_keys,
    policy_values,
    critic_lengths,
    critic_gain,
    critic_keys,
    critic_values,
    value_gain,
    value_head,
):
    steps, row_count = tokens.shape
    row_groups = lax.axis_size("rows")
    kv_width = policy_keys.shape[2]
    kv_count = kv_width // HEAD_DIM
    cache_size = policy_keys.shape[1]
    scale = 1.0 / math.sqrt(HEAD_DIM)
    count = steps * row_count
    tp = lax.axis_index("tp")

    mine = tokens.T.reshape(1, count)
    all_tokens = lax.all_to_all(
        jnp.broadcast_to(mine, (row_groups, count)), "rows", split_axis=0, concat_axis=0, tiled=True
    )
    table = embedding.transpose(1, 2, 0).reshape(embedding.shape[2], embedding.shape[0])
    picked = pick_rows(all_tokens.reshape(-1), table)
    picked = picked.reshape(row_groups, count // 2, LANES)
    blocks = lax.all_to_all(picked, "rows", split_axis=0, concat_axis=0, tiled=True)
    blocks = blocks.reshape(row_groups, count // 2, 2, LANES // 2)
    x = blocks.transpose(2, 1, 0, 3).reshape(count, -1)

    picked_f = x.astype(jnp.float32)
    gained = (picked_f * attn_gain.astype(jnp.float32)).astype(jnp.bfloat16)
    part_keys = jnp.dot(gained, key_weight, preferred_element_type=jnp.float32)
    part_values = jnp.dot(gained, value_weight, preferred_element_type=jnp.float32)
    squares = jnp.sum(picked_f * picked_f, axis=-1)

    def piece(by):
        at = (tp ^ by) * kv_width
        return jnp.concatenate(
            [
                lax.dynamic_slice_in_dim(part_keys, at, kv_width, 1),
                lax.dynamic_slice_in_dim(part_values, at, kv_width, 1),
                jnp.broadcast_to(squares[:, None], (count, LANES)),
            ],
            axis=1,
        )

    total = piece(0)
    for by in (1, 2, 3):
        total = total + swapped(piece(by), by)
    inv = lax.rsqrt(total[:, -1:] / D + norm_eps)
    new_key = (inv * total[:, :kv_width]).astype(jnp.bfloat16)
    new_value = (inv * total[:, kv_width : 2 * kv_width]).astype(jnp.bfloat16)

    grouped = grouped_heads(gained, row_count)
    scores = raw_scores(grouped, policy_keys)
    inv_rows = jnp.repeat(inv.reshape(row_count, 1, steps, 1), 8, axis=2) * scale
    visible = lax.broadcasted_iota(jnp.int32, (row_count, cache_size), 1) < lengths[:, None]
    scores = jnp.where(visible[:, None, None, :], scores * inv_rows, -1e30)
    fresh_keys = new_key.reshape(row_count, steps, kv_count, HEAD_DIM)
    fresh_values = new_value.reshape(row_count, steps, kv_count, HEAD_DIM)
    extra = jnp.einsum("rkgd,rtkd->rkgt", grouped, fresh_keys, preferred_element_type=jnp.float32)
    earlier = (jnp.arange(steps)[None, :] <= jnp.arange(steps * 8)[:, None] // 8)[None, None]
    extra = jnp.where(earlier, extra * inv_rows, -1e30)
    highest = jnp.maximum(jnp.max(scores, axis=-1), jnp.max(extra, axis=-1))[..., None]
    weights = jnp.exp(scores - highest)
    extra_weights = jnp.exp(extra - highest)
    inverse = 1.0 / (jnp.sum(weights, axis=-1) + jnp.sum(extra_weights, axis=-1))[..., None]
    probs = (weights * inverse).astype(jnp.bfloat16)
    extra_probs = (extra_weights * inverse).astype(jnp.bfloat16)
    attended = jnp.einsum(
        "rkgt,rtkd->rkgd",
        probs,
        policy_values.reshape(row_count, cache_size, kv_count, HEAD_DIM),
        preferred_element_type=jnp.float32,
    ) + jnp.einsum(
        "rkgt,rtkd->rkgd", extra_probs, fresh_values, preferred_element_type=jnp.float32
    )
    attended = attended.reshape(row_count, kv_count, steps, 8 * HEAD_DIM).transpose(0, 2, 1, 3)
    hidden = (picked_f + attended.reshape(count, -1)).astype(jnp.bfloat16)

    arrived = passed_along(hidden, "rows", row_groups // 2)
    critic_rows = arrived.astype(jnp.float32)
    squares_h = summed(
        jnp.broadcast_to(jnp.sum(critic_rows * critic_rows, axis=-1)[:, None], (count, LANES))
    )[:, :1]
    gained_h = (critic_rows * critic_gain.astype(jnp.float32)).astype(jnp.bfloat16)
    scores = raw_scores(grouped_heads(gained_h, row_count), critic_keys)
    inv_h = lax.rsqrt(squares_h / D + norm_eps)
    inv_rows = jnp.repeat(inv_h.reshape(row_count, 1, steps, 1), 8, axis=2) * scale
    visible = lax.broadcasted_iota(jnp.int32, (row_count, cache_size), 1) < critic_lengths[:, None]
    scores = jnp.where(visible[:, None, None, :], scores * inv_rows, -1e30)
    weights = jnp.exp(scores - jnp.max(scores, axis=-1, keepdims=True))
    probs = (weights / jnp.sum(weights, axis=-1, keepdims=True)).astype(jnp.bfloat16)
    critic_out = jnp.einsum(
        "rkgt,rtkd->rkgd",
        probs,
        critic_values.reshape(row_count, cache_size, kv_count, HEAD_DIM),
        preferred_element_type=jnp.float32,
    )
    critic_out = critic_out.reshape(row_count, kv_count, steps, 8 * HEAD_DIM).transpose(0, 2, 1, 3)
    combined = critic_rows + critic_out.reshape(count, -1)
    scaled = (combined * value_gain.astype(jnp.float32)).astype(jnp.bfloat16)
    part_logits = jnp.dot(scaled, value_head, preferred_element_type=jnp.float32)
    squares_c = jnp.sum(combined * combined, axis=-1, keepdims=True)
    full = summed(jnp.concatenate([part_logits, squares_c], axis=1))
    logits = lax.rsqrt(full[:, ATOMS:] / D + norm_eps) * full[:, :ATOMS]
    atom_index = lax.broadcasted_iota(jnp.int32, (ATOMS,), 0).astype(jnp.float32)
    atom_values = -atom_span + 2.0 * atom_span * atom_index / (ATOMS - 1)
    probs = jax.nn.softmax(logits, axis=-1)
    values = jnp.sum(probs * atom_values[None, :], axis=-1)
    return (
        hidden.reshape(row_count, steps, -1).transpose(1, 0, 2),
        values.reshape(row_count, steps).T,
    )


def solution(mesh):
    placed = (
        P(None, "rows"),
        P("rows"),
        P(None, "rows", "tp"),
        P("tp"),
        P("tp", None),
        P("tp", None),
        P("rows", None, "tp"),
        P("rows", None, "tp"),
        P("rows"),
        P("tp"),
        P("rows", None, "tp"),
        P("rows", None, "tp"),
        P("tp"),
        P("tp", None),
    )
    return jax.shard_map(
        on_device,
        mesh=mesh,
        in_specs=placed,
        out_specs=(P(None, "rows", "tp"), P(None, "rows")),
        check_vma=False,
    )
```

```python
import functools
import math

import jax
import jax.numpy as jnp
from jax import lax
from jax.experimental import pallas as pl
from jax.experimental.pallas import tpu as pltpu
from jax.sharding import PartitionSpec as P

D = 8192
HEAD_DIM = 128
GROUP = 8
ATOMS = 51
LANES = 128
HALF = 64
MIB = 1024 * 1024

norm_eps = 1e-06
atom_span = 10.0
masked = -1e30
attn_scale = 1.0 / math.sqrt(HEAD_DIM)

SMEM = pl.BlockSpec(memory_space=pltpu.SMEM)
VMEM = pl.BlockSpec(memory_space=pltpu.VMEM)
NT = (((1,), (1,)), ((), ()))


def kernel_call(body, outs, specs, scratch=(), limit=16, flops=0, moved=0, name=None):
    return pl.pallas_call(
        body,
        out_shape=outs,
        in_specs=specs,
        out_specs=jax.tree.map(lambda _: VMEM, outs),
        scratch_shapes=scratch,
        compiler_params=pltpu.CompilerParams(vmem_limit_bytes=limit * MIB),
        cost_estimate=pl.CostEstimate(flops=flops, bytes_accessed=moved, transcendentals=0),
        name=name,
    )


def array(shape, dtype):
    return jax.ShapeDtypeStruct(shape, dtype)


def pick_rows_kernel(token_ref, table_ref, out_ref):
    width = table_ref.shape[0]
    lane = lax.broadcasted_iota(jnp.int32, (width, LANES), 1)

    def column(token, place):
        block = pl.multiple_of(jnp.bitwise_and(token, ~(LANES - 1)), LANES)
        tile = table_ref[:, pl.ds(block, LANES)].astype(jnp.float32)
        return pltpu.roll(tile, jnp.bitwise_and(place - token, LANES - 1), 1)

    for group in range(out_ref.shape[0] // LANES):

        def step(place, carry):
            first, second = carry
            destination = group * (LANES // 8) + lax.shift_right_logical(place, 3)
            decode_step = jnp.bitwise_and(place, 3)
            row = jnp.bitwise_and(lax.shift_right_logical(place, 2), 1)
            here = lane == place
            first = jnp.where(here, column(token_ref[destination, decode_step, row], place), first)
            second = jnp.where(
                here, column(token_ref[destination, decode_step, row + 2], place), second
            )
            return first, second

        empty = jnp.zeros((width, LANES), jnp.float32)
        first, second = lax.fori_loop(0, LANES, step, (empty, empty), unroll=32)
        both = jnp.concatenate([first, second], axis=0)
        out_ref[pl.ds(group * LANES, LANES), :] = both.T.astype(out_ref.dtype)


def pick_rows(tokens, table):
    rows = tokens.size * table.shape[0] // LANES
    return kernel_call(
        pick_rows_kernel, array((rows, LANES), table.dtype), [SMEM, VMEM], name="pick_rows"
    )(tokens, table)


def project_kernel(
    tp_ref, blocks_ref, gain_ref, key_ref, value_ref, x_ref, query_ref, *rest
):
    parts, (gained_ref, placed_ref) = rest[:4], rest[4:]
    count, width = x_ref.shape
    kv_width = key_ref.shape[1] // 4
    left = lax.broadcasted_iota(jnp.int32, (8, LANES), 1) < HALF
    squares = jnp.zeros((count, LANES), jnp.float32)
    for k in range(width // LANES):
        pair = blocks_ref[pl.ds(16 * k, 16), :].astype(jnp.float32)
        one, two = pair[:8], pair[8:]
        low = jnp.where(left, one, pltpu.roll(two, HALF, 1))
        high = jnp.where(left, pltpu.roll(one, HALF, 1), two)
        x = jnp.concatenate([low, high], axis=0)
        squares += x * x
        columns = pl.ds(k * LANES, LANES)
        x_ref[:, columns] = x.astype(x_ref.dtype)
        gained = x * gain_ref[:, columns]
        gained_ref[:, columns] = gained.astype(gained_ref.dtype)
        head, group = divmod(k, GROUP)
        for row in range(4):
            placed_ref[2 * row + head, pl.ds(4 * group, 4), :] = gained[4 * row : 4 * row + 4]
    query_ref[...] = placed_ref[...].astype(query_ref.dtype)
    total = jnp.broadcast_to(jnp.sum(squares, axis=1, keepdims=True), (count, LANES))
    gained = gained_ref[...]
    for by, part_ref in enumerate(parts):
        start = pl.multiple_of(jnp.bitwise_xor(tp_ref[0], by) * kv_width, kv_width)
        peer = pl.ds(start, kv_width)
        part_ref[:, :kv_width] = jnp.dot(
            gained, key_ref[:, peer], preferred_element_type=jnp.float32
        )
        part_ref[:, kv_width : 2 * kv_width] = jnp.dot(
            gained, value_ref[:, peer], preferred_element_type=jnp.float32
        )
        part_ref[:, 2 * kv_width :] = total


def project(tp, blocks, gain, key_weight, value_weight):
    width, kv_all = key_weight.shape
    count = blocks.shape[0] * LANES // width
    part = array((count, kv_all // 2 + LANES), jnp.float32)
    heads = width // (GROUP * HEAD_DIM)
    queries = (4 * heads, 4 * GROUP, HEAD_DIM)
    x, query, *parts = kernel_call(
        project_kernel,
        (array((count, width), jnp.bfloat16), array(queries, jnp.bfloat16)) + (part,) * 4,
        [SMEM] + [VMEM] * 4,
        scratch=[pltpu.VMEM((count, width), jnp.bfloat16), pltpu.VMEM(queries, jnp.float32)],
        flops=4 * count * width * kv_all,
        moved=4 * width * kv_all,
        name="project",
    )(tp, blocks, gain, key_weight, value_weight)
    return x, query, parts


def scores_kernel(query_ref, keys_ref, out_ref):
    for at in range(query_ref.shape[0]):
        row, head = divmod(at, 2)
        keys = keys_ref[row, :, pl.ds(head * HEAD_DIM, HEAD_DIM)]
        out_ref[at] = lax.dot_general(
            query_ref[at], keys, NT, preferred_element_type=jnp.float32
        )


def raw_scores(query, keys, name):
    out = array(query.shape[:2] + (keys.shape[1],), jnp.float32)
    return kernel_call(
        scores_kernel,
        out,
        [VMEM, VMEM],
        flops=2 * out.size * HEAD_DIM,
        moved=2 * keys.size + 4 * out.size,
        name=name,
    )(query, keys)


def spread_rows(inv, spread_ref):
    for row in range(4):
        for group in range(GROUP):
            spread_ref[row, pl.ds(4 * group, 4), :] = inv[4 * row : 4 * row + 4]


def scaled_scores(raw, spread, length):
    wide = jnp.concatenate([spread] * (raw.shape[1] // LANES), axis=1)
    visible = lax.broadcasted_iota(jnp.int32, raw.shape, 1) < length
    return jnp.where(visible, raw * wide, masked)


def policy_kernel(
    length_ref,
    own_ref,
    one_ref,
    two_ref,
    three_ref,
    raw_ref,
    query_ref,
    x_ref,
    values_ref,
    passed_ref,
    squares_ref,
    hidden_ref,
    spread_ref,
    rows_ref,
):
    count, width = x_ref.shape
    kv_width = values_ref.shape[2]
    total = own_ref[...] + (one_ref[...] + (two_ref[...] + three_ref[...]))
    inv = lax.rsqrt(total[:, 2 * kv_width :] * (1.0 / D) + norm_eps)
    wide = jnp.concatenate([inv] * (kv_width // LANES), axis=1)
    new_key = (wide * total[:, :kv_width]).astype(jnp.bfloat16)
    new_value = (wide * total[:, kv_width : 2 * kv_width]).astype(jnp.bfloat16)
    spread_rows(inv * attn_scale, spread_ref)
    queries = query_ref.shape[1]
    query_step = jnp.bitwise_and(lax.broadcasted_iota(jnp.int32, (queries, count), 0), 3)
    fresh = lax.broadcasted_iota(jnp.int32, (queries, count), 1)
    earlier = jnp.bitwise_and(fresh, 3) <= query_step
    for at in range(query_ref.shape[0]):
        row, head = divmod(at, 2)
        columns = slice(head * HEAD_DIM, (head + 1) * HEAD_DIM)
        spread = spread_ref[row]
        scores = scaled_scores(raw_ref[at], spread, length_ref[row])
        extra = lax.dot_general(
            query_ref[at], new_key[:, columns], NT, preferred_element_type=jnp.float32
        )
        mine = jnp.logical_and(lax.shift_right_logical(fresh, 2) == row, earlier)
        extra = jnp.where(mine, extra * spread[:, :count], masked)
        highest = jnp.maximum(
            jnp.max(scores, axis=1, keepdims=True), jnp.max(extra, axis=1, keepdims=True)
        )
        weights = jnp.exp(scores - highest)
        extra = jnp.exp(extra - highest)
        inverse = 1.0 / (
            jnp.sum(weights, axis=1, keepdims=True) + jnp.sum(extra, axis=1, keepdims=True)
        )
        attended = jnp.dot(
            weights.astype(jnp.bfloat16),
            values_ref[row, :, columns],
            preferred_element_type=jnp.float32,
        ) + jnp.dot(
            extra.astype(jnp.bfloat16), new_value[:, columns], preferred_element_type=jnp.float32
        )
        attended = attended * inverse
        for group in range(GROUP):
            rows_ref[head * GROUP + group, pl.ds(4 * row, 4), :] = attended[
                4 * group : 4 * group + 4
            ]
    squares = jnp.zeros((count, LANES), jnp.float32)
    for k in range(width // LANES):
        columns = pl.ds(k * LANES, LANES)
        hidden = (x_ref[:, columns].astype(jnp.float32) + rows_ref[k]).astype(jnp.bfloat16)
        passed_ref[:, columns] = hidden
        hidden = hidden.astype(jnp.float32)
        squares += hidden * hidden
        rows_ref[k] = hidden
    squares_ref[...] = jnp.broadcast_to(
        jnp.sum(squares, axis=1, keepdims=True), squares_ref.shape
    )
    for step in range(4):
        for k in range(width // LANES):
            columns = pl.ds(k * LANES, LANES)
            hidden_ref[step, :, columns] = rows_ref[k, pl.ds(step, 4, stride=4), :].astype(
                hidden_ref.dtype
            )


def policy(lengths, parts, raw, query, x, values):
    count, width = x.shape
    return kernel_call(
        policy_kernel,
        (
            array((count, width), jnp.bfloat16),
            array((count, LANES), jnp.float32),
            array((4, 4, width), jnp.bfloat16),
        ),
        [SMEM] + [VMEM] * 8,
        scratch=[
            pltpu.VMEM((4, 4 * GROUP, LANES), jnp.float32),
            pltpu.VMEM((width // LANES, count, LANES), jnp.float32),
        ],
        flops=2 * raw.size * HEAD_DIM,
        moved=2 * values.size + 4 * raw.size,
        name="policy",
    )(lengths, *parts, raw, query, x, values)


def critic_scores_kernel(rows_ref, gain_ref, keys_ref, out_ref, placed_ref):
    for k in range(rows_ref.shape[1] // LANES):
        columns = pl.ds(k * LANES, LANES)
        gained = rows_ref[:, columns].astype(jnp.float32) * gain_ref[:, columns]
        head, group = divmod(k, GROUP)
        for row in range(4):
            placed_ref[2 * row + head, pl.ds(4 * group, 4), :] = gained[4 * row : 4 * row + 4]
    for at in range(placed_ref.shape[0]):
        row, head = divmod(at, 2)
        keys = keys_ref[row, :, pl.ds(head * HEAD_DIM, HEAD_DIM)]
        out_ref[at] = lax.dot_general(
            placed_ref[at].astype(jnp.bfloat16), keys, NT, preferred_element_type=jnp.float32
        )


def critic_scores(rows, gain, keys):
    heads = keys.shape[2] // HEAD_DIM
    placed = (4 * heads, 4 * GROUP, HEAD_DIM)
    out = array(placed[:2] + (keys.shape[1],), jnp.float32)
    return kernel_call(
        critic_scores_kernel,
        out,
        [VMEM] * 3,
        scratch=[pltpu.VMEM(placed, jnp.float32)],
        flops=2 * out.size * HEAD_DIM,
        moved=2 * keys.size + 4 * out.size,
        name="critic_scores",
    )(rows, gain, keys)


def critic_kernel(
    length_ref,
    own_ref,
    one_ref,
    two_ref,
    three_ref,
    raw_ref,
    rows_ref,
    gain_ref,
    values_ref,
    head_ref,
    out_ref,
    spread_ref,
    attended_ref,
    scaled_ref,
):
    count, width = rows_ref.shape
    total = own_ref[...] + (one_ref[...] + (two_ref[...] + three_ref[...]))
    spread_rows(lax.rsqrt(total * (1.0 / D) + norm_eps) * attn_scale, spread_ref)
    for at in range(raw_ref.shape[0]):
        row, head = divmod(at, 2)
        columns = slice(head * HEAD_DIM, (head + 1) * HEAD_DIM)
        scores = scaled_scores(raw_ref[at], spread_ref[row], length_ref[row])
        weights = jnp.exp(scores - jnp.max(scores, axis=1, keepdims=True))
        inverse = 1.0 / jnp.sum(weights, axis=1, keepdims=True)
        attended = inverse * jnp.dot(
            weights.astype(jnp.bfloat16),
            values_ref[row, :, columns],
            preferred_element_type=jnp.float32,
        )
        for group in range(GROUP):
            at_columns = pl.ds((head * GROUP + group) * HEAD_DIM, HEAD_DIM)
            attended_ref[pl.ds(4 * row, 4), at_columns] = attended[4 * group : 4 * group + 4]
    squares = jnp.zeros((count, LANES), jnp.float32)
    for k in range(width // LANES):
        columns = pl.ds(k * LANES, LANES)
        combined = rows_ref[:, columns].astype(jnp.float32) + attended_ref[:, columns]
        squares += combined * combined
        scaled_ref[:, columns] = (combined * gain_ref[:, columns]).astype(scaled_ref.dtype)
    logits = lax.dot_general(
        scaled_ref[...], head_ref[...], NT, preferred_element_type=jnp.float32
    )
    out_ref[...] = jnp.broadcast_to(jnp.sum(squares, axis=1, keepdims=True), (count, LANES))
    out_ref[:, :ATOMS] = logits


def critic(lengths, parts, raw, rows, gain, values, head):
    count, width = rows.shape
    return kernel_call(
        critic_kernel,
        array((count, LANES), jnp.float32),
        [SMEM] + [VMEM] * 9,
        scratch=[
            pltpu.VMEM((4, 4 * GROUP, LANES), jnp.float32),
            pltpu.VMEM((count, width), jnp.float32),
            pltpu.VMEM((count, width), jnp.bfloat16),
        ],
        flops=2 * raw.size * HEAD_DIM,
        moved=2 * values.size + 4 * raw.size,
        name="critic",
    )(lengths, *parts, raw, rows, gain, values, head)


def expect_kernel(own_ref, one_ref, two_ref, three_ref, out_ref):
    total = own_ref[...] + (one_ref[...] + (two_ref[...] + three_ref[...]))
    lane = lax.broadcasted_iota(jnp.int32, total.shape, 1)
    at = lax.broadcasted_iota(jnp.int32, total.shape, 0)
    logits = lax.rsqrt(total[:, LANES - 1 :] * (1.0 / D) + norm_eps) * total
    real = lane < ATOMS
    logits = jnp.where(real, logits, masked)
    weights = jnp.exp(logits - jnp.max(logits, axis=1, keepdims=True))
    atoms = -atom_span + 2.0 * atom_span * lane.astype(jnp.float32) / (ATOMS - 1)
    value = jnp.sum(weights * atoms, axis=1, keepdims=True) / jnp.sum(
        weights, axis=1, keepdims=True
    )
    placed = jnp.where(lane == lax.shift_right_logical(at, 2), value, 0.0)
    rows = [
        jnp.sum(jnp.where(jnp.bitwise_and(at, 3) == step, placed, 0.0), axis=0, keepdims=True)
        for step in range(4)
    ]
    out_ref[...] = jnp.concatenate(rows, axis=0)[:, :4]


def expect(parts):
    return kernel_call(expect_kernel, array((4, 4), jnp.float32), [VMEM] * 4, name="expect")(*parts)


def swapped(shard, by):
    peers = lax.axis_size("tp")
    return lax.ppermute(shard, "tp", [(i, i ^ by) for i in range(peers)])


def passed_along(shard, axis, by):
    peers = lax.axis_size(axis)
    return lax.ppermute(shard, axis, [(i, (i + by) % peers) for i in range(peers)])


def with_peers(shard):
    return [shard] + [swapped(shard, by) for by in (1, 2, 3)]


def on_device(
    tokens,
    lengths,
    embedding,
    attn_gain,
    key_weight,
    value_weight,
    policy_keys,
    policy_values,
    critic_lengths,
    critic_gain,
    critic_keys,
    critic_values,
    value_gain,
    value_head,
):
    row_groups = lax.axis_size("rows")
    tp = lax.axis_index("tp").astype(jnp.int32).reshape(1)

    def as_row(gain):
        return gain.astype(jnp.float32).reshape(1, -1)

    table = embedding.transpose(1, 2, 0).reshape(embedding.shape[2], embedding.shape[0])
    all_tokens = lax.all_to_all(
        jnp.broadcast_to(tokens[None], (row_groups,) + tokens.shape), "rows", 0, 0
    )
    picked = pick_rows(all_tokens, table)
    blocks = lax.all_to_all(picked.reshape(row_groups, -1, LANES), "rows", 0, 0)
    x, query, parts = project(
        tp, blocks.reshape(picked.shape), as_row(attn_gain), key_weight, value_weight
    )
    arrived = parts[:1] + [swapped(parts[by], by) for by in (1, 2, 3)]
    raw = raw_scores(query, policy_keys, "policy_scores")
    passed, squares, hidden = policy(lengths, arrived, raw, query, x, policy_values)

    rows = passed_along(passed, "rows", row_groups // 2)
    squares = passed_along(squares, "rows", row_groups // 2)
    raw = critic_scores(rows, as_row(critic_gain), critic_keys)
    logits = critic(
        critic_lengths,
        with_peers(squares),
        raw,
        rows,
        as_row(value_gain),
        critic_values,
        value_head.T,
    )
    values = expect(with_peers(logits))
    return hidden, values


def solution(mesh):
    placed = (
        P(None, "rows"),
        P("rows"),
        P(None, "rows", "tp"),
        P("tp"),
        P("tp", None),
        P("tp", None),
        P("rows", None, "tp"),
        P("rows", None, "tp"),
        P("rows"),
        P("tp"),
        P("rows", None, "tp"),
        P("rows", None, "tp"),
        P("tp"),
        P("tp", None),
    )
    return jax.shard_map(
        on_device,
        mesh=mesh,
        in_specs=placed,
        out_specs=(P(None, "rows", "tp"), P(None, "rows")),
        check_vma=False,
    )
```

```python
import functools
import math

import jax
import jax.numpy as jnp
from jax import lax
from jax.experimental import pallas as pl
from jax.experimental.pallas import tpu as pltpu
from jax.sharding import PartitionSpec as P

D = 8192
HEAD_DIM = 128
GROUP = 8
ATOMS = 51
LANES = 128
HALF = 64
MIB = 1024 * 1024

norm_eps = 1e-06
atom_span = 10.0
masked = -1e30
attn_scale = 1.0 / math.sqrt(HEAD_DIM)
log2_e = 1.0 / math.log(2.0)

SMEM = pl.BlockSpec(memory_space=pltpu.SMEM)
VMEM = pl.BlockSpec(memory_space=pltpu.VMEM)
HBM = pl.BlockSpec(memory_space=pltpu.HBM)
NT = (((1,), (1,)), ((), ()))


def kernel_call(body, outs, specs, scratch=(), limit=16, flops=0, moved=0, name=None):
    return pl.pallas_call(
        body,
        out_shape=outs,
        in_specs=specs,
        out_specs=jax.tree.map(lambda _: VMEM, outs),
        scratch_shapes=scratch,
        compiler_params=pltpu.CompilerParams(vmem_limit_bytes=limit * MIB),
        cost_estimate=pl.CostEstimate(flops=flops, bytes_accessed=moved, transcendentals=0),
        name=name,
    )


def array(shape, dtype):
    return jax.ShapeDtypeStruct(shape, dtype)


def in_hbm(x):
    return pltpu.with_memory_space_constraint(x, pltpu.HBM)


def pick_rows_kernel(token_ref, table_ref, out_ref, tiles_ref, sems):
    width = table_ref.shape[0]
    pieces = sems.shape[0]
    places = tiles_ref.shape[1] // pieces
    lane = lax.broadcasted_iota(jnp.int32, (width, LANES), 1)

    def token_of(place, half):
        destination = lax.shift_right_logical(place, 3)
        decode_step = jnp.bitwise_and(place, 3)
        row = jnp.bitwise_and(lax.shift_right_logical(place, 2), 1)
        return token_ref[destination, decode_step, row + 2 * half]

    for piece in range(pieces):

        def fetch(i, carry):
            place = piece * places + i
            for half in range(2):
                block = jnp.bitwise_and(token_of(place, half), ~(LANES - 1))
                pltpu.make_async_copy(
                    table_ref.at[:, pl.ds(pl.multiple_of(block, LANES), LANES)],
                    tiles_ref.at[half, place],
                    sems.at[piece],
                ).start()
            return carry

        lax.fori_loop(0, places, fetch, 0, unroll=8)

    empty = jnp.zeros((width, LANES), jnp.float32)
    pair = (empty, empty)
    for piece in range(pieces):
        part = tiles_ref.at[:, pl.ds(piece * places, places)]
        pltpu.make_async_copy(part, part, sems.at[piece]).wait()
        first_place = piece * places % LANES

        def step(i, carry):
            place = piece * places + i
            here = lane == first_place + i
            kept = []
            for half in range(2):
                shift = jnp.bitwise_and(place - token_of(place, half), LANES - 1)
                tile = pltpu.roll(tiles_ref[half, place].astype(jnp.float32), shift, 1)
                kept.append(jnp.where(here, tile, carry[half]))
            return tuple(kept)

        pair = lax.fori_loop(0, places, step, pair, unroll=min(places, 32))
        if first_place + places == LANES:
            both = jnp.concatenate(pair, axis=0)
            rows = pl.ds((piece + 1) * places - LANES, LANES)
            out_ref[rows, :] = both.T.astype(out_ref.dtype)
            pair = (empty, empty)


def pick_rows(tokens, table, pieces=8):
    width = table.shape[0]
    rows = tokens.size * width // LANES
    return kernel_call(
        pick_rows_kernel,
        array((rows, LANES), table.dtype),
        [SMEM, HBM],
        scratch=[
            pltpu.VMEM((2, rows, width, LANES), table.dtype),
            pltpu.SemaphoreType.DMA((pieces,)),
        ],
        limit=24,
        name="pick_rows",
    )(tokens, in_hbm(table))


def stage_kernel(source_ref, target_ref, sems):
    pieces = sems.shape[0]
    rows = target_ref.shape[0] // pieces
    copies = []
    for piece in range(pieces):
        part = pl.ds(piece * rows, rows)
        copies.append(
            pltpu.make_async_copy(source_ref.at[part], target_ref.at[part], sems.at[piece])
        )
    for copy in copies:
        copy.start()
    for copy in copies:
        copy.wait()


def staged(source, rows, pieces=4):
    shape = (rows, source.shape[1])
    return pl.pallas_call(
        stage_kernel,
        out_shape=pltpu.VMEM(shape, source.dtype),
        in_specs=[HBM],
        out_specs=VMEM,
        scratch_shapes=[pltpu.SemaphoreType.DMA((pieces,))],
        compiler_params=pltpu.CompilerParams(vmem_limit_bytes=MIB),
        cost_estimate=pl.CostEstimate(
            flops=0, bytes_accessed=4 * rows * shape[1], transcendentals=0
        ),
        name="stage_weights",
    )(in_hbm(source))


def project_kernel(
    tp_ref, blocks_ref, gain_ref, early_ref, key_ref, value_ref, x_ref, query_ref, *rest
):
    parts = rest[:4]
    gained_ref, placed_ref, sums_ref, late_ref, keys_ref, sems = rest[4:]
    count, width = x_ref.shape
    kv_width = key_ref.shape[1] // 4
    early = early_ref.shape[0]
    chunk = width - early
    copies = [pltpu.make_async_copy(value_ref.at[pl.ds(early, chunk)], late_ref, sems.at[0])]
    for at in range(width // chunk):
        rows = pl.ds(at * chunk, chunk)
        copies.append(
            pltpu.make_async_copy(key_ref.at[rows], keys_ref.at[rows], sems.at[at + 1])
        )
    for copy in copies:
        copy.start()
    left = lax.broadcasted_iota(jnp.int32, (8, LANES), 1) < HALF
    squares = jnp.zeros((count, LANES), jnp.float32)
    for k in range(width // LANES):
        pair = blocks_ref[pl.ds(16 * k, 16), :].astype(jnp.float32)
        one, two = pair[:8], pair[8:]
        low = jnp.where(left, one, pltpu.roll(two, HALF, 1))
        high = jnp.where(left, pltpu.roll(one, HALF, 1), two)
        x = jnp.concatenate([low, high], axis=0)
        squares += x * x
        columns = pl.ds(k * LANES, LANES)
        x_ref[:, columns] = x.astype(x_ref.dtype)
        gained = x * gain_ref[:, columns]
        gained_ref[:, columns] = gained.astype(gained_ref.dtype)
        head, group = divmod(k, GROUP)
        for row in range(4):
            placed_ref[4 * head + row, pl.ds(4 * group, 4), :] = gained[4 * row : 4 * row + 4]
    query_ref[...] = placed_ref[...].astype(query_ref.dtype)
    total = jnp.broadcast_to(jnp.sum(squares, axis=1, keepdims=True), (count, LANES))

    def product(rows, weight):
        return jnp.dot(gained_ref[:, rows], weight, preferred_element_type=jnp.float32)

    values = product(pl.ds(0, early), early_ref[...])
    copies[0].wait()
    sums_ref[1] = values + product(pl.ds(early, chunk), late_ref[...])
    keys = None
    for at in range(width // chunk):
        rows = pl.ds(at * chunk, chunk)
        copies[at + 1].wait()
        partial = product(rows, keys_ref[rows, :])
        keys = partial if keys is None else keys + partial
    sums_ref[0] = keys
    for by, part_ref in enumerate(parts):
        start = pl.multiple_of(jnp.bitwise_xor(tp_ref[0], by) * kv_width, kv_width)
        peer = pl.ds(start, kv_width)
        part_ref[:, :kv_width] = sums_ref[0, :, peer]
        part_ref[:, kv_width : 2 * kv_width] = sums_ref[1, :, peer]
        part_ref[:, 2 * kv_width :] = total


def project(tp, blocks, gain, key_weight, value_weight):
    width, kv_all = key_weight.shape
    count = blocks.shape[0] * LANES // width
    early = width * 3 // 4
    part = array((count, kv_all // 2 + LANES), jnp.float32)
    heads = width // (GROUP * HEAD_DIM)
    queries = (4 * heads, 4 * GROUP, HEAD_DIM)
    x, query, *parts = kernel_call(
        project_kernel,
        (array((count, width), jnp.bfloat16), array(queries, jnp.bfloat16)) + (part,) * 4,
        [SMEM] + [VMEM] * 3 + [HBM] * 2,
        scratch=[
            pltpu.VMEM((count, width), jnp.bfloat16),
            pltpu.VMEM(queries, jnp.float32),
            pltpu.VMEM((2, count, kv_all), jnp.float32),
            pltpu.VMEM((width - early, kv_all), key_weight.dtype),
            pltpu.VMEM((width, kv_all), key_weight.dtype),
            pltpu.SemaphoreType.DMA((1 + width // (width - early),)),
        ],
        flops=4 * count * width * kv_all,
        moved=4 * width * kv_all,
        name="project",
    )(
        tp,
        blocks,
        gain,
        staged(value_weight, early),
        in_hbm(key_weight),
        in_hbm(value_weight),
    )
    return x, query, parts


def masked_scores(query, keys, length, raw_ref, top_ref, at):
    raw = lax.dot_general(query, keys, NT, preferred_element_type=jnp.float32)
    visible = lax.broadcasted_iota(jnp.int32, raw.shape, 1) < length
    raw = jnp.where(visible, raw, masked)
    raw_ref[at] = raw
    top_ref[at] = jnp.broadcast_to(jnp.max(raw, axis=1, keepdims=True), top_ref.shape[1:])


def scores_kernel(length_ref, query_ref, keys_ref, raw_ref, top_ref):
    for at in range(query_ref.shape[0]):
        head, row = divmod(at, 4)
        keys = keys_ref[row, :, pl.ds(head * HEAD_DIM, HEAD_DIM)]
        masked_scores(query_ref[at], keys, length_ref[row], raw_ref, top_ref, at)


def policy_scores(lengths, query, keys):
    raw = array(query.shape[:2] + (keys.shape[1],), jnp.float32)
    return kernel_call(
        scores_kernel,
        (raw, array(query.shape, jnp.float32)),
        [SMEM, VMEM, VMEM],
        flops=2 * raw.size * HEAD_DIM,
        moved=2 * keys.size + 4 * raw.size,
        name="policy_scores",
    )(lengths, query, keys)


def spread_rows(inv, spread_ref):
    for row in range(4):
        for group in range(GROUP):
            spread_ref[row, pl.ds(4 * group, 4), :] = inv[4 * row : 4 * row + 4]


def widened(x, width):
    return jnp.concatenate([x] * (width // LANES), axis=1)


def policy_kernel(
    own_ref,
    one_ref,
    two_ref,
    three_ref,
    raw_ref,
    top_ref,
    query_ref,
    x_ref,
    values_ref,
    passed_ref,
    spread_ref,
    rows_ref,
):
    count, width = x_ref.shape
    kv_width = values_ref.shape[2]
    cache_size = values_ref.shape[1]
    total = own_ref[...] + (one_ref[...] + (two_ref[...] + three_ref[...]))
    inv = lax.rsqrt(total[:, 2 * kv_width :] * (1.0 / D) + norm_eps)
    wide = widened(inv, kv_width)
    new_key = (wide * total[:, :kv_width]).astype(jnp.bfloat16)
    new_value = (wide * total[:, kv_width : 2 * kv_width]).astype(jnp.bfloat16)
    spread_rows(inv * (attn_scale * log2_e), spread_ref)
    queries = query_ref.shape[1]
    at_query = lax.broadcasted_iota(jnp.int32, (4 * queries, count), 0)
    at_fresh = lax.broadcasted_iota(jnp.int32, (4 * queries, count), 1)
    mine = jnp.logical_and(
        lax.div(at_query, queries) == lax.shift_right_logical(at_fresh, 2),
        jnp.bitwise_and(at_fresh, 3) <= jnp.bitwise_and(at_query, 3),
    )
    for head in range(query_ref.shape[0] // 4):
        columns = slice(head * HEAD_DIM, (head + 1) * HEAD_DIM)
        all_queries = query_ref[pl.ds(4 * head, 4)].reshape(4 * queries, HEAD_DIM)
        fresh = lax.dot_general(
            all_queries, new_key[:, columns], NT, preferred_element_type=jnp.float32
        )
        fresh = jnp.where(mine, fresh, masked)
        fresh_top = jnp.max(fresh, axis=1, keepdims=True)
        fresh_weights, attended, inverses = [], [], []
        for row in range(4):
            at = 4 * head + row
            part = slice(row * queries, (row + 1) * queries)
            spread = spread_ref[row]
            highest = jnp.maximum(top_ref[at], fresh_top[part]) * spread
            weights = jnp.exp2(
                raw_ref[at] * widened(spread, cache_size) - widened(highest, cache_size)
            )
            extra = jnp.exp2(fresh[part] * spread[:, :count] - highest[:, :count])
            inverses.append(
                1.0
                / (jnp.sum(weights, axis=1, keepdims=True) + jnp.sum(extra, axis=1, keepdims=True))
            )
            fresh_weights.append(extra)
            attended.append(
                jnp.dot(
                    weights.astype(jnp.bfloat16),
                    values_ref[row, :, columns],
                    preferred_element_type=jnp.float32,
                )
            )
        fresh_weights = jnp.concatenate(fresh_weights, axis=0).astype(jnp.bfloat16)
        fresh_sum = jnp.dot(
            fresh_weights, new_value[:, columns], preferred_element_type=jnp.float32
        )
        for row in range(4):
            part = slice(row * queries, (row + 1) * queries)
            both = (attended[row] + fresh_sum[part]) * inverses[row]
            for group in range(GROUP):
                rows_ref[head * GROUP + group, pl.ds(4 * row, 4), :] = both[
                    4 * group : 4 * group + 4
                ]
    for k in range(width // LANES):
        columns = pl.ds(k * LANES, LANES)
        hidden = x_ref[:, columns].astype(jnp.float32) + rows_ref[k]
        passed_ref[:, columns] = hidden.astype(passed_ref.dtype)


def policy(parts, raw, top, query, x, values):
    count, width = x.shape
    return kernel_call(
        policy_kernel,
        array((count, width), jnp.bfloat16),
        [VMEM] * 9,
        scratch=[
            pltpu.VMEM((4, 4 * GROUP, LANES), jnp.float32),
            pltpu.VMEM((width // LANES, count, LANES), jnp.float32),
        ],
        flops=2 * raw.size * HEAD_DIM,
        moved=2 * values.size + 4 * raw.size,
        name="policy",
    )(*parts, raw, top, query, x, values)


def by_step_kernel(rows_ref, out_ref, wide_ref):
    for k in range(rows_ref.shape[1] // LANES):
        columns = pl.ds(k * LANES, LANES)
        wide_ref[k] = rows_ref[:, columns].astype(jnp.float32)
        for step in range(4):
            out_ref[step, :, columns] = wide_ref[k, pl.ds(step, 4, stride=4), :].astype(
                out_ref.dtype
            )


def by_step(rows):
    count, width = rows.shape
    return kernel_call(
        by_step_kernel,
        array((4, count // 4, width), rows.dtype),
        [VMEM],
        scratch=[pltpu.VMEM((width // LANES, count, LANES), jnp.float32)],
        moved=16 * rows.size,
        name="by_step",
    )(rows)


def squares_kernel(rows_ref, out_ref):
    squares = jnp.zeros(out_ref.shape, jnp.float32)
    for k in range(rows_ref.shape[1] // LANES):
        part = rows_ref[:, pl.ds(k * LANES, LANES)].astype(jnp.float32)
        squares += part * part
    out_ref[...] = jnp.broadcast_to(jnp.sum(squares, axis=1, keepdims=True), out_ref.shape)


def row_squares(rows):
    return kernel_call(
        squares_kernel, array((rows.shape[0], LANES), jnp.float32), [VMEM], name="row_squares"
    )(rows)


def critic_scores_kernel(
    length_ref, rows_ref, gain_ref, keys_ref, raw_ref, top_ref, placed_ref
):
    for k in range(rows_ref.shape[1] // LANES):
        columns = pl.ds(k * LANES, LANES)
        gained = rows_ref[:, columns].astype(jnp.float32) * gain_ref[:, columns]
        head, group = divmod(k, GROUP)
        for row in range(4):
            placed_ref[4 * head + row, pl.ds(4 * group, 4), :] = gained[4 * row : 4 * row + 4]
    for at in range(placed_ref.shape[0]):
        head, row = divmod(at, 4)
        keys = keys_ref[row, :, pl.ds(head * HEAD_DIM, HEAD_DIM)]
        query = placed_ref[at].astype(jnp.bfloat16)
        masked_scores(query, keys, length_ref[row], raw_ref, top_ref, at)


def critic_scores(lengths, rows, gain, keys):
    heads = keys.shape[2] // HEAD_DIM
    placed = (4 * heads, 4 * GROUP, HEAD_DIM)
    raw = array(placed[:2] + (keys.shape[1],), jnp.float32)
    return kernel_call(
        critic_scores_kernel,
        (raw, array(placed, jnp.float32)),
        [SMEM] + [VMEM] * 3,
        scratch=[pltpu.VMEM(placed, jnp.float32)],
        flops=2 * raw.size * HEAD_DIM,
        moved=2 * keys.size + 4 * raw.size,
        name="critic_scores",
    )(lengths, rows, gain, keys)


def critic_kernel(
    own_ref,
    one_ref,
    two_ref,
    three_ref,
    raw_ref,
    top_ref,
    rows_ref,
    gain_ref,
    values_ref,
    head_ref,
    out_ref,
    spread_ref,
    attended_ref,
    scaled_ref,
):
    count, width = rows_ref.shape
    cache_size = values_ref.shape[1]
    total = own_ref[...] + (one_ref[...] + (two_ref[...] + three_ref[...]))
    inv = lax.rsqrt(total * (1.0 / D) + norm_eps)
    spread_rows(inv * (attn_scale * log2_e), spread_ref)
    for at in range(raw_ref.shape[0]):
        head, row = divmod(at, 4)
        spread = spread_ref[row]
        weights = jnp.exp2(
            raw_ref[at] * widened(spread, cache_size) - widened(top_ref[at] * spread, cache_size)
        )
        inverse = 1.0 / jnp.sum(weights, axis=1, keepdims=True)
        attended = inverse * jnp.dot(
            weights.astype(jnp.bfloat16),
            values_ref[row, :, pl.ds(head * HEAD_DIM, HEAD_DIM)],
            preferred_element_type=jnp.float32,
        )
        for group in range(GROUP):
            attended_ref[head * GROUP + group, pl.ds(4 * row, 4), :] = attended[
                4 * group : 4 * group + 4
            ]
    squares = jnp.zeros((count, LANES), jnp.float32)
    for k in range(width // LANES):
        columns = pl.ds(k * LANES, LANES)
        combined = rows_ref[:, columns].astype(jnp.float32) + attended_ref[k]
        squares += combined * combined
        scaled_ref[:, columns] = (combined * gain_ref[:, columns]).astype(scaled_ref.dtype)
    logits = lax.dot_general(
        scaled_ref[...], head_ref[...], NT, preferred_element_type=jnp.float32
    )
    out_ref[...] = jnp.broadcast_to(jnp.sum(squares, axis=1, keepdims=True), (count, LANES))
    out_ref[:, :ATOMS] = logits


def critic(parts, raw, top, rows, gain, values, head):
    count, width = rows.shape
    return kernel_call(
        critic_kernel,
        array((count, LANES), jnp.float32),
        [VMEM] * 10,
        scratch=[
            pltpu.VMEM((4, 4 * GROUP, LANES), jnp.float32),
            pltpu.VMEM((width // LANES, count, LANES), jnp.float32),
            pltpu.VMEM((count, width), jnp.bfloat16),
        ],
        flops=2 * raw.size * HEAD_DIM,
        moved=2 * values.size + 4 * raw.size,
        name="critic",
    )(*parts, raw, top, rows, gain, values, head)


def expect_kernel(own_ref, one_ref, two_ref, three_ref, out_ref):
    total = own_ref[...] + (one_ref[...] + (two_ref[...] + three_ref[...]))
    lane = lax.broadcasted_iota(jnp.int32, total.shape, 1)
    at = lax.broadcasted_iota(jnp.int32, total.shape, 0)
    logits = lax.rsqrt(total[:, LANES - 1 :] * (1.0 / D) + norm_eps) * total
    real = lane < ATOMS
    logits = jnp.where(real, logits, masked)
    weights = jnp.exp(logits - jnp.max(logits, axis=1, keepdims=True))
    atoms = -atom_span + 2.0 * atom_span * lane.astype(jnp.float32) / (ATOMS - 1)
    value = jnp.sum(weights * atoms, axis=1, keepdims=True) / jnp.sum(
        weights, axis=1, keepdims=True
    )
    placed = jnp.where(lane == lax.shift_right_logical(at, 2), value, 0.0)
    rows = [
        jnp.sum(jnp.where(jnp.bitwise_and(at, 3) == step, placed, 0.0), axis=0, keepdims=True)
        for step in range(4)
    ]
    out_ref[...] = jnp.concatenate(rows, axis=0)[:, :4]


def expect(parts):
    return kernel_call(expect_kernel, array((4, 4), jnp.float32), [VMEM] * 4, name="expect")(*parts)


def swapped(shard, by):
    peers = lax.axis_size("tp")
    return lax.ppermute(shard, "tp", [(i, i ^ by) for i in range(peers)])


def passed_along(shard, axis, by):
    peers = lax.axis_size(axis)
    return lax.ppermute(shard, axis, [(i, (i + by) % peers) for i in range(peers)])


def with_peers(shard):
    return [shard] + [swapped(shard, by) for by in (1, 2, 3)]


def on_device(
    tokens,
    lengths,
    embedding,
    attn_gain,
    key_weight,
    value_weight,
    policy_keys,
    policy_values,
    critic_lengths,
    critic_gain,
    critic_keys,
    critic_values,
    value_gain,
    value_head,
):
    row_groups = lax.axis_size("rows")
    tp = lax.axis_index("tp").astype(jnp.int32).reshape(1)

    def as_row(gain):
        return gain.astype(jnp.float32).reshape(1, -1)

    table = embedding.transpose(1, 2, 0).reshape(embedding.shape[2], embedding.shape[0])
    all_tokens = lax.all_to_all(
        jnp.broadcast_to(tokens[None], (row_groups,) + tokens.shape), "rows", 0, 0
    )
    picked = pick_rows(all_tokens, table)
    blocks = lax.all_to_all(picked.reshape(row_groups, -1, LANES), "rows", 0, 0)
    x, query, parts = project(
        tp, blocks.reshape(picked.shape), as_row(attn_gain), key_weight, value_weight
    )
    arrived = parts[:1] + [swapped(parts[by], by) for by in (1, 2, 3)]
    raw, top = policy_scores(lengths, query, policy_keys)
    passed = policy(arrived, raw, top, query, x, policy_values)
    rows = passed_along(passed, "rows", row_groups // 2)
    hidden = by_step(passed)

    raw, top = critic_scores(critic_lengths, rows, as_row(critic_gain), critic_keys)
    logits = critic(
        with_peers(row_squares(rows)),
        raw,
        top,
        rows,
        as_row(value_gain),
        critic_values,
        value_head.T,
    )
    values = expect(with_peers(logits))
    return hidden, values


def solution(mesh):
    placed = (
        P(None, "rows"),
        P("rows"),
        P(None, "rows", "tp"),
        P("tp"),
        P("tp", None),
        P("tp", None),
        P("rows", None, "tp"),
        P("rows", None, "tp"),
        P("rows"),
        P("tp"),
        P("rows", None, "tp"),
        P("rows", None, "tp"),
        P("tp"),
        P("tp", None),
    )
    return jax.shard_map(
        on_device,
        mesh=mesh,
        in_specs=placed,
        out_specs=(P(None, "rows", "tp"), P(None, "rows")),
        check_vma=False,
    )
```

```python
import functools
import math

import jax
import jax.numpy as jnp
from jax import lax
from jax.experimental import pallas as pl
from jax.experimental.pallas import tpu as pltpu
from jax.sharding import PartitionSpec as P

D = 8192
HEAD_DIM = 128
GROUP = 8
ATOMS = 51
LANES = 128
HALF = 64
MIB = 1024 * 1024

norm_eps = 1e-06
atom_span = 10.0
masked = -1e30
attn_scale = 1.0 / math.sqrt(HEAD_DIM)
log2_e = 1.0 / math.log(2.0)

SMEM = pl.BlockSpec(memory_space=pltpu.SMEM)
VMEM = pl.BlockSpec(memory_space=pltpu.VMEM)
HBM = pl.BlockSpec(memory_space=pltpu.HBM)
NT = (((1,), (1,)), ((), ()))


def kernel_call(body, outs, specs, scratch=(), limit=16, flops=0, moved=0, name=None):
    return pl.pallas_call(
        body,
        out_shape=outs,
        in_specs=specs,
        out_specs=jax.tree.map(lambda _: VMEM, outs),
        scratch_shapes=scratch,
        compiler_params=pltpu.CompilerParams(vmem_limit_bytes=limit * MIB),
        cost_estimate=pl.CostEstimate(flops=flops, bytes_accessed=moved, transcendentals=0),
        name=name,
    )


def array(shape, dtype):
    return jax.ShapeDtypeStruct(shape, dtype)


def in_hbm(x):
    return pltpu.with_memory_space_constraint(x, pltpu.HBM)


def lay_out_kernel(token_ref, out_ref):
    row = jnp.concatenate([token_ref[step : step + 1, :] for step in range(4)], axis=1)
    out_ref[...] = jnp.broadcast_to(row[None], out_ref.shape)


def laid_out(tokens, copies):
    out = array((copies, 1, tokens.size), tokens.dtype)
    return kernel_call(lay_out_kernel, out, [VMEM], name="lay_out")(tokens)


def pick_rows_kernel(token_ref, table_ref, out_ref, tiles_ref, sems):
    width = table_ref.shape[0]
    pieces = sems.shape[0]
    destinations = token_ref.shape[0] // pieces
    places = 8 * destinations
    lane = lax.broadcasted_iota(jnp.int32, (width, LANES), 1)

    def token_of(destination, i, half):
        m = 8 * half + i
        return token_ref[destination, 0, 4 * (m % 4) + m // 4]

    for piece in range(pieces):

        def fetch(at, carry):
            destination = piece * destinations + at
            for half in range(2):
                for i in range(8):
                    block = jnp.bitwise_and(token_of(destination, i, half), ~(LANES - 1))
                    pltpu.make_async_copy(
                        table_ref.at[:, pl.ds(pl.multiple_of(block, LANES), LANES)],
                        tiles_ref.at[half, 8 * destination + i],
                        sems.at[piece],
                    ).start()
            return carry

        lax.fori_loop(0, destinations, fetch, 0)

    empty = jnp.zeros((width, LANES), jnp.float32)
    pair = (empty, empty)
    for piece in range(pieces):
        part = tiles_ref.at[:, pl.ds(piece * places, places)]
        pltpu.make_async_copy(part, part, sems.at[piece]).wait()
        first_place = piece * places % LANES

        def step(at, carry):
            destination = piece * destinations + at
            pair = list(carry)
            for i in range(8):
                place = 8 * destination + i
                here = lane == first_place + 8 * at + i
                for half in range(2):
                    shift = jnp.bitwise_and(place - token_of(destination, i, half), LANES - 1)
                    tile = pltpu.roll(tiles_ref[half, place].astype(jnp.float32), shift, 1)
                    pair[half] = jnp.where(here, tile, pair[half])
            return tuple(pair)

        pair = lax.fori_loop(0, destinations, step, pair, unroll=min(destinations, 4))
        if first_place + places == LANES:
            both = jnp.concatenate(pair, axis=0)
            rows = pl.ds((piece + 1) * places - LANES, LANES)
            out_ref[rows, :] = both.T.astype(out_ref.dtype)
            pair = (empty, empty)


def pick_rows(tokens, table, pieces=8):
    width = table.shape[0]
    rows = tokens.size * width // LANES
    return kernel_call(
        pick_rows_kernel,
        array((rows, LANES), table.dtype),
        [SMEM, HBM],
        scratch=[
            pltpu.VMEM((2, rows, width, LANES), table.dtype),
            pltpu.SemaphoreType.DMA((pieces,)),
        ],
        limit=24,
        name="pick_rows",
    )(tokens, in_hbm(table))


def stage_kernel(source_ref, target_ref, sems):
    pieces = sems.shape[0]
    rows = target_ref.shape[0] // pieces
    copies = []
    for piece in range(pieces):
        part = pl.ds(piece * rows, rows)
        copies.append(
            pltpu.make_async_copy(source_ref.at[part], target_ref.at[part], sems.at[piece])
        )
    for copy in copies:
        copy.start()
    for copy in copies:
        copy.wait()


def staged(source, rows, pieces=4):
    shape = (rows, source.shape[1])
    return pl.pallas_call(
        stage_kernel,
        out_shape=pltpu.VMEM(shape, source.dtype),
        in_specs=[HBM],
        out_specs=VMEM,
        scratch_shapes=[pltpu.SemaphoreType.DMA((pieces,))],
        compiler_params=pltpu.CompilerParams(vmem_limit_bytes=MIB),
        cost_estimate=pl.CostEstimate(
            flops=0, bytes_accessed=4 * rows * shape[1], transcendentals=0
        ),
        name="stage_weights",
    )(in_hbm(source))


def project_kernel(
    tp_ref, blocks_ref, gain_ref, early_ref, key_ref, value_ref, x_ref, query_ref, *rest
):
    parts = rest[:4]
    gained_ref, placed_ref, sums_ref, late_ref, keys_ref, sems = rest[4:]
    count, width = x_ref.shape
    kv_width = key_ref.shape[1] // 4
    early = early_ref.shape[0]
    chunk = width - early
    copies = [pltpu.make_async_copy(value_ref.at[pl.ds(early, chunk)], late_ref, sems.at[0])]
    for at in range(width // chunk):
        rows = pl.ds(at * chunk, chunk)
        copies.append(
            pltpu.make_async_copy(key_ref.at[rows], keys_ref.at[rows], sems.at[at + 1])
        )
    for copy in copies:
        copy.start()
    left = lax.broadcasted_iota(jnp.int32, (8, LANES), 1) < HALF
    squares = jnp.zeros((count, LANES), jnp.float32)
    for k in range(width // LANES):
        pair = blocks_ref[pl.ds(16 * k, 16), :].astype(jnp.float32)
        one, two = pair[:8], pair[8:]
        low = jnp.where(left, one, pltpu.roll(two, HALF, 1))
        high = jnp.where(left, pltpu.roll(one, HALF, 1), two)
        x = jnp.concatenate([low, high], axis=0)
        squares += x * x
        columns = pl.ds(k * LANES, LANES)
        x_ref[:, columns] = x.astype(x_ref.dtype)
        gained = x * gain_ref[:, columns]
        gained_ref[:, columns] = gained.astype(gained_ref.dtype)
        head, group = divmod(k, GROUP)
        for row in range(4):
            placed_ref[4 * head + row, pl.ds(4 * group, 4), :] = gained[4 * row : 4 * row + 4]
    query_ref[...] = placed_ref[...].astype(query_ref.dtype)
    total = jnp.broadcast_to(jnp.sum(squares, axis=1, keepdims=True), (count, LANES))

    def product(rows, weight):
        return jnp.dot(gained_ref[:, rows], weight, preferred_element_type=jnp.float32)

    values = product(pl.ds(0, early), early_ref[...])
    copies[0].wait()
    sums_ref[1] = values + product(pl.ds(early, chunk), late_ref[...])
    keys = None
    for at in range(width // chunk):
        rows = pl.ds(at * chunk, chunk)
        copies[at + 1].wait()
        partial = product(rows, keys_ref[rows, :])
        keys = partial if keys is None else keys + partial
    sums_ref[0] = keys
    for by, part_ref in enumerate(parts):
        start = pl.multiple_of(jnp.bitwise_xor(tp_ref[0], by) * kv_width, kv_width)
        peer = pl.ds(start, kv_width)
        part_ref[:, :kv_width] = sums_ref[0, :, peer]
        part_ref[:, kv_width : 2 * kv_width] = sums_ref[1, :, peer]
        part_ref[:, 2 * kv_width :] = total


def project(tp, blocks, gain, key_weight, value_weight):
    width, kv_all = key_weight.shape
    count = blocks.shape[0] * LANES // width
    early = width * 3 // 4
    part = array((count, kv_all // 2 + LANES), jnp.float32)
    heads = width // (GROUP * HEAD_DIM)
    queries = (4 * heads, 4 * GROUP, HEAD_DIM)
    x, query, *parts = kernel_call(
        project_kernel,
        (array((count, width), jnp.bfloat16), array(queries, jnp.bfloat16)) + (part,) * 4,
        [SMEM] + [VMEM] * 3 + [HBM] * 2,
        scratch=[
            pltpu.VMEM((count, width), jnp.bfloat16),
            pltpu.VMEM(queries, jnp.float32),
            pltpu.VMEM((2, count, kv_all), jnp.float32),
            pltpu.VMEM((width - early, kv_all), key_weight.dtype),
            pltpu.VMEM((width, kv_all), key_weight.dtype),
            pltpu.SemaphoreType.DMA((1 + width // (width - early),)),
        ],
        flops=4 * count * width * kv_all,
        moved=4 * width * kv_all,
        name="project",
    )(
        tp,
        blocks,
        gain,
        staged(value_weight, early),
        in_hbm(key_weight),
        in_hbm(value_weight),
    )
    return x, query, parts


def masked_scores(query, keys, length, raw_ref, top_ref, at):
    raw = lax.dot_general(query, keys, NT, preferred_element_type=jnp.float32)
    visible = lax.broadcasted_iota(jnp.int32, raw.shape, 1) < length
    raw = jnp.where(visible, raw, masked)
    raw_ref[at] = raw
    top_ref[at] = jnp.broadcast_to(jnp.max(raw, axis=1, keepdims=True), top_ref.shape[1:])


def scores_kernel(length_ref, query_ref, keys_ref, raw_ref, top_ref):
    for at in range(query_ref.shape[0]):
        head, row = divmod(at, 4)
        keys = keys_ref[row, :, pl.ds(head * HEAD_DIM, HEAD_DIM)]
        masked_scores(query_ref[at], keys, length_ref[row], raw_ref, top_ref, at)


def policy_scores(lengths, query, keys):
    raw = array(query.shape[:2] + (keys.shape[1],), jnp.float32)
    return kernel_call(
        scores_kernel,
        (raw, array(query.shape, jnp.float32)),
        [SMEM, VMEM, VMEM],
        flops=2 * raw.size * HEAD_DIM,
        moved=2 * keys.size + 4 * raw.size,
        name="policy_scores",
    )(lengths, query, keys)


def spread_rows(inv, spread_ref):
    for row in range(4):
        for group in range(GROUP):
            spread_ref[row, pl.ds(4 * group, 4), :] = inv[4 * row : 4 * row + 4]


def widened(x, width):
    return jnp.concatenate([x] * (width // LANES), axis=1)


def policy_kernel(
    own_ref,
    one_ref,
    two_ref,
    three_ref,
    raw_ref,
    top_ref,
    query_ref,
    x_ref,
    values_ref,
    passed_ref,
    spread_ref,
    rows_ref,
):
    count, width = x_ref.shape
    kv_width = values_ref.shape[2]
    cache_size = values_ref.shape[1]
    total = own_ref[...] + (one_ref[...] + (two_ref[...] + three_ref[...]))
    inv = lax.rsqrt(total[:, 2 * kv_width :] * (1.0 / D) + norm_eps)
    wide = widened(inv, kv_width)
    new_key = (wide * total[:, :kv_width]).astype(jnp.bfloat16)
    new_value = (wide * total[:, kv_width : 2 * kv_width]).astype(jnp.bfloat16)
    spread_rows(inv * (attn_scale * log2_e), spread_ref)
    queries = query_ref.shape[1]
    at_query = lax.broadcasted_iota(jnp.int32, (4 * queries, count), 0)
    at_fresh = lax.broadcasted_iota(jnp.int32, (4 * queries, count), 1)
    mine = jnp.logical_and(
        lax.div(at_query, queries) == lax.shift_right_logical(at_fresh, 2),
        jnp.bitwise_and(at_fresh, 3) <= jnp.bitwise_and(at_query, 3),
    )
    for head in range(query_ref.shape[0] // 4):
        columns = slice(head * HEAD_DIM, (head + 1) * HEAD_DIM)
        all_queries = query_ref[pl.ds(4 * head, 4)].reshape(4 * queries, HEAD_DIM)
        fresh = lax.dot_general(
            all_queries, new_key[:, columns], NT, preferred_element_type=jnp.float32
        )
        fresh = jnp.where(mine, fresh, masked)
        fresh_top = jnp.max(fresh, axis=1, keepdims=True)
        fresh_weights, attended, inverses = [], [], []
        for row in range(4):
            at = 4 * head + row
            part = slice(row * queries, (row + 1) * queries)
            spread = spread_ref[row]
            highest = jnp.maximum(top_ref[at], fresh_top[part]) * spread
            weights = jnp.exp2(
                raw_ref[at] * widened(spread, cache_size) - widened(highest, cache_size)
            )
            extra = jnp.exp2(fresh[part] * spread[:, :count] - highest[:, :count])
            inverses.append(
                1.0
                / (jnp.sum(weights, axis=1, keepdims=True) + jnp.sum(extra, axis=1, keepdims=True))
            )
            fresh_weights.append(extra)
            attended.append(
                jnp.dot(
                    weights.astype(jnp.bfloat16),
                    values_ref[row, :, columns],
                    preferred_element_type=jnp.float32,
                )
            )
        fresh_weights = jnp.concatenate(fresh_weights, axis=0).astype(jnp.bfloat16)
        fresh_sum = jnp.dot(
            fresh_weights, new_value[:, columns], preferred_element_type=jnp.float32
        )
        for row in range(4):
            part = slice(row * queries, (row + 1) * queries)
            both = (attended[row] + fresh_sum[part]) * inverses[row]
            for group in range(GROUP):
                rows_ref[head * GROUP + group, pl.ds(4 * row, 4), :] = both[
                    4 * group : 4 * group + 4
                ]
    for k in range(width // LANES):
        columns = pl.ds(k * LANES, LANES)
        hidden = x_ref[:, columns].astype(jnp.float32) + rows_ref[k]
        passed_ref[:, columns] = hidden.astype(passed_ref.dtype)


def policy(parts, raw, top, query, x, values):
    count, width = x.shape
    return kernel_call(
        policy_kernel,
        array((count, width), jnp.bfloat16),
        [VMEM] * 9,
        scratch=[
            pltpu.VMEM((4, 4 * GROUP, LANES), jnp.float32),
            pltpu.VMEM((width // LANES, count, LANES), jnp.float32),
        ],
        flops=2 * raw.size * HEAD_DIM,
        moved=2 * values.size + 4 * raw.size,
        name="policy",
    )(*parts, raw, top, query, x, values)


def by_step_kernel(rows_ref, out_ref, wide_ref):
    for k in range(rows_ref.shape[1] // LANES):
        columns = pl.ds(k * LANES, LANES)
        wide_ref[k] = rows_ref[:, columns].astype(jnp.float32)
        for step in range(4):
            out_ref[step, :, columns] = wide_ref[k, pl.ds(step, 4, stride=4), :].astype(
                out_ref.dtype
            )


def by_step(rows):
    count, width = rows.shape
    return kernel_call(
        by_step_kernel,
        array((4, count // 4, width), rows.dtype),
        [VMEM],
        scratch=[pltpu.VMEM((width // LANES, count, LANES), jnp.float32)],
        moved=16 * rows.size,
        name="by_step",
    )(rows)


def squares_kernel(rows_ref, out_ref):
    squares = jnp.zeros(out_ref.shape, jnp.float32)
    for k in range(rows_ref.shape[1] // LANES):
        part = rows_ref[:, pl.ds(k * LANES, LANES)].astype(jnp.float32)
        squares += part * part
    out_ref[...] = jnp.broadcast_to(jnp.sum(squares, axis=1, keepdims=True), out_ref.shape)


def row_squares(rows):
    return kernel_call(
        squares_kernel, array((rows.shape[0], LANES), jnp.float32), [VMEM], name="row_squares"
    )(rows)


def critic_scores_kernel(
    length_ref, rows_ref, gain_ref, keys_ref, raw_ref, top_ref, placed_ref
):
    for k in range(rows_ref.shape[1] // LANES):
        columns = pl.ds(k * LANES, LANES)
        gained = rows_ref[:, columns].astype(jnp.float32) * gain_ref[:, columns]
        head, group = divmod(k, GROUP)
        for row in range(4):
            placed_ref[4 * head + row, pl.ds(4 * group, 4), :] = gained[4 * row : 4 * row + 4]
    for at in range(placed_ref.shape[0]):
        head, row = divmod(at, 4)
        keys = keys_ref[row, :, pl.ds(head * HEAD_DIM, HEAD_DIM)]
        query = placed_ref[at].astype(jnp.bfloat16)
        masked_scores(query, keys, length_ref[row], raw_ref, top_ref, at)


def critic_scores(lengths, rows, gain, keys):
    heads = keys.shape[2] // HEAD_DIM
    placed = (4 * heads, 4 * GROUP, HEAD_DIM)
    raw = array(placed[:2] + (keys.shape[1],), jnp.float32)
    return kernel_call(
        critic_scores_kernel,
        (raw, array(placed, jnp.float32)),
        [SMEM] + [VMEM] * 3,
        scratch=[pltpu.VMEM(placed, jnp.float32)],
        flops=2 * raw.size * HEAD_DIM,
        moved=2 * keys.size + 4 * raw.size,
        name="critic_scores",
    )(lengths, rows, gain, keys)


def critic_kernel(
    own_ref,
    one_ref,
    two_ref,
    three_ref,
    raw_ref,
    top_ref,
    rows_ref,
    gain_ref,
    values_ref,
    head_ref,
    out_ref,
    spread_ref,
    attended_ref,
    scaled_ref,
):
    count, width = rows_ref.shape
    cache_size = values_ref.shape[1]
    total = own_ref[...] + (one_ref[...] + (two_ref[...] + three_ref[...]))
    inv = lax.rsqrt(total * (1.0 / D) + norm_eps)
    spread_rows(inv * (attn_scale * log2_e), spread_ref)
    for at in range(raw_ref.shape[0]):
        head, row = divmod(at, 4)
        spread = spread_ref[row]
        weights = jnp.exp2(
            raw_ref[at] * widened(spread, cache_size) - widened(top_ref[at] * spread, cache_size)
        )
        inverse = 1.0 / jnp.sum(weights, axis=1, keepdims=True)
        attended = inverse * jnp.dot(
            weights.astype(jnp.bfloat16),
            values_ref[row, :, pl.ds(head * HEAD_DIM, HEAD_DIM)],
            preferred_element_type=jnp.float32,
        )
        for group in range(GROUP):
            attended_ref[head * GROUP + group, pl.ds(4 * row, 4), :] = attended[
                4 * group : 4 * group + 4
            ]
    squares = jnp.zeros((count, LANES), jnp.float32)
    for k in range(width // LANES):
        columns = pl.ds(k * LANES, LANES)
        combined = rows_ref[:, columns].astype(jnp.float32) + attended_ref[k]
        squares += combined * combined
        scaled_ref[:, columns] = (combined * gain_ref[:, columns]).astype(scaled_ref.dtype)
    logits = lax.dot_general(
        scaled_ref[...], head_ref[...], NT, preferred_element_type=jnp.float32
    )
    out_ref[...] = jnp.broadcast_to(jnp.sum(squares, axis=1, keepdims=True), (count, LANES))
    out_ref[:, :ATOMS] = logits


def critic(parts, raw, top, rows, gain, values, head):
    count, width = rows.shape
    return kernel_call(
        critic_kernel,
        array((count, LANES), jnp.float32),
        [VMEM] * 10,
        scratch=[
            pltpu.VMEM((4, 4 * GROUP, LANES), jnp.float32),
            pltpu.VMEM((width // LANES, count, LANES), jnp.float32),
            pltpu.VMEM((count, width), jnp.bfloat16),
        ],
        flops=2 * raw.size * HEAD_DIM,
        moved=2 * values.size + 4 * raw.size,
        name="critic",
    )(*parts, raw, top, rows, gain, values, head)


def expect_kernel(own_ref, one_ref, two_ref, three_ref, out_ref):
    total = own_ref[...] + (one_ref[...] + (two_ref[...] + three_ref[...]))
    lane = lax.broadcasted_iota(jnp.int32, total.shape, 1)
    at = lax.broadcasted_iota(jnp.int32, total.shape, 0)
    logits = lax.rsqrt(total[:, LANES - 1 :] * (1.0 / D) + norm_eps) * total
    real = lane < ATOMS
    logits = jnp.where(real, logits, masked)
    weights = jnp.exp(logits - jnp.max(logits, axis=1, keepdims=True))
    atoms = -atom_span + 2.0 * atom_span * lane.astype(jnp.float32) / (ATOMS - 1)
    value = jnp.sum(weights * atoms, axis=1, keepdims=True) / jnp.sum(
        weights, axis=1, keepdims=True
    )
    placed = jnp.where(lane == lax.shift_right_logical(at, 2), value, 0.0)
    rows = [
        jnp.sum(jnp.where(jnp.bitwise_and(at, 3) == step, placed, 0.0), axis=0, keepdims=True)
        for step in range(4)
    ]
    out_ref[...] = jnp.concatenate(rows, axis=0)[:, :4]


def expect(parts):
    return kernel_call(expect_kernel, array((4, 4), jnp.float32), [VMEM] * 4, name="expect")(*parts)


def swapped(shard, by):
    peers = lax.axis_size("tp")
    return lax.ppermute(shard, "tp", [(i, i ^ by) for i in range(peers)])


def passed_along(shard, axis, by):
    peers = lax.axis_size(axis)
    return lax.ppermute(shard, axis, [(i, (i + by) % peers) for i in range(peers)])


def with_peers(shard):
    return [shard] + [swapped(shard, by) for by in (1, 2, 3)]


def on_device(
    tokens,
    lengths,
    embedding,
    attn_gain,
    key_weight,
    value_weight,
    policy_keys,
    policy_values,
    critic_lengths,
    critic_gain,
    critic_keys,
    critic_values,
    value_gain,
    value_head,
):
    row_groups = lax.axis_size("rows")
    tp = lax.axis_index("tp").astype(jnp.int32).reshape(1)

    def as_row(gain):
        return gain.astype(jnp.float32).reshape(1, -1)

    table = embedding.transpose(1, 2, 0).reshape(embedding.shape[2], embedding.shape[0])
    all_tokens = lax.all_to_all(laid_out(tokens, row_groups), "rows", 0, 0)
    picked = pick_rows(all_tokens, table)
    blocks = lax.all_to_all(picked.reshape(row_groups, -1, LANES), "rows", 0, 0)
    x, query, parts = project(
        tp, blocks.reshape(picked.shape), as_row(attn_gain), key_weight, value_weight
    )
    arrived = parts[:1] + [swapped(parts[by], by) for by in (1, 2, 3)]
    raw, top = policy_scores(lengths, query, policy_keys)
    passed = policy(arrived, raw, top, query, x, policy_values)
    rows = passed_along(passed, "rows", row_groups // 2)
    hidden = by_step(passed)

    raw, top = critic_scores(critic_lengths, rows, as_row(critic_gain), critic_keys)
    logits = critic(
        with_peers(row_squares(rows)),
        raw,
        top,
        rows,
        as_row(value_gain),
        critic_values,
        value_head.T,
    )
    values = expect(with_peers(logits))
    return hidden, values


def solution(mesh):
    placed = (
        P(None, "rows"),
        P("rows"),
        P(None, "rows", "tp"),
        P("tp"),
        P("tp", None),
        P("tp", None),
        P("rows", None, "tp"),
        P("rows", None, "tp"),
        P("rows"),
        P("tp"),
        P("rows", None, "tp"),
        P("rows", None, "tp"),
        P("tp"),
        P("tp", None),
    )
    return jax.shard_map(
        on_device,
        mesh=mesh,
        in_specs=placed,
        out_specs=(P(None, "rows", "tp"), P(None, "rows")),
        check_vma=False,
    )
```

```python
import functools
import math

import jax
import jax.numpy as jnp
from jax import lax
from jax.experimental import pallas as pl
from jax.experimental.pallas import tpu as pltpu
from jax.sharding import PartitionSpec as P

D = 8192
HEAD_DIM = 128
GROUP = 8
ATOMS = 51
LANES = 128
HALF = 64
MIB = 1024 * 1024

norm_eps = 1e-06
atom_span = 10.0
masked = -1e30
attn_scale = 1.0 / math.sqrt(HEAD_DIM)
log2_e = 1.0 / math.log(2.0)

SMEM = pl.BlockSpec(memory_space=pltpu.SMEM)
VMEM = pl.BlockSpec(memory_space=pltpu.VMEM)
HBM = pl.BlockSpec(memory_space=pltpu.HBM)
NT = (((1,), (1,)), ((), ()))


def kernel_call(body, outs, specs, scratch=(), limit=16, flops=0, moved=0, name=None):
    return pl.pallas_call(
        body,
        out_shape=outs,
        in_specs=specs,
        out_specs=tuple(VMEM for _ in outs) if isinstance(outs, tuple) else VMEM,
        scratch_shapes=scratch,
        compiler_params=pltpu.CompilerParams(vmem_limit_bytes=limit * MIB),
        cost_estimate=pl.CostEstimate(flops=flops, bytes_accessed=moved, transcendentals=0),
        name=name,
    )


def array(shape, dtype):
    return jax.ShapeDtypeStruct(shape, dtype)


def in_hbm(x):
    return pltpu.with_memory_space_constraint(x, pltpu.HBM)


def lay_out_kernel(token_ref, out_ref):
    row = jnp.concatenate([token_ref[step : step + 1, :] for step in range(4)], axis=1)
    out_ref[...] = jnp.broadcast_to(row[None], out_ref.shape)


def laid_out(tokens, copies):
    out = array((copies, 1, tokens.size), tokens.dtype)
    return kernel_call(lay_out_kernel, out, [VMEM], name="lay_out")(tokens)


def pick_rows_kernel(
    token_ref, table_ref, weight_ref, out_ref, early_ref, tiles_ref, sems, early_sem
):
    width = table_ref.shape[0]
    pieces = sems.shape[0]
    destinations = token_ref.shape[0] // pieces
    places = 8 * destinations
    lane = lax.broadcasted_iota(jnp.int32, (width, LANES), 1)

    def token_of(destination, i, half):
        m = 8 * half + i
        return token_ref[destination, 0, 4 * (m % 4) + m // 4]

    for piece in range(pieces):

        def fetch(at, carry):
            destination = piece * destinations + at
            for half in range(2):
                for i in range(8):
                    block = jnp.bitwise_and(token_of(destination, i, half), ~(LANES - 1))
                    pltpu.make_async_copy(
                        table_ref.at[:, pl.ds(pl.multiple_of(block, LANES), LANES)],
                        tiles_ref.at[half, 8 * destination + i],
                        sems.at[piece],
                    ).start()
            return carry

        lax.fori_loop(0, destinations, fetch, 0)

    early = pltpu.make_async_copy(
        weight_ref.at[pl.ds(0, early_ref.shape[0])], early_ref, early_sem
    )
    early.start()
    empty = jnp.zeros((width, LANES), jnp.float32)
    pair = (empty, empty)
    for piece in range(pieces):
        part = tiles_ref.at[:, pl.ds(piece * places, places)]
        pltpu.make_async_copy(part, part, sems.at[piece]).wait()
        first_place = piece * places % LANES

        def step(at, carry):
            destination = piece * destinations + at
            pair = list(carry)
            for i in range(8):
                place = 8 * destination + i
                here = lane == first_place + 8 * at + i
                for half in range(2):
                    shift = jnp.bitwise_and(place - token_of(destination, i, half), LANES - 1)
                    tile = pltpu.roll(tiles_ref[half, place].astype(jnp.float32), shift, 1)
                    pair[half] = jnp.where(here, tile, pair[half])
            return tuple(pair)

        pair = lax.fori_loop(0, destinations, step, pair, unroll=min(destinations, 4))
        if first_place + places == LANES:
            both = jnp.concatenate(pair, axis=0)
            rows = pl.ds((piece + 1) * places - LANES, LANES)
            out_ref[rows, :] = both.T.astype(out_ref.dtype)
            pair = (empty, empty)
    early.wait()


def pick_rows(tokens, table, weight, pieces=8):
    width = table.shape[0]
    rows = tokens.size * width // LANES
    early = (weight.shape[0] * 3 // 4, weight.shape[1])
    return kernel_call(
        pick_rows_kernel,
        (array((rows, LANES), table.dtype), pltpu.VMEM(early, weight.dtype)),
        [SMEM, HBM, HBM],
        scratch=[
            pltpu.VMEM((2, rows, width, LANES), table.dtype),
            pltpu.SemaphoreType.DMA((pieces,)),
            pltpu.SemaphoreType.DMA,
        ],
        limit=24,
        name="pick_rows",
    )(tokens, in_hbm(table), in_hbm(weight))


def project_kernel(
    blocks_ref, gain_ref, early_ref, key_ref, value_ref, x_ref, query_ref, *rest
):
    parts = rest[:4]
    gained_ref, placed_ref, sums_ref, late_ref, keys_ref, sems = rest[4:]
    count, width = x_ref.shape
    kv_width = key_ref.shape[1] // 4
    tp = lax.axis_index("tp")
    early = early_ref.shape[0]
    chunk = width - early
    copies = [pltpu.make_async_copy(value_ref.at[pl.ds(early, chunk)], late_ref, sems.at[0])]
    for at in range(width // chunk):
        rows = pl.ds(at * chunk, chunk)
        copies.append(
            pltpu.make_async_copy(key_ref.at[rows], keys_ref.at[rows], sems.at[at + 1])
        )
    for copy in copies:
        copy.start()
    left = lax.broadcasted_iota(jnp.int32, (8, LANES), 1) < HALF
    squares = jnp.zeros((count, LANES), jnp.float32)
    for k in range(width // LANES):
        pair = blocks_ref[pl.ds(16 * k, 16), :].astype(jnp.float32)
        one, two = pair[:8], pair[8:]
        low = jnp.where(left, one, pltpu.roll(two, HALF, 1))
        high = jnp.where(left, pltpu.roll(one, HALF, 1), two)
        x = jnp.concatenate([low, high], axis=0)
        squares += x * x
        columns = pl.ds(k * LANES, LANES)
        x_ref[:, columns] = x.astype(x_ref.dtype)
        gained = x * gain_ref[k : k + 1, :].astype(jnp.float32)
        gained_ref[:, columns] = gained.astype(gained_ref.dtype)
        head, group = divmod(k, GROUP)
        for row in range(4):
            placed_ref[4 * head + row, pl.ds(4 * group, 4), :] = gained[4 * row : 4 * row + 4]
    query_ref[...] = placed_ref[...].astype(query_ref.dtype)
    total = jnp.broadcast_to(jnp.sum(squares, axis=1, keepdims=True), (count, LANES))

    def product(rows, weight):
        return jnp.dot(gained_ref[:, rows], weight, preferred_element_type=jnp.float32)

    values = product(pl.ds(0, early), early_ref[...])
    copies[0].wait()
    sums_ref[1] = values + product(pl.ds(early, chunk), late_ref[...])
    keys = None
    for at in range(width // chunk):
        rows = pl.ds(at * chunk, chunk)
        copies[at + 1].wait()
        partial = product(rows, keys_ref[rows, :])
        keys = partial if keys is None else keys + partial
    sums_ref[0] = keys
    for by, part_ref in enumerate(parts):
        start = pl.multiple_of(jnp.bitwise_xor(tp, by) * kv_width, kv_width)
        peer = pl.ds(start, kv_width)
        part_ref[:, :kv_width] = sums_ref[0, :, peer]
        part_ref[:, kv_width : 2 * kv_width] = sums_ref[1, :, peer]
        part_ref[:, 2 * kv_width :] = total


def project(blocks, gain, early_values, key_weight, value_weight):
    width, kv_all = key_weight.shape
    count = blocks.shape[0] * LANES // width
    early = early_values.shape[0]
    part = array((count, kv_all // 2 + LANES), jnp.float32)
    heads = width // (GROUP * HEAD_DIM)
    queries = (4 * heads, 4 * GROUP, HEAD_DIM)
    x, query, *parts = kernel_call(
        project_kernel,
        (array((count, width), jnp.bfloat16), array(queries, jnp.bfloat16)) + (part,) * 4,
        [VMEM] * 3 + [HBM] * 2,
        scratch=[
            pltpu.VMEM((count, width), jnp.bfloat16),
            pltpu.VMEM(queries, jnp.float32),
            pltpu.VMEM((2, count, kv_all), jnp.float32),
            pltpu.VMEM((width - early, kv_all), key_weight.dtype),
            pltpu.VMEM((width, kv_all), key_weight.dtype),
            pltpu.SemaphoreType.DMA((1 + width // (width - early),)),
        ],
        flops=4 * count * width * kv_all,
        moved=4 * width * kv_all,
        name="project",
    )(
        blocks,
        gain,
        early_values,
        in_hbm(key_weight),
        in_hbm(value_weight),
    )
    return x, query, parts


def masked_scores(query, keys, length, raw_ref, top_ref, at):
    raw = lax.dot_general(query, keys, NT, preferred_element_type=jnp.float32)
    visible = lax.broadcasted_iota(jnp.int32, raw.shape, 1) < length
    raw = jnp.where(visible, raw, masked)
    raw_ref[at] = raw
    top_ref[at] = jnp.broadcast_to(jnp.max(raw, axis=1, keepdims=True), top_ref.shape[1:])


def scores_kernel(length_ref, query_ref, keys_ref, raw_ref, top_ref):
    for at in range(query_ref.shape[0]):
        head, row = divmod(at, 4)
        keys = keys_ref[row, :, pl.ds(head * HEAD_DIM, HEAD_DIM)]
        masked_scores(query_ref[at], keys, length_ref[row], raw_ref, top_ref, at)


def policy_scores(lengths, query, keys):
    raw = array(query.shape[:2] + (keys.shape[1],), jnp.float32)
    return kernel_call(
        scores_kernel,
        (raw, array(query.shape, jnp.float32)),
        [SMEM, VMEM, VMEM],
        flops=2 * raw.size * HEAD_DIM,
        moved=2 * keys.size + 4 * raw.size,
        name="policy_scores",
    )(lengths, query, keys)


def spread_rows(inv, spread_ref):
    for row in range(4):
        for group in range(GROUP):
            spread_ref[row, pl.ds(4 * group, 4), :] = inv[4 * row : 4 * row + 4]


def widened(x, width):
    return jnp.concatenate([x] * (width // LANES), axis=1)


def policy_kernel(
    own_ref,
    one_ref,
    two_ref,
    three_ref,
    raw_ref,
    top_ref,
    query_ref,
    x_ref,
    values_ref,
    passed_ref,
    spread_ref,
    rows_ref,
):
    count, width = x_ref.shape
    kv_width = values_ref.shape[2]
    cache_size = values_ref.shape[1]
    total = own_ref[...] + (one_ref[...] + (two_ref[...] + three_ref[...]))
    inv = lax.rsqrt(total[:, 2 * kv_width :] * (1.0 / D) + norm_eps)
    wide = widened(inv, kv_width)
    new_key = (wide * total[:, :kv_width]).astype(jnp.bfloat16)
    new_value = (wide * total[:, kv_width : 2 * kv_width]).astype(jnp.bfloat16)
    spread_rows(inv * (attn_scale * log2_e), spread_ref)
    queries = query_ref.shape[1]
    at_query = lax.broadcasted_iota(jnp.int32, (4 * queries, count), 0)
    at_fresh = lax.broadcasted_iota(jnp.int32, (4 * queries, count), 1)
    mine = jnp.logical_and(
        lax.div(at_query, queries) == lax.shift_right_logical(at_fresh, 2),
        jnp.bitwise_and(at_fresh, 3) <= jnp.bitwise_and(at_query, 3),
    )
    for head in range(query_ref.shape[0] // 4):
        columns = slice(head * HEAD_DIM, (head + 1) * HEAD_DIM)
        all_queries = query_ref[pl.ds(4 * head, 4)].reshape(4 * queries, HEAD_DIM)
        fresh = lax.dot_general(
            all_queries, new_key[:, columns], NT, preferred_element_type=jnp.float32
        )
        fresh = jnp.where(mine, fresh, masked)
        fresh_top = jnp.max(fresh, axis=1, keepdims=True)
        fresh_weights, attended, inverses = [], [], []
        for row in range(4):
            at = 4 * head + row
            part = slice(row * queries, (row + 1) * queries)
            spread = spread_ref[row]
            highest = jnp.maximum(top_ref[at], fresh_top[part]) * spread
            weights = jnp.exp2(
                raw_ref[at] * widened(spread, cache_size) - widened(highest, cache_size)
            )
            extra = jnp.exp2(fresh[part] * spread[:, :count] - highest[:, :count])
            inverses.append(
                1.0
                / (jnp.sum(weights, axis=1, keepdims=True) + jnp.sum(extra, axis=1, keepdims=True))
            )
            fresh_weights.append(extra)
            attended.append(
                jnp.dot(
                    weights.astype(jnp.bfloat16),
                    values_ref[row, :, columns],
                    preferred_element_type=jnp.float32,
                )
            )
        fresh_weights = jnp.concatenate(fresh_weights, axis=0).astype(jnp.bfloat16)
        fresh_sum = jnp.dot(
            fresh_weights, new_value[:, columns], preferred_element_type=jnp.float32
        )
        for row in range(4):
            part = slice(row * queries, (row + 1) * queries)
            both = (attended[row] + fresh_sum[part]) * inverses[row]
            for group in range(GROUP):
                rows_ref[head * GROUP + group, pl.ds(4 * row, 4), :] = both[
                    4 * group : 4 * group + 4
                ]
    for k in range(width // LANES):
        columns = pl.ds(k * LANES, LANES)
        hidden = x_ref[:, columns].astype(jnp.float32) + rows_ref[k]
        passed_ref[:, columns] = hidden.astype(passed_ref.dtype)


def policy(parts, raw, top, query, x, values):
    count, width = x.shape
    return kernel_call(
        policy_kernel,
        array((count, width), jnp.bfloat16),
        [VMEM] * 9,
        scratch=[
            pltpu.VMEM((4, 4 * GROUP, LANES), jnp.float32),
            pltpu.VMEM((width // LANES, count, LANES), jnp.float32),
        ],
        flops=2 * raw.size * HEAD_DIM,
        moved=2 * values.size + 4 * raw.size,
        name="policy",
    )(*parts, raw, top, query, x, values)


def by_step_kernel(rows_ref, out_ref, wide_ref):
    for k in range(rows_ref.shape[1] // LANES):
        columns = pl.ds(k * LANES, LANES)
        wide_ref[k] = rows_ref[:, columns].astype(jnp.float32)
        for step in range(4):
            out_ref[step, :, columns] = wide_ref[k, pl.ds(step, 4, stride=4), :].astype(
                out_ref.dtype
            )


def by_step(rows):
    count, width = rows.shape
    return kernel_call(
        by_step_kernel,
        array((4, count // 4, width), rows.dtype),
        [VMEM],
        scratch=[pltpu.VMEM((width // LANES, count, LANES), jnp.float32)],
        moved=16 * rows.size,
        name="by_step",
    )(rows)


def squares_kernel(rows_ref, out_ref):
    squares = jnp.zeros(out_ref.shape, jnp.float32)
    for k in range(rows_ref.shape[1] // LANES):
        part = rows_ref[:, pl.ds(k * LANES, LANES)].astype(jnp.float32)
        squares += part * part
    out_ref[...] = jnp.broadcast_to(jnp.sum(squares, axis=1, keepdims=True), out_ref.shape)


def row_squares(rows):
    return kernel_call(
        squares_kernel, array((rows.shape[0], LANES), jnp.float32), [VMEM], name="row_squares"
    )(rows)


def critic_scores_kernel(
    length_ref, rows_ref, gain_ref, keys_ref, raw_ref, top_ref, placed_ref
):
    for k in range(rows_ref.shape[1] // LANES):
        columns = pl.ds(k * LANES, LANES)
        gained = rows_ref[:, columns].astype(jnp.float32) * gain_ref[k : k + 1, :].astype(jnp.float32)
        head, group = divmod(k, GROUP)
        for row in range(4):
            placed_ref[4 * head + row, pl.ds(4 * group, 4), :] = gained[4 * row : 4 * row + 4]
    for at in range(placed_ref.shape[0]):
        head, row = divmod(at, 4)
        keys = keys_ref[row, :, pl.ds(head * HEAD_DIM, HEAD_DIM)]
        query = placed_ref[at].astype(jnp.bfloat16)
        masked_scores(query, keys, length_ref[row], raw_ref, top_ref, at)


def critic_scores(lengths, rows, gain, keys):
    heads = keys.shape[2] // HEAD_DIM
    placed = (4 * heads, 4 * GROUP, HEAD_DIM)
    raw = array(placed[:2] + (keys.shape[1],), jnp.float32)
    return kernel_call(
        critic_scores_kernel,
        (raw, array(placed, jnp.float32)),
        [SMEM] + [VMEM] * 3,
        scratch=[pltpu.VMEM(placed, jnp.float32)],
        flops=2 * raw.size * HEAD_DIM,
        moved=2 * keys.size + 4 * raw.size,
        name="critic_scores",
    )(lengths, rows, gain, keys)


def critic_kernel(
    own_ref,
    one_ref,
    two_ref,
    three_ref,
    raw_ref,
    top_ref,
    rows_ref,
    gain_ref,
    values_ref,
    head_ref,
    out_ref,
    spread_ref,
    attended_ref,
    scaled_ref,
):
    count, width = rows_ref.shape
    cache_size = values_ref.shape[1]
    total = own_ref[...] + (one_ref[...] + (two_ref[...] + three_ref[...]))
    inv = lax.rsqrt(total * (1.0 / D) + norm_eps)
    spread_rows(inv * (attn_scale * log2_e), spread_ref)
    for at in range(raw_ref.shape[0]):
        head, row = divmod(at, 4)
        spread = spread_ref[row]
        weights = jnp.exp2(
            raw_ref[at] * widened(spread, cache_size) - widened(top_ref[at] * spread, cache_size)
        )
        inverse = 1.0 / jnp.sum(weights, axis=1, keepdims=True)
        attended = inverse * jnp.dot(
            weights.astype(jnp.bfloat16),
            values_ref[row, :, pl.ds(head * HEAD_DIM, HEAD_DIM)],
            preferred_element_type=jnp.float32,
        )
        for group in range(GROUP):
            attended_ref[head * GROUP + group, pl.ds(4 * row, 4), :] = attended[
                4 * group : 4 * group + 4
            ]
    squares = jnp.zeros((count, LANES), jnp.float32)
    for k in range(width // LANES):
        columns = pl.ds(k * LANES, LANES)
        combined = rows_ref[:, columns].astype(jnp.float32) + attended_ref[k]
        squares += combined * combined
        scaled_ref[:, columns] = (combined * gain_ref[k : k + 1, :].astype(jnp.float32)).astype(
            scaled_ref.dtype
        )
    logits = lax.dot_general(
        scaled_ref[...], head_ref[...], NT, preferred_element_type=jnp.float32
    )
    out_ref[...] = jnp.broadcast_to(jnp.sum(squares, axis=1, keepdims=True), (count, LANES))
    out_ref[:, :ATOMS] = logits


def critic(parts, raw, top, rows, gain, values, head):
    count, width = rows.shape
    return kernel_call(
        critic_kernel,
        array((count, LANES), jnp.float32),
        [VMEM] * 10,
        scratch=[
            pltpu.VMEM((4, 4 * GROUP, LANES), jnp.float32),
            pltpu.VMEM((width // LANES, count, LANES), jnp.float32),
            pltpu.VMEM((count, width), jnp.bfloat16),
        ],
        flops=2 * raw.size * HEAD_DIM,
        moved=2 * values.size + 4 * raw.size,
        name="critic",
    )(*parts, raw, top, rows, gain, values, head)


def expect_kernel(own_ref, one_ref, two_ref, three_ref, out_ref):
    total = own_ref[...] + (one_ref[...] + (two_ref[...] + three_ref[...]))
    lane = lax.broadcasted_iota(jnp.int32, total.shape, 1)
    at = lax.broadcasted_iota(jnp.int32, total.shape, 0)
    logits = lax.rsqrt(total[:, LANES - 1 :] * (1.0 / D) + norm_eps) * total
    real = lane < ATOMS
    logits = jnp.where(real, logits, masked)
    weights = jnp.exp(logits - jnp.max(logits, axis=1, keepdims=True))
    atoms = -atom_span + 2.0 * atom_span * lane.astype(jnp.float32) / (ATOMS - 1)
    value = jnp.sum(weights * atoms, axis=1, keepdims=True) / jnp.sum(
        weights, axis=1, keepdims=True
    )
    placed = jnp.where(lane == lax.shift_right_logical(at, 2), value, 0.0)
    rows = [
        jnp.sum(jnp.where(jnp.bitwise_and(at, 3) == step, placed, 0.0), axis=0, keepdims=True)
        for step in range(4)
    ]
    out_ref[...] = jnp.concatenate(rows, axis=0)[:, :4]


def expect(parts):
    return kernel_call(expect_kernel, array((4, 4), jnp.float32), [VMEM] * 4, name="expect")(*parts)


def swapped(shard, by):
    peers = lax.axis_size("tp")
    return lax.ppermute(shard, "tp", [(i, i ^ by) for i in range(peers)])


def passed_along(shard, axis, by):
    peers = lax.axis_size(axis)
    return lax.ppermute(shard, axis, [(i, (i + by) % peers) for i in range(peers)])


def with_peers(shard):
    return [shard] + [swapped(shard, by) for by in (1, 2, 3)]


def on_device(
    tokens,
    lengths,
    embedding,
    attn_gain,
    key_weight,
    value_weight,
    policy_keys,
    policy_values,
    critic_lengths,
    critic_gain,
    critic_keys,
    critic_values,
    value_gain,
    value_head,
):
    row_groups = lax.axis_size("rows")

    def as_rows(gain):
        return gain.reshape(-1, LANES)

    table = embedding.transpose(1, 2, 0).reshape(embedding.shape[2], embedding.shape[0])
    all_tokens = lax.all_to_all(laid_out(tokens, row_groups), "rows", 0, 0)
    picked, early_values = pick_rows(all_tokens, table, value_weight)
    blocks = lax.all_to_all(picked.reshape(row_groups, -1, LANES), "rows", 0, 0)
    x, query, parts = project(
        blocks.reshape(picked.shape), as_rows(attn_gain), early_values, key_weight, value_weight
    )
    arrived = parts[:1] + [swapped(parts[by], by) for by in (1, 2, 3)]
    raw, top = policy_scores(lengths, query, policy_keys)
    passed = policy(arrived, raw, top, query, x, policy_values)
    rows = passed_along(passed, "rows", row_groups // 2)
    hidden = by_step(passed)

    raw, top = critic_scores(critic_lengths, rows, as_rows(critic_gain), critic_keys)
    logits = critic(
        with_peers(row_squares(rows)),
        raw,
        top,
        rows,
        as_rows(value_gain),
        critic_values,
        value_head.T,
    )
    values = expect(with_peers(logits))
    return hidden, values


def solution(mesh):
    placed = (
        P(None, "rows"),
        P("rows"),
        P(None, "rows", "tp"),
        P("tp"),
        P("tp", None),
        P("tp", None),
        P("rows", None, "tp"),
        P("rows", None, "tp"),
        P("rows"),
        P("tp"),
        P("rows", None, "tp"),
        P("rows", None, "tp"),
        P("tp"),
        P("tp", None),
    )
    return jax.shard_map(
        on_device,
        mesh=mesh,
        in_specs=placed,
        out_specs=(P(None, "rows", "tp"), P(None, "rows")),
        check_vma=False,
    )
```

```python
import functools
import math

import jax
import jax.numpy as jnp
from jax import lax
from jax.experimental import pallas as pl
from jax.experimental.pallas import tpu as pltpu
from jax.sharding import PartitionSpec as P

D = 8192
HEAD_DIM = 128
GROUP = 8
ATOMS = 51
LANES = 128
HALF = 64
MIB = 1024 * 1024

norm_eps = 1e-06
atom_span = 10.0
masked = -1e30
shrink = 2.0**-64
attn_scale = 1.0 / math.sqrt(HEAD_DIM)
log2_e = 1.0 / math.log(2.0)

SMEM = pl.BlockSpec(memory_space=pltpu.SMEM)
VMEM = pl.BlockSpec(memory_space=pltpu.VMEM)
HBM = pl.BlockSpec(memory_space=pltpu.HBM)
NT = (((1,), (1,)), ((), ()))


def kernel_call(body, outs, specs, scratch=(), limit=16, flops=0, moved=0, name=None):
    return pl.pallas_call(
        body,
        out_shape=outs,
        in_specs=specs,
        out_specs=tuple(VMEM for _ in outs) if isinstance(outs, tuple) else VMEM,
        scratch_shapes=scratch,
        compiler_params=pltpu.CompilerParams(vmem_limit_bytes=limit * MIB),
        cost_estimate=pl.CostEstimate(flops=flops, bytes_accessed=moved, transcendentals=0),
        name=name,
    )


def array(shape, dtype):
    return jax.ShapeDtypeStruct(shape, dtype)


def in_hbm(x):
    return pltpu.with_memory_space_constraint(x, pltpu.HBM)


def lay_out_kernel(token_ref, out_ref):
    row = jnp.concatenate([token_ref[step : step + 1, :] for step in range(4)], axis=1)
    out_ref[...] = jnp.broadcast_to(row[None], out_ref.shape)


def laid_out(tokens, copies):
    out = array((copies, 1, tokens.size), tokens.dtype)
    return kernel_call(lay_out_kernel, out, [VMEM], name="lay_out")(tokens)


def pick_rows_kernel(
    token_ref, table_ref, weight_ref, out_ref, early_ref, tiles_ref, sems, early_sem
):
    width = table_ref.shape[0]
    pieces = sems.shape[0]
    destinations = token_ref.shape[0] // pieces
    places = 8 * destinations
    lane = lax.broadcasted_iota(jnp.int32, (width, LANES), 1)

    def token_of(destination, i, half):
        m = 8 * half + i
        return token_ref[destination, 0, 4 * (m % 4) + m // 4]

    for piece in range(pieces):

        def fetch(at, carry):
            destination = piece * destinations + at
            for half in range(2):
                for i in range(8):
                    block = jnp.bitwise_and(token_of(destination, i, half), ~(LANES - 1))
                    pltpu.make_async_copy(
                        table_ref.at[:, pl.ds(pl.multiple_of(block, LANES), LANES)],
                        tiles_ref.at[half, 8 * destination + i],
                        sems.at[piece],
                    ).start()
            return carry

        lax.fori_loop(0, destinations, fetch, 0)

    early = pltpu.make_async_copy(
        weight_ref.at[pl.ds(0, early_ref.shape[0])], early_ref, early_sem
    )
    early.start()
    empty = jnp.zeros((width, LANES), jnp.float32)
    pair = (empty, empty)
    for piece in range(pieces):
        part = tiles_ref.at[:, pl.ds(piece * places, places)]
        pltpu.make_async_copy(part, part, sems.at[piece]).wait()
        first_place = piece * places % LANES

        def step(at, carry):
            destination = piece * destinations + at
            pair = list(carry)
            for i in range(8):
                place = 8 * destination + i
                here = lane == first_place + 8 * at + i
                for half in range(2):
                    shift = jnp.bitwise_and(place - token_of(destination, i, half), LANES - 1)
                    tile = pltpu.roll(tiles_ref[half, place].astype(jnp.float32), shift, 1)
                    pair[half] = jnp.where(here, tile, pair[half])
            return tuple(pair)

        pair = lax.fori_loop(0, destinations, step, pair, unroll=min(destinations, 4))
        if first_place + places == LANES:
            both = jnp.concatenate(pair, axis=0)
            rows = pl.ds((piece + 1) * places - LANES, LANES)
            out_ref[rows, :] = both.T.astype(out_ref.dtype)
            pair = (empty, empty)
    early.wait()


def pick_rows(tokens, table, weight, pieces=8):
    width = table.shape[0]
    rows = tokens.size * width // LANES
    early = (weight.shape[0] * 3 // 4, weight.shape[1])
    return kernel_call(
        pick_rows_kernel,
        (array((rows, LANES), table.dtype), pltpu.VMEM(early, weight.dtype)),
        [SMEM, HBM, HBM],
        scratch=[
            pltpu.VMEM((2, rows, width, LANES), table.dtype),
            pltpu.SemaphoreType.DMA((pieces,)),
            pltpu.SemaphoreType.DMA,
        ],
        limit=24,
        name="pick_rows",
    )(tokens, in_hbm(table), in_hbm(weight))


def project_kernel(
    blocks_ref, gain_ref, early_ref, key_ref, value_ref, x_ref, query_ref, *rest
):
    parts = rest[:4]
    gained_ref, placed_ref, sums_ref, late_ref, keys_ref, sems = rest[4:]
    count, width = x_ref.shape
    kv_width = key_ref.shape[1] // 4
    tp = lax.axis_index("tp")
    early = early_ref.shape[0]
    chunk = width - early
    copies = [pltpu.make_async_copy(value_ref.at[pl.ds(early, chunk)], late_ref, sems.at[0])]
    for at in range(width // chunk):
        rows = pl.ds(at * chunk, chunk)
        copies.append(
            pltpu.make_async_copy(key_ref.at[rows], keys_ref.at[rows], sems.at[at + 1])
        )
    for copy in copies:
        copy.start()
    left = lax.broadcasted_iota(jnp.int32, (8, LANES), 1) < HALF
    squares = jnp.zeros((count, LANES), jnp.float32)
    for k in range(width // LANES):
        pair = blocks_ref[pl.ds(16 * k, 16), :].astype(jnp.float32)
        one, two = pair[:8], pair[8:]
        low = jnp.where(left, one, pltpu.roll(two, HALF, 1))
        high = jnp.where(left, pltpu.roll(one, HALF, 1), two)
        x = jnp.concatenate([low, high], axis=0)
        squares += x * x
        columns = pl.ds(k * LANES, LANES)
        x_ref[:, columns] = x.astype(x_ref.dtype)
        gained = x * gain_ref[k : k + 1, :].astype(jnp.float32)
        gained_ref[:, columns] = gained.astype(gained_ref.dtype)
        head, group = divmod(k, GROUP)
        for row in range(4):
            placed_ref[4 * head + row, pl.ds(4 * group, 4), :] = gained[4 * row : 4 * row + 4]
    query_ref[...] = (placed_ref[...] * shrink).astype(query_ref.dtype)
    total = jnp.broadcast_to(jnp.sum(squares, axis=1, keepdims=True), (count, LANES))

    def product(rows, weight):
        return jnp.dot(gained_ref[:, rows], weight, preferred_element_type=jnp.float32)

    values = product(pl.ds(0, early), early_ref[...])
    copies[0].wait()
    sums_ref[1] = values + product(pl.ds(early, chunk), late_ref[...])
    keys = None
    for at in range(width // chunk):
        rows = pl.ds(at * chunk, chunk)
        copies[at + 1].wait()
        partial = product(rows, keys_ref[rows, :])
        keys = partial if keys is None else keys + partial
    sums_ref[0] = keys
    head = total.astype(jnp.bfloat16)
    tail = jnp.where(total < 3e38, total - head.astype(jnp.float32), 0.0).astype(jnp.bfloat16)
    for by, part_ref in enumerate(parts):
        start = pl.multiple_of(jnp.bitwise_xor(tp, by) * kv_width, kv_width)
        peer = pl.ds(start, kv_width)
        part_ref[:, :kv_width] = sums_ref[0, :, peer].astype(part_ref.dtype)
        part_ref[:, kv_width : 2 * kv_width] = sums_ref[1, :, peer].astype(part_ref.dtype)
        if by == 0:
            part_ref[:, 2 * kv_width :] = total
        else:
            part_ref[:, 2 * kv_width : 2 * kv_width + LANES] = head
            part_ref[:, 2 * kv_width + LANES :] = tail


def project(blocks, gain, early_values, key_weight, value_weight):
    width, kv_all = key_weight.shape
    count = blocks.shape[0] * LANES // width
    early = early_values.shape[0]
    own = array((count, kv_all // 2 + LANES), jnp.float32)
    part = array((count, kv_all // 2 + 2 * LANES), jnp.bfloat16)
    heads = width // (GROUP * HEAD_DIM)
    queries = (4 * heads, 4 * GROUP, HEAD_DIM)
    x, query, *parts = kernel_call(
        project_kernel,
        (array((count, width), jnp.bfloat16), array(queries, jnp.bfloat16), own) + (part,) * 3,
        [VMEM] * 3 + [HBM] * 2,
        scratch=[
            pltpu.VMEM((count, width), jnp.bfloat16),
            pltpu.VMEM(queries, jnp.float32),
            pltpu.VMEM((2, count, kv_all), jnp.float32),
            pltpu.VMEM((width - early, kv_all), key_weight.dtype),
            pltpu.VMEM((width, kv_all), key_weight.dtype),
            pltpu.SemaphoreType.DMA((1 + width // (width - early),)),
        ],
        flops=4 * count * width * kv_all,
        moved=4 * width * kv_all,
        name="project",
    )(
        blocks,
        gain,
        early_values,
        in_hbm(key_weight),
        in_hbm(value_weight),
    )
    return x, query, parts


def masked_scores(query, keys, length, raw_ref, top_ref, at):
    raw = lax.dot_general(query, keys, NT, preferred_element_type=jnp.float32)
    visible = lax.broadcasted_iota(jnp.int32, raw.shape, 1) < length
    raw = jnp.where(visible, raw, masked)
    raw_ref[at] = raw
    top_ref[at] = jnp.broadcast_to(jnp.max(raw, axis=1, keepdims=True), top_ref.shape[1:])


def scores_kernel(length_ref, query_ref, keys_ref, raw_ref, top_ref):
    for at in range(query_ref.shape[0]):
        head, row = divmod(at, 4)
        keys = keys_ref[row, :, pl.ds(head * HEAD_DIM, HEAD_DIM)]
        masked_scores(query_ref[at], keys, length_ref[row], raw_ref, top_ref, at)


def policy_scores(lengths, query, keys):
    raw = array(query.shape[:2] + (keys.shape[1],), jnp.float32)
    return kernel_call(
        scores_kernel,
        (raw, array(query.shape, jnp.float32)),
        [SMEM, VMEM, VMEM],
        flops=2 * raw.size * HEAD_DIM,
        moved=2 * keys.size + 4 * raw.size,
        name="policy_scores",
    )(lengths, query, keys)


def spread_rows(inv, spread_ref):
    for row in range(4):
        for group in range(GROUP):
            spread_ref[row, pl.ds(4 * group, 4), :] = inv[4 * row : 4 * row + 4]


def widened(x, width):
    return jnp.concatenate([x] * (width // LANES), axis=1)


def masked_weights(raw, spread, highest):
    return jnp.where(raw > 0.5 * masked, jnp.exp2(raw * spread - highest), 0.0)


def policy_kernel(
    own_ref,
    one_ref,
    two_ref,
    three_ref,
    raw_ref,
    top_ref,
    query_ref,
    x_ref,
    values_ref,
    passed_ref,
    spread_ref,
    rows_ref,
):
    count, width = x_ref.shape
    kv_width = values_ref.shape[2]
    cache_size = values_ref.shape[1]
    total = own_ref[...]
    for part_ref in (one_ref, two_ref, three_ref):
        part = part_ref[...].astype(jnp.float32)
        squares = part[:, 2 * kv_width : 2 * kv_width + LANES] + part[:, 2 * kv_width + LANES :]
        total = total + jnp.concatenate([part[:, : 2 * kv_width], squares], axis=1)
    inv = lax.rsqrt(total[:, 2 * kv_width :] * (1.0 / D) + norm_eps)
    wide = widened(inv, kv_width)
    new_key = (wide * total[:, :kv_width]).astype(jnp.bfloat16)
    new_value = (wide * total[:, kv_width : 2 * kv_width]).astype(jnp.bfloat16)
    spread_rows(inv * (attn_scale * log2_e / shrink), spread_ref)
    queries = query_ref.shape[1]
    at_query = lax.broadcasted_iota(jnp.int32, (4 * queries, count), 0)
    at_fresh = lax.broadcasted_iota(jnp.int32, (4 * queries, count), 1)
    mine = jnp.logical_and(
        lax.div(at_query, queries) == lax.shift_right_logical(at_fresh, 2),
        jnp.bitwise_and(at_fresh, 3) <= jnp.bitwise_and(at_query, 3),
    )
    for head in range(query_ref.shape[0] // 4):
        columns = slice(head * HEAD_DIM, (head + 1) * HEAD_DIM)
        all_queries = query_ref[pl.ds(4 * head, 4)].reshape(4 * queries, HEAD_DIM)
        fresh = lax.dot_general(
            all_queries, new_key[:, columns], NT, preferred_element_type=jnp.float32
        )
        fresh = jnp.where(mine, fresh, masked)
        fresh_top = jnp.max(fresh, axis=1, keepdims=True)
        fresh_weights, attended, inverses = [], [], []
        for row in range(4):
            at = 4 * head + row
            part = slice(row * queries, (row + 1) * queries)
            spread = spread_ref[row]
            highest = jnp.maximum(top_ref[at], fresh_top[part]) * spread
            weights = masked_weights(
                raw_ref[at], widened(spread, cache_size), widened(highest, cache_size)
            )
            extra = masked_weights(fresh[part], spread[:, :count], highest[:, :count])
            inverses.append(
                1.0
                / (jnp.sum(weights, axis=1, keepdims=True) + jnp.sum(extra, axis=1, keepdims=True))
            )
            fresh_weights.append(extra)
            attended.append(
                jnp.dot(
                    weights.astype(jnp.bfloat16),
                    values_ref[row, :, columns],
                    preferred_element_type=jnp.float32,
                )
            )
        fresh_weights = jnp.concatenate(fresh_weights, axis=0).astype(jnp.bfloat16)
        fresh_sum = jnp.dot(
            fresh_weights, new_value[:, columns], preferred_element_type=jnp.float32
        )
        for row in range(4):
            part = slice(row * queries, (row + 1) * queries)
            both = (attended[row] + fresh_sum[part]) * inverses[row]
            for group in range(GROUP):
                rows_ref[head * GROUP + group, pl.ds(4 * row, 4), :] = both[
                    4 * group : 4 * group + 4
                ]
    for k in range(width // LANES):
        columns = pl.ds(k * LANES, LANES)
        hidden = x_ref[:, columns].astype(jnp.float32) + rows_ref[k]
        passed_ref[:, columns] = hidden.astype(passed_ref.dtype)


def policy(parts, raw, top, query, x, values):
    count, width = x.shape
    return kernel_call(
        policy_kernel,
        array((count, width), jnp.bfloat16),
        [VMEM] * 9,
        scratch=[
            pltpu.VMEM((4, 4 * GROUP, LANES), jnp.float32),
            pltpu.VMEM((width // LANES, count, LANES), jnp.float32),
        ],
        flops=2 * raw.size * HEAD_DIM,
        moved=2 * values.size + 4 * raw.size,
        name="policy",
    )(*parts, raw, top, query, x, values)


def by_step_kernel(rows_ref, out_ref, wide_ref):
    for k in range(rows_ref.shape[1] // LANES):
        columns = pl.ds(k * LANES, LANES)
        wide_ref[k] = rows_ref[:, columns].astype(jnp.float32)
        for step in range(4):
            out_ref[step, :, columns] = wide_ref[k, pl.ds(step, 4, stride=4), :].astype(
                out_ref.dtype
            )


def by_step(rows):
    count, width = rows.shape
    return kernel_call(
        by_step_kernel,
        array((4, count // 4, width), rows.dtype),
        [VMEM],
        scratch=[pltpu.VMEM((width // LANES, count, LANES), jnp.float32)],
        moved=16 * rows.size,
        name="by_step",
    )(rows)


def squares_kernel(rows_ref, out_ref):
    squares = jnp.zeros(out_ref.shape, jnp.float32)
    for k in range(rows_ref.shape[1] // LANES):
        part = rows_ref[:, pl.ds(k * LANES, LANES)].astype(jnp.float32)
        squares += part * part
    out_ref[...] = jnp.broadcast_to(jnp.sum(squares, axis=1, keepdims=True), out_ref.shape)


def row_squares(rows):
    return kernel_call(
        squares_kernel, array((rows.shape[0], LANES), jnp.float32), [VMEM], name="row_squares"
    )(rows)


def critic_scores_kernel(
    length_ref, rows_ref, gain_ref, keys_ref, raw_ref, top_ref, placed_ref
):
    for k in range(rows_ref.shape[1] // LANES):
        columns = pl.ds(k * LANES, LANES)
        gained = rows_ref[:, columns].astype(jnp.float32) * gain_ref[k : k + 1, :].astype(jnp.float32)
        head, group = divmod(k, GROUP)
        for row in range(4):
            placed_ref[4 * head + row, pl.ds(4 * group, 4), :] = gained[4 * row : 4 * row + 4]
    for at in range(placed_ref.shape[0]):
        head, row = divmod(at, 4)
        keys = keys_ref[row, :, pl.ds(head * HEAD_DIM, HEAD_DIM)]
        query = (placed_ref[at] * shrink).astype(jnp.bfloat16)
        masked_scores(query, keys, length_ref[row], raw_ref, top_ref, at)


def critic_scores(lengths, rows, gain, keys):
    heads = keys.shape[2] // HEAD_DIM
    placed = (4 * heads, 4 * GROUP, HEAD_DIM)
    raw = array(placed[:2] + (keys.shape[1],), jnp.float32)
    return kernel_call(
        critic_scores_kernel,
        (raw, array(placed, jnp.float32)),
        [SMEM] + [VMEM] * 3,
        scratch=[pltpu.VMEM(placed, jnp.float32)],
        flops=2 * raw.size * HEAD_DIM,
        moved=2 * keys.size + 4 * raw.size,
        name="critic_scores",
    )(lengths, rows, gain, keys)


def critic_kernel(
    own_ref,
    one_ref,
    two_ref,
    three_ref,
    raw_ref,
    top_ref,
    rows_ref,
    gain_ref,
    values_ref,
    head_ref,
    out_ref,
    spread_ref,
    attended_ref,
    scaled_ref,
):
    count, width = rows_ref.shape
    cache_size = values_ref.shape[1]
    total = own_ref[...] + (one_ref[...] + (two_ref[...] + three_ref[...]))
    inv = lax.rsqrt(total * (1.0 / D) + norm_eps)
    spread_rows(inv * (attn_scale * log2_e / shrink), spread_ref)
    for at in range(raw_ref.shape[0]):
        head, row = divmod(at, 4)
        spread = spread_ref[row]
        weights = masked_weights(
            raw_ref[at],
            widened(spread, cache_size),
            widened(top_ref[at] * spread, cache_size),
        )
        inverse = 1.0 / jnp.sum(weights, axis=1, keepdims=True)
        attended = inverse * jnp.dot(
            weights.astype(jnp.bfloat16),
            values_ref[row, :, pl.ds(head * HEAD_DIM, HEAD_DIM)],
            preferred_element_type=jnp.float32,
        )
        for group in range(GROUP):
            attended_ref[head * GROUP + group, pl.ds(4 * row, 4), :] = attended[
                4 * group : 4 * group + 4
            ]
    squares = jnp.zeros((count, LANES), jnp.float32)
    for k in range(width // LANES):
        columns = pl.ds(k * LANES, LANES)
        combined = rows_ref[:, columns].astype(jnp.float32) + attended_ref[k]
        squares += combined * combined
        scaled_ref[:, columns] = (combined * gain_ref[k : k + 1, :].astype(jnp.float32)).astype(
            scaled_ref.dtype
        )
    logits = lax.dot_general(
        scaled_ref[...], head_ref[...], NT, preferred_element_type=jnp.float32
    )
    out_ref[...] = jnp.broadcast_to(jnp.sum(squares, axis=1, keepdims=True), (count, LANES))
    out_ref[:, :ATOMS] = logits


def critic(parts, raw, top, rows, gain, values, head):
    count, width = rows.shape
    return kernel_call(
        critic_kernel,
        array((count, LANES), jnp.float32),
        [VMEM] * 10,
        scratch=[
            pltpu.VMEM((4, 4 * GROUP, LANES), jnp.float32),
            pltpu.VMEM((width // LANES, count, LANES), jnp.float32),
            pltpu.VMEM((count, width), jnp.bfloat16),
        ],
        flops=2 * raw.size * HEAD_DIM,
        moved=2 * values.size + 4 * raw.size,
        name="critic",
    )(*parts, raw, top, rows, gain, values, head)


def expect_kernel(own_ref, one_ref, two_ref, three_ref, out_ref):
    total = own_ref[...] + (one_ref[...] + (two_ref[...] + three_ref[...]))
    lane = lax.broadcasted_iota(jnp.int32, total.shape, 1)
    at = lax.broadcasted_iota(jnp.int32, total.shape, 0)
    logits = lax.rsqrt(total[:, LANES - 1 :] * (1.0 / D) + norm_eps) * total
    real = lane < ATOMS
    logits = jnp.where(real, logits, masked)
    weights = jnp.exp(logits - jnp.max(logits, axis=1, keepdims=True))
    atoms = -atom_span + 2.0 * atom_span * lane.astype(jnp.float32) / (ATOMS - 1)
    value = jnp.sum(weights * atoms, axis=1, keepdims=True) / jnp.sum(
        weights, axis=1, keepdims=True
    )
    placed = jnp.where(lane == lax.shift_right_logical(at, 2), value, 0.0)
    rows = [
        jnp.sum(jnp.where(jnp.bitwise_and(at, 3) == step, placed, 0.0), axis=0, keepdims=True)
        for step in range(4)
    ]
    out_ref[...] = jnp.concatenate(rows, axis=0)[:, :4]


def expect(parts):
    return kernel_call(expect_kernel, array((4, 4), jnp.float32), [VMEM] * 4, name="expect")(*parts)


def swapped(shard, by):
    peers = lax.axis_size("tp")
    return lax.ppermute(shard, "tp", [(i, i ^ by) for i in range(peers)])


def passed_along(shard, axis, by):
    peers = lax.axis_size(axis)
    return lax.ppermute(shard, axis, [(i, (i + by) % peers) for i in range(peers)])


def with_peers(shard):
    return [shard] + [swapped(shard, by) for by in (1, 2, 3)]


def on_device(
    tokens,
    lengths,
    embedding,
    attn_gain,
    key_weight,
    value_weight,
    policy_keys,
    policy_values,
    critic_lengths,
    critic_gain,
    critic_keys,
    critic_values,
    value_gain,
    value_head,
):
    row_groups = lax.axis_size("rows")

    def as_rows(gain):
        return gain.reshape(-1, LANES)

    table = embedding.transpose(1, 2, 0).reshape(embedding.shape[2], embedding.shape[0])
    all_tokens = lax.all_to_all(laid_out(tokens, row_groups), "rows", 0, 0)
    picked, early_values = pick_rows(all_tokens, table, value_weight)
    blocks = lax.all_to_all(picked.reshape(row_groups, -1, LANES), "rows", 0, 0)
    x, query, parts = project(
        blocks.reshape(picked.shape), as_rows(attn_gain), early_values, key_weight, value_weight
    )
    arrived = parts[:1] + [swapped(parts[by], by) for by in (1, 2, 3)]
    raw, top = policy_scores(lengths, query, policy_keys)
    passed = policy(arrived, raw, top, query, x, policy_values)
    rows = passed_along(passed, "rows", row_groups // 2)
    hidden = by_step(passed)

    raw, top = critic_scores(critic_lengths, rows, as_rows(critic_gain), critic_keys)
    logits = critic(
        with_peers(row_squares(rows)),
        raw,
        top,
        rows,
        as_rows(value_gain),
        critic_values,
        value_head.T,
    )
    values = expect(with_peers(logits))
    return hidden, values


def solution(mesh):
    placed = (
        P(None, "rows"),
        P("rows"),
        P(None, "rows", "tp"),
        P("tp"),
        P("tp", None),
        P("tp", None),
        P("rows", None, "tp"),
        P("rows", None, "tp"),
        P("rows"),
        P("tp"),
        P("rows", None, "tp"),
        P("rows", None, "tp"),
        P("tp"),
        P("tp", None),
    )
    return jax.shard_map(
        on_device,
        mesh=mesh,
        in_specs=placed,
        out_specs=(P(None, "rows", "tp"), P(None, "rows")),
        check_vma=False,
    )
```

```python
import functools
import math

import jax
import jax.numpy as jnp
from jax import lax
from jax.experimental import pallas as pl
from jax.experimental.pallas import tpu as pltpu
from jax.sharding import PartitionSpec as P

D = 8192
HEAD_DIM = 128
GROUP = 8
ATOMS = 51
LANES = 128
HALF = 64
MIB = 1024 * 1024

norm_eps = 1e-06
atom_span = 10.0
masked = -1e30
shrink = 2.0**-64
attn_scale = 1.0 / math.sqrt(HEAD_DIM)
log2_e = 1.0 / math.log(2.0)

SMEM = pl.BlockSpec(memory_space=pltpu.SMEM)
VMEM = pl.BlockSpec(memory_space=pltpu.VMEM)
HBM = pl.BlockSpec(memory_space=pltpu.HBM)
NT = (((1,), (1,)), ((), ()))


def kernel_call(body, outs, specs, scratch=(), limit=16, flops=0, moved=0, name=None):
    return pl.pallas_call(
        body,
        out_shape=outs,
        in_specs=specs,
        out_specs=tuple(VMEM for _ in outs) if isinstance(outs, tuple) else VMEM,
        scratch_shapes=scratch,
        compiler_params=pltpu.CompilerParams(vmem_limit_bytes=limit * MIB),
        cost_estimate=pl.CostEstimate(flops=flops, bytes_accessed=moved, transcendentals=0),
        name=name,
    )


def array(shape, dtype):
    return jax.ShapeDtypeStruct(shape, dtype)


def in_hbm(x):
    return pltpu.with_memory_space_constraint(x, pltpu.HBM)


def lay_out_kernel(token_ref, out_ref):
    row = jnp.concatenate([token_ref[step : step + 1, :] for step in range(4)], axis=1)
    out_ref[...] = jnp.broadcast_to(row[None], out_ref.shape)


def laid_out(tokens, copies):
    out = array((copies, 1, tokens.size), tokens.dtype)
    return kernel_call(lay_out_kernel, out, [VMEM], name="lay_out")(tokens)


def pick_rows_kernel(
    token_ref, table_ref, weight_ref, out_ref, early_ref, tiles_ref, sems, early_sem
):
    width = table_ref.shape[0]
    pieces = sems.shape[0]
    destinations = token_ref.shape[0] // pieces
    places = 8 * destinations
    lane = lax.broadcasted_iota(jnp.int32, (width, LANES), 1)

    def token_of(destination, i, half):
        m = 8 * half + i
        return token_ref[destination, 0, 4 * (m % 4) + m // 4]

    for piece in range(pieces):

        def fetch(at, carry):
            destination = piece * destinations + at
            for half in range(2):
                for i in range(8):
                    block = jnp.bitwise_and(token_of(destination, i, half), ~(LANES - 1))
                    pltpu.make_async_copy(
                        table_ref.at[:, pl.ds(pl.multiple_of(block, LANES), LANES)],
                        tiles_ref.at[half, 8 * destination + i],
                        sems.at[piece],
                    ).start()
            return carry

        lax.fori_loop(0, destinations, fetch, 0)

    early = pltpu.make_async_copy(
        weight_ref.at[pl.ds(0, early_ref.shape[0])], early_ref, early_sem
    )
    early.start()
    empty = jnp.zeros((width, LANES), jnp.float32)
    pair = (empty, empty)
    for piece in range(pieces):
        part = tiles_ref.at[:, pl.ds(piece * places, places)]
        pltpu.make_async_copy(part, part, sems.at[piece]).wait()
        first_place = piece * places % LANES

        def step(at, carry):
            destination = piece * destinations + at
            pair = list(carry)
            for i in range(8):
                place = 8 * destination + i
                here = lane == first_place + 8 * at + i
                for half in range(2):
                    shift = jnp.bitwise_and(place - token_of(destination, i, half), LANES - 1)
                    tile = pltpu.roll(tiles_ref[half, place].astype(jnp.float32), shift, 1)
                    pair[half] = jnp.where(here, tile, pair[half])
            return tuple(pair)

        pair = lax.fori_loop(0, destinations, step, pair, unroll=min(destinations, 4))
        if first_place + places == LANES:
            both = jnp.concatenate(pair, axis=0)
            rows = pl.ds((piece + 1) * places - LANES, LANES)
            out_ref[rows, :] = both.T.astype(out_ref.dtype)
            pair = (empty, empty)
    early.wait()


def pick_rows(tokens, table, weight, pieces=8):
    width = table.shape[0]
    rows = tokens.size * width // LANES
    early = (weight.shape[0] * 3 // 4, weight.shape[1])
    return kernel_call(
        pick_rows_kernel,
        (array((rows, LANES), table.dtype), pltpu.VMEM(early, weight.dtype)),
        [SMEM, HBM, HBM],
        scratch=[
            pltpu.VMEM((2, rows, width, LANES), table.dtype),
            pltpu.SemaphoreType.DMA((pieces,)),
            pltpu.SemaphoreType.DMA,
        ],
        limit=24,
        name="pick_rows",
    )(tokens, in_hbm(table), in_hbm(weight))


def project_kernel(
    blocks_ref, gain_ref, early_ref, key_ref, value_ref, x_ref, query_ref, *rest
):
    parts = rest[:4]
    gained_ref, placed_ref, sums_ref, late_ref, keys_ref, sems = rest[4:]
    count, width = x_ref.shape
    kv_width = key_ref.shape[1] // 4
    tp = lax.axis_index("tp")
    early = early_ref.shape[0]
    chunk = width - early
    copies = [pltpu.make_async_copy(value_ref.at[pl.ds(early, chunk)], late_ref, sems.at[0])]
    for at in range(width // chunk):
        rows = pl.ds(at * chunk, chunk)
        copies.append(
            pltpu.make_async_copy(key_ref.at[rows], keys_ref.at[rows], sems.at[at + 1])
        )
    for copy in copies:
        copy.start()
    left = lax.broadcasted_iota(jnp.int32, (8, LANES), 1) < HALF
    squares = jnp.zeros((count, LANES), jnp.float32)
    for k in range(width // LANES):
        pair = blocks_ref[pl.ds(16 * k, 16), :].astype(jnp.float32)
        one, two = pair[:8], pair[8:]
        low = jnp.where(left, one, pltpu.roll(two, HALF, 1))
        high = jnp.where(left, pltpu.roll(one, HALF, 1), two)
        x = jnp.concatenate([low, high], axis=0)
        squares += x * x
        columns = pl.ds(k * LANES, LANES)
        x_ref[:, columns] = x.astype(x_ref.dtype)
        gained = x * gain_ref[k : k + 1, :].astype(jnp.float32)
        gained_ref[:, columns] = gained.astype(gained_ref.dtype)
        head, group = divmod(k, GROUP)
        for row in range(4):
            placed_ref[4 * head + row, pl.ds(4 * group, 4), :] = gained[4 * row : 4 * row + 4]
    query_ref[...] = (placed_ref[...] * shrink).astype(query_ref.dtype)
    total = jnp.broadcast_to(jnp.sum(squares, axis=1, keepdims=True), (count, LANES))

    def product(rows, weight):
        return jnp.dot(gained_ref[:, rows], weight, preferred_element_type=jnp.float32)

    values = product(pl.ds(0, early), early_ref[...])
    copies[0].wait()
    sums_ref[1] = values + product(pl.ds(early, chunk), late_ref[...])
    keys = None
    for at in range(width // chunk):
        rows = pl.ds(at * chunk, chunk)
        copies[at + 1].wait()
        partial = product(rows, keys_ref[rows, :])
        keys = partial if keys is None else keys + partial
    sums_ref[0] = keys
    head = total.astype(jnp.bfloat16)
    tail = jnp.where(total < 3e38, total - head.astype(jnp.float32), 0.0).astype(jnp.bfloat16)
    for by, part_ref in enumerate(parts):
        start = pl.multiple_of(jnp.bitwise_xor(tp, by) * kv_width, kv_width)
        peer = pl.ds(start, kv_width)
        part_ref[:, :kv_width] = sums_ref[0, :, peer].astype(part_ref.dtype)
        part_ref[:, kv_width : 2 * kv_width] = sums_ref[1, :, peer].astype(part_ref.dtype)
        if by == 0:
            part_ref[:, 2 * kv_width :] = total
        else:
            part_ref[:, 2 * kv_width : 2 * kv_width + LANES] = head
            part_ref[:, 2 * kv_width + LANES :] = tail


def project(blocks, gain, early_values, key_weight, value_weight):
    width, kv_all = key_weight.shape
    count = blocks.shape[0] * LANES // width
    early = early_values.shape[0]
    own = array((count, kv_all // 2 + LANES), jnp.float32)
    part = array((count, kv_all // 2 + 2 * LANES), jnp.bfloat16)
    heads = width // (GROUP * HEAD_DIM)
    queries = (4 * heads, 4 * GROUP, HEAD_DIM)
    x, query, *parts = kernel_call(
        project_kernel,
        (array((count, width), jnp.bfloat16), array(queries, jnp.bfloat16), own) + (part,) * 3,
        [VMEM] * 3 + [HBM] * 2,
        scratch=[
            pltpu.VMEM((count, width), jnp.bfloat16),
            pltpu.VMEM(queries, jnp.float32),
            pltpu.VMEM((2, count, kv_all), jnp.float32),
            pltpu.VMEM((width - early, kv_all), key_weight.dtype),
            pltpu.VMEM((width, kv_all), key_weight.dtype),
            pltpu.SemaphoreType.DMA((1 + width // (width - early),)),
        ],
        flops=4 * count * width * kv_all,
        moved=4 * width * kv_all,
        name="project",
    )(
        blocks,
        gain,
        early_values,
        in_hbm(key_weight),
        in_hbm(value_weight),
    )
    return x, query, parts


def masked_scores(query, keys, length, raw_ref, top_ref, at):
    raw = lax.dot_general(query, keys, NT, preferred_element_type=jnp.float32)
    visible = lax.broadcasted_iota(jnp.int32, raw.shape, 1) < length
    raw = jnp.where(visible, raw, masked)
    raw_ref[at] = raw
    top_ref[at] = jnp.broadcast_to(jnp.max(raw, axis=1, keepdims=True), top_ref.shape[1:])


def scores_kernel(length_ref, query_ref, keys_ref, raw_ref, top_ref):
    for at in range(query_ref.shape[0]):
        head, row = divmod(at, 4)
        keys = keys_ref[row, :, pl.ds(head * HEAD_DIM, HEAD_DIM)]
        masked_scores(query_ref[at], keys, length_ref[row], raw_ref, top_ref, at)


def policy_scores(lengths, query, keys):
    raw = array(query.shape[:2] + (keys.shape[1],), jnp.float32)
    return kernel_call(
        scores_kernel,
        (raw, array(query.shape, jnp.float32)),
        [SMEM, VMEM, VMEM],
        flops=2 * raw.size * HEAD_DIM,
        moved=2 * keys.size + 4 * raw.size,
        name="policy_scores",
    )(lengths, query, keys)


def spread_rows(inv, spread_ref):
    for row in range(4):
        for group in range(GROUP):
            spread_ref[row, pl.ds(4 * group, 4), :] = inv[4 * row : 4 * row + 4]


def widened(x, width):
    return jnp.concatenate([x] * (width // LANES), axis=1)


def masked_weights(raw, spread, highest):
    return jnp.where(raw > 0.5 * masked, jnp.exp2(raw * spread - highest), 0.0)


def policy_kernel(
    own_ref,
    one_ref,
    two_ref,
    three_ref,
    raw_ref,
    top_ref,
    query_ref,
    x_ref,
    values_ref,
    passed_ref,
    squares_ref,
    spread_ref,
    rows_ref,
):
    count, width = x_ref.shape
    kv_width = values_ref.shape[2]
    cache_size = values_ref.shape[1]
    total = own_ref[...]
    for part_ref in (one_ref, two_ref, three_ref):
        part = part_ref[...].astype(jnp.float32)
        squares = part[:, 2 * kv_width : 2 * kv_width + LANES] + part[:, 2 * kv_width + LANES :]
        total = total + jnp.concatenate([part[:, : 2 * kv_width], squares], axis=1)
    inv = lax.rsqrt(total[:, 2 * kv_width :] * (1.0 / D) + norm_eps)
    wide = widened(inv, kv_width)
    new_key = (wide * total[:, :kv_width]).astype(jnp.bfloat16)
    new_value = (wide * total[:, kv_width : 2 * kv_width]).astype(jnp.bfloat16)
    spread_rows(inv * (attn_scale * log2_e / shrink), spread_ref)
    queries = query_ref.shape[1]
    at_query = lax.broadcasted_iota(jnp.int32, (4 * queries, count), 0)
    at_fresh = lax.broadcasted_iota(jnp.int32, (4 * queries, count), 1)
    mine = jnp.logical_and(
        lax.div(at_query, queries) == lax.shift_right_logical(at_fresh, 2),
        jnp.bitwise_and(at_fresh, 3) <= jnp.bitwise_and(at_query, 3),
    )
    for head in range(query_ref.shape[0] // 4):
        columns = slice(head * HEAD_DIM, (head + 1) * HEAD_DIM)
        all_queries = query_ref[pl.ds(4 * head, 4)].reshape(4 * queries, HEAD_DIM)
        fresh = lax.dot_general(
            all_queries, new_key[:, columns], NT, preferred_element_type=jnp.float32
        )
        fresh = jnp.where(mine, fresh, masked)
        fresh_top = jnp.max(fresh, axis=1, keepdims=True)
        fresh_weights, attended, inverses = [], [], []
        for row in range(4):
            at = 4 * head + row
            part = slice(row * queries, (row + 1) * queries)
            spread = spread_ref[row]
            highest = jnp.maximum(top_ref[at], fresh_top[part]) * spread
            weights = masked_weights(
                raw_ref[at], widened(spread, cache_size), widened(highest, cache_size)
            )
            extra = masked_weights(fresh[part], spread[:, :count], highest[:, :count])
            inverses.append(
                1.0
                / (jnp.sum(weights, axis=1, keepdims=True) + jnp.sum(extra, axis=1, keepdims=True))
            )
            fresh_weights.append(extra)
            attended.append(
                jnp.dot(
                    weights.astype(jnp.bfloat16),
                    values_ref[row, :, columns],
                    preferred_element_type=jnp.float32,
                )
            )
        fresh_weights = jnp.concatenate(fresh_weights, axis=0).astype(jnp.bfloat16)
        fresh_sum = jnp.dot(
            fresh_weights, new_value[:, columns], preferred_element_type=jnp.float32
        )
        for row in range(4):
            part = slice(row * queries, (row + 1) * queries)
            both = (attended[row] + fresh_sum[part]) * inverses[row]
            for group in range(GROUP):
                rows_ref[head * GROUP + group, pl.ds(4 * row, 4), :] = both[
                    4 * group : 4 * group + 4
                ]
    squares = jnp.zeros((count, LANES), jnp.float32)
    for k in range(width // LANES):
        columns = pl.ds(k * LANES, LANES)
        hidden = (x_ref[:, columns].astype(jnp.float32) + rows_ref[k]).astype(passed_ref.dtype)
        passed_ref[:, columns] = hidden
        hidden = hidden.astype(jnp.float32)
        squares += hidden * hidden
    squares_ref[...] = jnp.broadcast_to(jnp.sum(squares, axis=1, keepdims=True), squares_ref.shape)


def policy(parts, raw, top, query, x, values):
    count, width = x.shape
    return kernel_call(
        policy_kernel,
        (array((count, width), jnp.bfloat16), array((count, LANES), jnp.float32)),
        [VMEM] * 9,
        scratch=[
            pltpu.VMEM((4, 4 * GROUP, LANES), jnp.float32),
            pltpu.VMEM((width // LANES, count, LANES), jnp.float32),
        ],
        flops=2 * raw.size * HEAD_DIM,
        moved=2 * values.size + 4 * raw.size,
        name="policy",
    )(*parts, raw, top, query, x, values)


def by_step_kernel(rows_ref, out_ref, wide_ref):
    for k in range(rows_ref.shape[1] // LANES):
        columns = pl.ds(k * LANES, LANES)
        wide_ref[k] = rows_ref[:, columns].astype(jnp.float32)
        for step in range(4):
            out_ref[step, :, columns] = wide_ref[k, pl.ds(step, 4, stride=4), :].astype(
                out_ref.dtype
            )


def by_step(rows):
    count, width = rows.shape
    return kernel_call(
        by_step_kernel,
        array((4, count // 4, width), rows.dtype),
        [VMEM],
        scratch=[pltpu.VMEM((width // LANES, count, LANES), jnp.float32)],
        moved=16 * rows.size,
        name="by_step",
    )(rows)


def squares_kernel(rows_ref, other_ref, _, out_ref):
    squares = jnp.zeros(out_ref.shape, jnp.float32)
    for k in range(rows_ref.shape[1] // LANES):
        part = rows_ref[:, pl.ds(k * LANES, LANES)].astype(jnp.float32)
        squares += part * part
    out_ref[...] = other_ref[...] + jnp.sum(squares, axis=1, keepdims=True)


def row_squares(rows, other, after):
    return kernel_call(
        squares_kernel,
        array(other.shape, jnp.float32),
        [VMEM, VMEM, pl.BlockSpec(memory_space=pl.ANY)],
        name="row_squares",
    )(rows, other, after)


def critic_scores_kernel(
    length_ref, rows_ref, gain_ref, keys_ref, raw_ref, top_ref, placed_ref
):
    for k in range(rows_ref.shape[1] // LANES):
        columns = pl.ds(k * LANES, LANES)
        gained = rows_ref[:, columns].astype(jnp.float32) * gain_ref[k : k + 1, :].astype(jnp.float32)
        head, group = divmod(k, GROUP)
        for row in range(4):
            placed_ref[4 * head + row, pl.ds(4 * group, 4), :] = gained[4 * row : 4 * row + 4]
    for at in range(placed_ref.shape[0]):
        head, row = divmod(at, 4)
        keys = keys_ref[row, :, pl.ds(head * HEAD_DIM, HEAD_DIM)]
        query = (placed_ref[at] * shrink).astype(jnp.bfloat16)
        masked_scores(query, keys, length_ref[row], raw_ref, top_ref, at)


def critic_scores(lengths, rows, gain, keys):
    heads = keys.shape[2] // HEAD_DIM
    placed = (4 * heads, 4 * GROUP, HEAD_DIM)
    raw = array(placed[:2] + (keys.shape[1],), jnp.float32)
    return kernel_call(
        critic_scores_kernel,
        (raw, array(placed, jnp.float32)),
        [SMEM] + [VMEM] * 3,
        scratch=[pltpu.VMEM(placed, jnp.float32)],
        flops=2 * raw.size * HEAD_DIM,
        moved=2 * keys.size + 4 * raw.size,
        name="critic_scores",
    )(lengths, rows, gain, keys)


def critic_kernel(
    near_ref,
    far_ref,
    raw_ref,
    top_ref,
    rows_ref,
    gain_ref,
    values_ref,
    head_ref,
    out_ref,
    spread_ref,
    attended_ref,
    scaled_ref,
):
    count, width = rows_ref.shape
    cache_size = values_ref.shape[1]
    inv = lax.rsqrt((near_ref[...] + far_ref[...]) * (1.0 / D) + norm_eps)
    spread_rows(inv * (attn_scale * log2_e / shrink), spread_ref)
    for at in range(raw_ref.shape[0]):
        head, row = divmod(at, 4)
        spread = spread_ref[row]
        weights = masked_weights(
            raw_ref[at],
            widened(spread, cache_size),
            widened(top_ref[at] * spread, cache_size),
        )
        inverse = 1.0 / jnp.sum(weights, axis=1, keepdims=True)
        attended = inverse * jnp.dot(
            weights.astype(jnp.bfloat16),
            values_ref[row, :, pl.ds(head * HEAD_DIM, HEAD_DIM)],
            preferred_element_type=jnp.float32,
        )
        for group in range(GROUP):
            attended_ref[head * GROUP + group, pl.ds(4 * row, 4), :] = attended[
                4 * group : 4 * group + 4
            ]
    squares = jnp.zeros((count, LANES), jnp.float32)
    for k in range(width // LANES):
        columns = pl.ds(k * LANES, LANES)
        combined = rows_ref[:, columns].astype(jnp.float32) + attended_ref[k]
        squares += combined * combined
        scaled_ref[:, columns] = (combined * gain_ref[k : k + 1, :].astype(jnp.float32)).astype(
            scaled_ref.dtype
        )
    logits = lax.dot_general(
        scaled_ref[...], head_ref[...], NT, preferred_element_type=jnp.float32
    )
    out_ref[...] = jnp.broadcast_to(jnp.sum(squares, axis=1, keepdims=True), (count, LANES))
    out_ref[:, :ATOMS] = logits


def critic(parts, raw, top, rows, gain, values, head):
    count, width = rows.shape
    return kernel_call(
        critic_kernel,
        array((count, LANES), jnp.float32),
        [VMEM] * 8,
        scratch=[
            pltpu.VMEM((4, 4 * GROUP, LANES), jnp.float32),
            pltpu.VMEM((width // LANES, count, LANES), jnp.float32),
            pltpu.VMEM((count, width), jnp.bfloat16),
        ],
        flops=2 * raw.size * HEAD_DIM,
        moved=2 * values.size + 4 * raw.size,
        name="critic",
    )(*parts, raw, top, rows, gain, values, head)


def expect_kernel(own_ref, one_ref, two_ref, three_ref, out_ref):
    total = own_ref[...] + (one_ref[...] + (two_ref[...] + three_ref[...]))
    lane = lax.broadcasted_iota(jnp.int32, total.shape, 1)
    at = lax.broadcasted_iota(jnp.int32, total.shape, 0)
    logits = lax.rsqrt(total[:, LANES - 1 :] * (1.0 / D) + norm_eps) * total
    real = lane < ATOMS
    logits = jnp.where(real, logits, masked)
    weights = jnp.exp(logits - jnp.max(logits, axis=1, keepdims=True))
    atoms = -atom_span + 2.0 * atom_span * lane.astype(jnp.float32) / (ATOMS - 1)
    value = jnp.sum(weights * atoms, axis=1, keepdims=True) / jnp.sum(
        weights, axis=1, keepdims=True
    )
    placed = jnp.where(lane == lax.shift_right_logical(at, 2), value, 0.0)
    rows = [
        jnp.sum(jnp.where(jnp.bitwise_and(at, 3) == step, placed, 0.0), axis=0, keepdims=True)
        for step in range(4)
    ]
    out_ref[...] = jnp.concatenate(rows, axis=0)[:, :4]


def expect(parts):
    return kernel_call(expect_kernel, array((4, 4), jnp.float32), [VMEM] * 4, name="expect")(*parts)


def swapped(shard, by):
    peers = lax.axis_size("tp")
    return lax.ppermute(shard, "tp", [(i, i ^ by) for i in range(peers)])


def passed_along(shard, axis, by):
    peers = lax.axis_size(axis)
    return lax.ppermute(shard, axis, [(i, (i + by) % peers) for i in range(peers)])


def crossed(shard, by_rows, by_tp):
    peers = lax.axis_size("tp")
    groups = lax.axis_size("rows")
    pairs = [
        (r * peers + t, (r + by_rows) % groups * peers + (t ^ by_tp))
        for r in range(groups)
        for t in range(peers)
    ]
    return lax.ppermute(shard, ("rows", "tp"), pairs)


def with_peers(shard):
    return [shard] + [swapped(shard, by) for by in (1, 2, 3)]


def on_device(
    tokens,
    lengths,
    embedding,
    attn_gain,
    key_weight,
    value_weight,
    policy_keys,
    policy_values,
    critic_lengths,
    critic_gain,
    critic_keys,
    critic_values,
    value_gain,
    value_head,
):
    row_groups = lax.axis_size("rows")

    def as_rows(gain):
        return gain.reshape(-1, LANES)

    table = embedding.transpose(1, 2, 0).reshape(embedding.shape[2], embedding.shape[0])
    all_tokens = lax.all_to_all(laid_out(tokens, row_groups), "rows", 0, 0)
    picked, early_values = pick_rows(all_tokens, table, value_weight)
    blocks = lax.all_to_all(picked.reshape(row_groups, -1, LANES), "rows", 0, 0)
    x, query, parts = project(
        blocks.reshape(picked.shape), as_rows(attn_gain), early_values, key_weight, value_weight
    )
    arrived = parts[:1] + [swapped(parts[by], by) for by in (1, 2, 3)]
    raw, top = policy_scores(lengths, query, policy_keys)
    passed, squares = policy(arrived, raw, top, query, x, policy_values)
    rows = passed_along(passed, "rows", row_groups // 2)
    squares = crossed(squares, row_groups // 2, 2)
    hidden = by_step(passed)

    raw, top = critic_scores(critic_lengths, rows, as_rows(critic_gain), critic_keys)
    near = row_squares(rows, squares, top)
    logits = critic(
        (near, swapped(near, 1)),
        raw,
        top,
        rows,
        as_rows(value_gain),
        critic_values,
        value_head.T,
    )
    values = expect(with_peers(logits))
    return hidden, values


def solution(mesh):
    placed = (
        P(None, "rows"),
        P("rows"),
        P(None, "rows", "tp"),
        P("tp"),
        P("tp", None),
        P("tp", None),
        P("rows", None, "tp"),
        P("rows", None, "tp"),
        P("rows"),
        P("tp"),
        P("rows", None, "tp"),
        P("rows", None, "tp"),
        P("tp"),
        P("tp", None),
    )
    return jax.shard_map(
        on_device,
        mesh=mesh,
        in_specs=placed,
        out_specs=(P(None, "rows", "tp"), P(None, "rows")),
        check_vma=False,
    )
```

```python
import functools
import math

import jax
import jax.numpy as jnp
from jax import lax
from jax.experimental import pallas as pl
from jax.experimental.pallas import tpu as pltpu
from jax.sharding import PartitionSpec as P

D = 8192
HEAD_DIM = 128
GROUP = 8
ATOMS = 51
LANES = 128
HALF = 64
MIB = 1024 * 1024

norm_eps = 1e-06
atom_span = 10.0
masked = -1e30
shrink = 2.0**-64
attn_scale = 1.0 / math.sqrt(HEAD_DIM)
log2_e = 1.0 / math.log(2.0)

SMEM = pl.BlockSpec(memory_space=pltpu.SMEM)
VMEM = pl.BlockSpec(memory_space=pltpu.VMEM)
HBM = pl.BlockSpec(memory_space=pltpu.HBM)
NT = (((1,), (1,)), ((), ()))


def kernel_call(body, outs, specs, scratch=(), limit=16, flops=0, moved=0, name=None):
    return pl.pallas_call(
        body,
        out_shape=outs,
        in_specs=specs,
        out_specs=tuple(VMEM for _ in outs) if isinstance(outs, tuple) else VMEM,
        scratch_shapes=scratch,
        compiler_params=pltpu.CompilerParams(vmem_limit_bytes=limit * MIB),
        cost_estimate=pl.CostEstimate(flops=flops, bytes_accessed=moved, transcendentals=0),
        name=name,
    )


def array(shape, dtype):
    return jax.ShapeDtypeStruct(shape, dtype)


def in_hbm(x):
    return pltpu.with_memory_space_constraint(x, pltpu.HBM)


def lay_out_kernel(token_ref, out_ref):
    row = jnp.concatenate([token_ref[step : step + 1, :] for step in range(4)], axis=1)
    out_ref[...] = jnp.broadcast_to(row[None], out_ref.shape)


def laid_out(tokens, copies):
    out = array((copies, 1, tokens.size), tokens.dtype)
    return kernel_call(lay_out_kernel, out, [VMEM], name="lay_out")(tokens)


def pick_rows_kernel(
    token_ref, table_ref, weight_ref, out_ref, early_ref, tiles_ref, sems, early_sem
):
    width = table_ref.shape[0]
    pieces = sems.shape[0]
    destinations = token_ref.shape[0] // pieces
    places = 8 * destinations
    lane = lax.broadcasted_iota(jnp.int32, (width, LANES), 1)

    def token_of(destination, i, half):
        m = 8 * half + i
        return token_ref[destination, 0, 4 * (m % 4) + m // 4]

    for piece in range(pieces):

        def fetch(at, carry):
            destination = piece * destinations + at
            for half in range(2):
                for i in range(8):
                    block = jnp.bitwise_and(token_of(destination, i, half), ~(LANES - 1))
                    pltpu.make_async_copy(
                        table_ref.at[:, pl.ds(pl.multiple_of(block, LANES), LANES)],
                        tiles_ref.at[half, 8 * destination + i],
                        sems.at[piece],
                    ).start()
            return carry

        lax.fori_loop(0, destinations, fetch, 0)

    early = pltpu.make_async_copy(
        weight_ref.at[pl.ds(0, early_ref.shape[0])], early_ref, early_sem
    )
    early.start()
    empty = jnp.zeros((width, LANES), jnp.float32)
    pair = (empty, empty)
    for piece in range(pieces):
        part = tiles_ref.at[:, pl.ds(piece * places, places)]
        pltpu.make_async_copy(part, part, sems.at[piece]).wait()
        first_place = piece * places % LANES

        def step(at, carry):
            destination = piece * destinations + at
            pair = list(carry)
            for i in range(8):
                place = 8 * destination + i
                here = lane == first_place + 8 * at + i
                for half in range(2):
                    shift = jnp.bitwise_and(place - token_of(destination, i, half), LANES - 1)
                    tile = pltpu.roll(tiles_ref[half, place].astype(jnp.float32), shift, 1)
                    pair[half] = jnp.where(here, tile, pair[half])
            return tuple(pair)

        pair = lax.fori_loop(0, destinations, step, pair, unroll=min(destinations, 4))
        if first_place + places == LANES:
            both = jnp.concatenate(pair, axis=0)
            rows = pl.ds((piece + 1) * places - LANES, LANES)
            out_ref[rows, :] = both.T.astype(out_ref.dtype)
            pair = (empty, empty)
    early.wait()


def pick_rows(tokens, table, weight, pieces=8):
    width = table.shape[0]
    rows = tokens.size * width // LANES
    early = (weight.shape[0] * 3 // 4, weight.shape[1])
    return kernel_call(
        pick_rows_kernel,
        (array((rows, LANES), table.dtype), pltpu.VMEM(early, weight.dtype)),
        [SMEM, HBM, HBM],
        scratch=[
            pltpu.VMEM((2, rows, width, LANES), table.dtype),
            pltpu.SemaphoreType.DMA((pieces,)),
            pltpu.SemaphoreType.DMA,
        ],
        limit=24,
        name="pick_rows",
    )(tokens, in_hbm(table), in_hbm(weight))


def project_kernel(
    blocks_ref, gain_ref, early_ref, key_ref, value_ref, x_ref, query_ref, *rest
):
    parts = rest[:4]
    gained_ref, placed_ref, sums_ref, late_ref, keys_ref, sems = rest[4:]
    count, width = x_ref.shape
    kv_width = key_ref.shape[1] // 4
    tp = lax.axis_index("tp")
    early = early_ref.shape[0]
    chunk = width - early
    copies = [pltpu.make_async_copy(value_ref.at[pl.ds(early, chunk)], late_ref, sems.at[0])]
    for at in range(width // chunk):
        rows = pl.ds(at * chunk, chunk)
        copies.append(
            pltpu.make_async_copy(key_ref.at[rows], keys_ref.at[rows], sems.at[at + 1])
        )
    for copy in copies:
        copy.start()
    left = lax.broadcasted_iota(jnp.int32, (8, LANES), 1) < HALF
    squares = jnp.zeros((count, LANES), jnp.float32)
    for k in range(width // LANES):
        pair = blocks_ref[pl.ds(16 * k, 16), :].astype(jnp.float32)
        one, two = pair[:8], pair[8:]
        low = jnp.where(left, one, pltpu.roll(two, HALF, 1))
        high = jnp.where(left, pltpu.roll(one, HALF, 1), two)
        x = jnp.concatenate([low, high], axis=0)
        squares += x * x
        columns = pl.ds(k * LANES, LANES)
        x_ref[:, columns] = x.astype(x_ref.dtype)
        gained = x * gain_ref[k : k + 1, :].astype(jnp.float32)
        gained_ref[:, columns] = gained.astype(gained_ref.dtype)
        head, group = divmod(k, GROUP)
        for row in range(4):
            placed_ref[4 * head + row, pl.ds(4 * group, 4), :] = gained[4 * row : 4 * row + 4]
    query_ref[...] = (placed_ref[...] * shrink).astype(query_ref.dtype)
    total = jnp.broadcast_to(jnp.sum(squares, axis=1, keepdims=True), (count, LANES))

    def product(rows, weight):
        return jnp.dot(gained_ref[:, rows], weight, preferred_element_type=jnp.float32)

    values = product(pl.ds(0, early), early_ref[...])
    copies[0].wait()
    sums_ref[1] = values + product(pl.ds(early, chunk), late_ref[...])
    keys = None
    for at in range(width // chunk):
        rows = pl.ds(at * chunk, chunk)
        copies[at + 1].wait()
        partial = product(rows, keys_ref[rows, :])
        keys = partial if keys is None else keys + partial
    sums_ref[0] = keys
    head = total.astype(jnp.bfloat16)
    tail = jnp.where(total < 3e38, total - head.astype(jnp.float32), 0.0).astype(jnp.bfloat16)
    for by, part_ref in enumerate(parts):
        start = pl.multiple_of(jnp.bitwise_xor(tp, by) * kv_width, kv_width)
        peer = pl.ds(start, kv_width)
        part_ref[:, :kv_width] = sums_ref[0, :, peer].astype(part_ref.dtype)
        part_ref[:, kv_width : 2 * kv_width] = sums_ref[1, :, peer].astype(part_ref.dtype)
        if by == 0:
            part_ref[:, 2 * kv_width :] = total
        else:
            part_ref[:, 2 * kv_width : 2 * kv_width + LANES] = head
            part_ref[:, 2 * kv_width + LANES :] = tail


def project(blocks, gain, early_values, key_weight, value_weight):
    width, kv_all = key_weight.shape
    count = blocks.shape[0] * LANES // width
    early = early_values.shape[0]
    own = array((count, kv_all // 2 + LANES), jnp.float32)
    part = array((count, kv_all // 2 + 2 * LANES), jnp.bfloat16)
    heads = width // (GROUP * HEAD_DIM)
    queries = (4 * heads, 4 * GROUP, HEAD_DIM)
    x, query, *parts = kernel_call(
        project_kernel,
        (array((count, width), jnp.bfloat16), array(queries, jnp.bfloat16), own) + (part,) * 3,
        [VMEM] * 3 + [HBM] * 2,
        scratch=[
            pltpu.VMEM((count, width), jnp.bfloat16),
            pltpu.VMEM(queries, jnp.float32),
            pltpu.VMEM((2, count, kv_all), jnp.float32),
            pltpu.VMEM((width - early, kv_all), key_weight.dtype),
            pltpu.VMEM((width, kv_all), key_weight.dtype),
            pltpu.SemaphoreType.DMA((1 + width // (width - early),)),
        ],
        flops=4 * count * width * kv_all,
        moved=4 * width * kv_all,
        name="project",
    )(
        blocks,
        gain,
        early_values,
        in_hbm(key_weight),
        in_hbm(value_weight),
    )
    return x, query, parts


def masked_scores(query, keys, length, raw_ref, top_ref, at):
    raw = lax.dot_general(query, keys, NT, preferred_element_type=jnp.float32)
    visible = lax.broadcasted_iota(jnp.int32, raw.shape, 1) < length
    raw = jnp.where(visible, raw, masked)
    raw_ref[at] = raw
    top_ref[at] = jnp.broadcast_to(jnp.max(raw, axis=1, keepdims=True), top_ref.shape[1:])


def scores_kernel(length_ref, query_ref, keys_ref, raw_ref, top_ref):
    for at in range(query_ref.shape[0]):
        head, row = divmod(at, 4)
        keys = keys_ref[row, :, pl.ds(head * HEAD_DIM, HEAD_DIM)]
        masked_scores(query_ref[at], keys, length_ref[row], raw_ref, top_ref, at)


def policy_scores(lengths, query, keys):
    raw = array(query.shape[:2] + (keys.shape[1],), jnp.float32)
    return kernel_call(
        scores_kernel,
        (raw, array(query.shape, jnp.float32)),
        [SMEM, VMEM, VMEM],
        flops=2 * raw.size * HEAD_DIM,
        moved=2 * keys.size + 4 * raw.size,
        name="policy_scores",
    )(lengths, query, keys)


def spread_rows(inv, spread_ref):
    for row in range(4):
        for group in range(GROUP):
            spread_ref[row, pl.ds(4 * group, 4), :] = inv[4 * row : 4 * row + 4]


def widened(x, width):
    return jnp.concatenate([x] * (width // LANES), axis=1)


def masked_weights(raw, spread, highest):
    return jnp.where(raw > 0.5 * masked, jnp.exp2(raw * spread - highest), 0.0)


def policy_kernel(
    own_ref,
    one_ref,
    two_ref,
    three_ref,
    raw_ref,
    top_ref,
    query_ref,
    x_ref,
    values_ref,
    passed_ref,
    squares_ref,
    spread_ref,
    rows_ref,
):
    count, width = x_ref.shape
    kv_width = values_ref.shape[2]
    cache_size = values_ref.shape[1]
    total = own_ref[...]
    for part_ref in (one_ref, two_ref, three_ref):
        part = part_ref[...].astype(jnp.float32)
        squares = part[:, 2 * kv_width : 2 * kv_width + LANES] + part[:, 2 * kv_width + LANES :]
        total = total + jnp.concatenate([part[:, : 2 * kv_width], squares], axis=1)
    inv = lax.rsqrt(total[:, 2 * kv_width :] * (1.0 / D) + norm_eps)
    wide = widened(inv, kv_width)
    new_key = (wide * total[:, :kv_width]).astype(jnp.bfloat16)
    new_value = (wide * total[:, kv_width : 2 * kv_width]).astype(jnp.bfloat16)
    spread_rows(inv * (attn_scale * log2_e / shrink), spread_ref)
    queries = query_ref.shape[1]
    at_query = lax.broadcasted_iota(jnp.int32, (4 * queries, count), 0)
    at_fresh = lax.broadcasted_iota(jnp.int32, (4 * queries, count), 1)
    mine = jnp.logical_and(
        lax.div(at_query, queries) == lax.shift_right_logical(at_fresh, 2),
        jnp.bitwise_and(at_fresh, 3) <= jnp.bitwise_and(at_query, 3),
    )
    for head in range(query_ref.shape[0] // 4):
        columns = slice(head * HEAD_DIM, (head + 1) * HEAD_DIM)
        all_queries = query_ref[pl.ds(4 * head, 4)].reshape(4 * queries, HEAD_DIM)
        fresh = lax.dot_general(
            all_queries, new_key[:, columns], NT, preferred_element_type=jnp.float32
        )
        fresh = jnp.where(mine, fresh, masked)
        fresh_top = jnp.max(fresh, axis=1, keepdims=True)
        fresh_weights, attended, inverses = [], [], []
        for row in range(4):
            at = 4 * head + row
            part = slice(row * queries, (row + 1) * queries)
            spread = spread_ref[row]
            highest = jnp.maximum(top_ref[at], fresh_top[part]) * spread
            weights = masked_weights(
                raw_ref[at], widened(spread, cache_size), widened(highest, cache_size)
            )
            extra = masked_weights(fresh[part], spread[:, :count], highest[:, :count])
            inverses.append(
                1.0
                / (jnp.sum(weights, axis=1, keepdims=True) + jnp.sum(extra, axis=1, keepdims=True))
            )
            fresh_weights.append(extra)
            attended.append(
                jnp.dot(
                    weights.astype(jnp.bfloat16),
                    values_ref[row, :, columns],
                    preferred_element_type=jnp.float32,
                )
            )
        fresh_weights = jnp.concatenate(fresh_weights, axis=0).astype(jnp.bfloat16)
        fresh_sum = jnp.dot(
            fresh_weights, new_value[:, columns], preferred_element_type=jnp.float32
        )
        for row in range(4):
            part = slice(row * queries, (row + 1) * queries)
            both = (attended[row] + fresh_sum[part]) * inverses[row]
            for group in range(GROUP):
                rows_ref[head * GROUP + group, pl.ds(4 * row, 4), :] = both[
                    4 * group : 4 * group + 4
                ]
    squares = jnp.zeros((count, LANES), jnp.float32)
    for k in range(width // LANES):
        columns = pl.ds(k * LANES, LANES)
        hidden = (x_ref[:, columns].astype(jnp.float32) + rows_ref[k]).astype(passed_ref.dtype)
        passed_ref[:, columns] = hidden
        hidden = hidden.astype(jnp.float32)
        squares += hidden * hidden
    squares_ref[...] = jnp.broadcast_to(jnp.sum(squares, axis=1, keepdims=True), squares_ref.shape)


def policy(parts, raw, top, query, x, values):
    count, width = x.shape
    return kernel_call(
        policy_kernel,
        (array((count, width), jnp.bfloat16), array((count, LANES), jnp.float32)),
        [VMEM] * 9,
        scratch=[
            pltpu.VMEM((4, 4 * GROUP, LANES), jnp.float32),
            pltpu.VMEM((width // LANES, count, LANES), jnp.float32),
        ],
        flops=2 * raw.size * HEAD_DIM,
        moved=2 * values.size + 4 * raw.size,
        name="policy",
    )(*parts, raw, top, query, x, values)


def by_step_kernel(rows_ref, out_ref, wide_ref):
    for k in range(rows_ref.shape[1] // LANES):
        columns = pl.ds(k * LANES, LANES)
        wide_ref[k] = rows_ref[:, columns].astype(jnp.float32)
        for step in range(4):
            out_ref[step, :, columns] = wide_ref[k, pl.ds(step, 4, stride=4), :].astype(
                out_ref.dtype
            )


def by_step(rows):
    count, width = rows.shape
    return kernel_call(
        by_step_kernel,
        array((4, count // 4, width), rows.dtype),
        [VMEM],
        scratch=[pltpu.VMEM((width // LANES, count, LANES), jnp.float32)],
        moved=16 * rows.size,
        name="by_step",
    )(rows)


def add_kernel(one_ref, two_ref, out_ref):
    out_ref[...] = one_ref[...] + two_ref[...]


def added(one, two):
    return kernel_call(add_kernel, array(one.shape, one.dtype), [VMEM] * 2, name="add")(one, two)


def squares_kernel(rows_ref, out_ref):
    squares = jnp.zeros(out_ref.shape, jnp.float32)
    for k in range(rows_ref.shape[1] // LANES):
        part = rows_ref[:, pl.ds(k * LANES, LANES)].astype(jnp.float32)
        squares += part * part
    out_ref[...] = jnp.broadcast_to(jnp.sum(squares, axis=1, keepdims=True), out_ref.shape)


def row_squares(rows):
    return kernel_call(
        squares_kernel, array((rows.shape[0], LANES), jnp.float32), [VMEM], name="row_squares"
    )(rows)


def critic_scores_kernel(
    length_ref, rows_ref, gain_ref, keys_ref, raw_ref, top_ref, placed_ref
):
    for k in range(rows_ref.shape[1] // LANES):
        columns = pl.ds(k * LANES, LANES)
        gained = rows_ref[:, columns].astype(jnp.float32) * gain_ref[k : k + 1, :].astype(jnp.float32)
        head, group = divmod(k, GROUP)
        for row in range(4):
            placed_ref[4 * head + row, pl.ds(4 * group, 4), :] = gained[4 * row : 4 * row + 4]
    for at in range(placed_ref.shape[0]):
        head, row = divmod(at, 4)
        keys = keys_ref[row, :, pl.ds(head * HEAD_DIM, HEAD_DIM)]
        query = (placed_ref[at] * shrink).astype(jnp.bfloat16)
        masked_scores(query, keys, length_ref[row], raw_ref, top_ref, at)


def critic_scores(lengths, rows, gain, keys):
    heads = keys.shape[2] // HEAD_DIM
    placed = (4 * heads, 4 * GROUP, HEAD_DIM)
    raw = array(placed[:2] + (keys.shape[1],), jnp.float32)
    return kernel_call(
        critic_scores_kernel,
        (raw, array(placed, jnp.float32)),
        [SMEM] + [VMEM] * 3,
        scratch=[pltpu.VMEM(placed, jnp.float32)],
        flops=2 * raw.size * HEAD_DIM,
        moved=2 * keys.size + 4 * raw.size,
        name="critic_scores",
    )(lengths, rows, gain, keys)


def critic_kernel(
    own_ref,
    near_ref,
    far_ref,
    raw_ref,
    top_ref,
    rows_ref,
    gain_ref,
    values_ref,
    head_ref,
    out_ref,
    spread_ref,
    attended_ref,
    scaled_ref,
):
    count, width = rows_ref.shape
    cache_size = values_ref.shape[1]
    total = (own_ref[...] + near_ref[...]) + far_ref[...]
    inv = lax.rsqrt(total * (1.0 / D) + norm_eps)
    spread_rows(inv * (attn_scale * log2_e / shrink), spread_ref)
    for at in range(raw_ref.shape[0]):
        head, row = divmod(at, 4)
        spread = spread_ref[row]
        weights = masked_weights(
            raw_ref[at],
            widened(spread, cache_size),
            widened(top_ref[at] * spread, cache_size),
        )
        inverse = 1.0 / jnp.sum(weights, axis=1, keepdims=True)
        attended = inverse * jnp.dot(
            weights.astype(jnp.bfloat16),
            values_ref[row, :, pl.ds(head * HEAD_DIM, HEAD_DIM)],
            preferred_element_type=jnp.float32,
        )
        for group in range(GROUP):
            attended_ref[head * GROUP + group, pl.ds(4 * row, 4), :] = attended[
                4 * group : 4 * group + 4
            ]
    squares = jnp.zeros((count, LANES), jnp.float32)
    for k in range(width // LANES):
        columns = pl.ds(k * LANES, LANES)
        combined = rows_ref[:, columns].astype(jnp.float32) + attended_ref[k]
        squares += combined * combined
        scaled_ref[:, columns] = (combined * gain_ref[k : k + 1, :].astype(jnp.float32)).astype(
            scaled_ref.dtype
        )
    logits = lax.dot_general(
        scaled_ref[...], head_ref[...], NT, preferred_element_type=jnp.float32
    )
    out_ref[...] = jnp.broadcast_to(jnp.sum(squares, axis=1, keepdims=True), (count, LANES))
    out_ref[:, :ATOMS] = logits


def critic(parts, raw, top, rows, gain, values, head):
    count, width = rows.shape
    return kernel_call(
        critic_kernel,
        array((count, LANES), jnp.float32),
        [VMEM] * 9,
        scratch=[
            pltpu.VMEM((4, 4 * GROUP, LANES), jnp.float32),
            pltpu.VMEM((width // LANES, count, LANES), jnp.float32),
            pltpu.VMEM((count, width), jnp.bfloat16),
        ],
        flops=2 * raw.size * HEAD_DIM,
        moved=2 * values.size + 4 * raw.size,
        name="critic",
    )(*parts, raw, top, rows, gain, values, head)


def expect_kernel(own_ref, one_ref, two_ref, three_ref, out_ref):
    total = own_ref[...] + (one_ref[...] + (two_ref[...] + three_ref[...]))
    lane = lax.broadcasted_iota(jnp.int32, total.shape, 1)
    at = lax.broadcasted_iota(jnp.int32, total.shape, 0)
    logits = lax.rsqrt(total[:, LANES - 1 :] * (1.0 / D) + norm_eps) * total
    real = lane < ATOMS
    logits = jnp.where(real, logits, masked)
    weights = jnp.exp(logits - jnp.max(logits, axis=1, keepdims=True))
    atoms = -atom_span + 2.0 * atom_span * lane.astype(jnp.float32) / (ATOMS - 1)
    value = jnp.sum(weights * atoms, axis=1, keepdims=True) / jnp.sum(
        weights, axis=1, keepdims=True
    )
    placed = jnp.where(lane == lax.shift_right_logical(at, 2), value, 0.0)
    rows = [
        jnp.sum(jnp.where(jnp.bitwise_and(at, 3) == step, placed, 0.0), axis=0, keepdims=True)
        for step in range(4)
    ]
    out_ref[...] = jnp.concatenate(rows, axis=0)[:, :4]


def expect(parts):
    return kernel_call(expect_kernel, array((4, 4), jnp.float32), [VMEM] * 4, name="expect")(*parts)


def swapped(shard, by):
    peers = lax.axis_size("tp")
    return lax.ppermute(shard, "tp", [(i, i ^ by) for i in range(peers)])


def passed_along(shard, axis, by):
    peers = lax.axis_size(axis)
    return lax.ppermute(shard, axis, [(i, (i + by) % peers) for i in range(peers)])


def crossed(shard, by_rows, by_tp):
    peers = lax.axis_size("tp")
    groups = lax.axis_size("rows")
    pairs = [
        (r * peers + t, (r + by_rows) % groups * peers + (t ^ by_tp))
        for r in range(groups)
        for t in range(peers)
    ]
    return lax.ppermute(shard, ("rows", "tp"), pairs)


def with_peers(shard):
    return [shard] + [swapped(shard, by) for by in (1, 2, 3)]


def on_device(
    tokens,
    lengths,
    embedding,
    attn_gain,
    key_weight,
    value_weight,
    policy_keys,
    policy_values,
    critic_lengths,
    critic_gain,
    critic_keys,
    critic_values,
    value_gain,
    value_head,
):
    row_groups = lax.axis_size("rows")

    def as_rows(gain):
        return gain.reshape(-1, LANES)

    table = embedding.transpose(1, 2, 0).reshape(embedding.shape[2], embedding.shape[0])
    all_tokens = lax.all_to_all(laid_out(tokens, row_groups), "rows", 0, 0)
    picked, early_values = pick_rows(all_tokens, table, value_weight)
    blocks = lax.all_to_all(picked.reshape(row_groups, -1, LANES), "rows", 0, 0)
    x, query, parts = project(
        blocks.reshape(picked.shape), as_rows(attn_gain), early_values, key_weight, value_weight
    )
    arrived = parts[:1] + [swapped(parts[by], by) for by in (1, 2, 3)]
    raw, top = policy_scores(lengths, query, policy_keys)
    passed, squares = policy(arrived, raw, top, query, x, policy_values)
    rows = passed_along(passed, "rows", row_groups // 2)
    far = crossed(added(squares, swapped(squares, 1)), row_groups // 2, 2)
    hidden = by_step(passed)

    raw, top = critic_scores(critic_lengths, rows, as_rows(critic_gain), critic_keys)
    own = row_squares(rows)
    logits = critic(
        (own, swapped(own, 1), far),
        raw,
        top,
        rows,
        as_rows(value_gain),
        critic_values,
        value_head.T,
    )
    values = expect(with_peers(logits))
    return hidden, values


def solution(mesh):
    placed = (
        P(None, "rows"),
        P("rows"),
        P(None, "rows", "tp"),
        P("tp"),
        P("tp", None),
        P("tp", None),
        P("rows", None, "tp"),
        P("rows", None, "tp"),
        P("rows"),
        P("tp"),
        P("rows", None, "tp"),
        P("rows", None, "tp"),
        P("tp"),
        P("tp", None),
    )
    return jax.shard_map(
        on_device,
        mesh=mesh,
        in_specs=placed,
        out_specs=(P(None, "rows", "tp"), P(None, "rows")),
        check_vma=False,
    )
```

```python
import functools
import math

import jax
import jax.numpy as jnp
from jax import lax
from jax.experimental import pallas as pl
from jax.experimental.pallas import tpu as pltpu
from jax.sharding import PartitionSpec as P

D = 8192
HEAD_DIM = 128
GROUP = 8
ATOMS = 51
LANES = 128
HALF = 64
MIB = 1024 * 1024

norm_eps = 1e-06
atom_span = 10.0
masked = -1e30
shrink = 2.0**-64
attn_scale = 1.0 / math.sqrt(HEAD_DIM)
log2_e = 1.0 / math.log(2.0)

SMEM = pl.BlockSpec(memory_space=pltpu.SMEM)
VMEM = pl.BlockSpec(memory_space=pltpu.VMEM)
HBM = pl.BlockSpec(memory_space=pltpu.HBM)
NT = (((1,), (1,)), ((), ()))


def kernel_call(body, outs, specs, scratch=(), limit=16, flops=0, moved=0, name=None):
    return pl.pallas_call(
        body,
        out_shape=outs,
        in_specs=specs,
        out_specs=tuple(VMEM for _ in outs) if isinstance(outs, tuple) else VMEM,
        scratch_shapes=scratch,
        compiler_params=pltpu.CompilerParams(vmem_limit_bytes=limit * MIB),
        cost_estimate=pl.CostEstimate(flops=flops, bytes_accessed=moved, transcendentals=0),
        name=name,
    )


def array(shape, dtype):
    return jax.ShapeDtypeStruct(shape, dtype)


def in_hbm(x):
    return pltpu.with_memory_space_constraint(x, pltpu.HBM)


def lay_out_kernel(token_ref, out_ref):
    row = jnp.concatenate([token_ref[step : step + 1, :] for step in range(4)], axis=1)
    out_ref[...] = jnp.broadcast_to(row[None], out_ref.shape)


def laid_out(tokens, copies):
    out = array((copies, 1, tokens.size), tokens.dtype)
    return kernel_call(lay_out_kernel, out, [VMEM], name="lay_out")(tokens)


def pick_rows_kernel(
    source_ref,
    table_ref,
    weight_ref,
    out_ref,
    early_ref,
    token_ref,
    tiles_ref,
    sems,
    early_sem,
    token_sem,
):
    early = pltpu.make_async_copy(
        weight_ref.at[pl.ds(0, early_ref.shape[0])], early_ref, early_sem
    )
    early.start()
    tokens = pltpu.make_async_copy(source_ref, token_ref, token_sem)
    tokens.start()
    tokens.wait()
    width = table_ref.shape[0]
    pieces = sems.shape[0]
    destinations = token_ref.shape[0] // pieces
    places = 8 * destinations
    lane = lax.broadcasted_iota(jnp.int32, (width, LANES), 1)

    def token_of(destination, i, half):
        m = 8 * half + i
        return token_ref[destination, 0, 4 * (m % 4) + m // 4]

    for piece in range(pieces):

        def fetch(at, carry):
            destination = piece * destinations + at
            for half in range(2):
                for i in range(8):
                    block = jnp.bitwise_and(token_of(destination, i, half), ~(LANES - 1))
                    pltpu.make_async_copy(
                        table_ref.at[:, pl.ds(pl.multiple_of(block, LANES), LANES)],
                        tiles_ref.at[half, 8 * destination + i],
                        sems.at[piece],
                    ).start()
            return carry

        lax.fori_loop(0, destinations, fetch, 0)

    empty = jnp.zeros((width, LANES), jnp.float32)
    pair = (empty, empty)
    for piece in range(pieces):
        part = tiles_ref.at[:, pl.ds(piece * places, places)]
        pltpu.make_async_copy(part, part, sems.at[piece]).wait()
        first_place = piece * places % LANES

        def step(at, carry):
            destination = piece * destinations + at
            pair = list(carry)
            for i in range(8):
                place = 8 * destination + i
                here = lane == first_place + 8 * at + i
                for half in range(2):
                    shift = jnp.bitwise_and(place - token_of(destination, i, half), LANES - 1)
                    tile = pltpu.roll(tiles_ref[half, place].astype(jnp.float32), shift, 1)
                    pair[half] = jnp.where(here, tile, pair[half])
            return tuple(pair)

        pair = lax.fori_loop(0, destinations, step, pair, unroll=min(destinations, 4))
        if first_place + places == LANES:
            both = jnp.concatenate(pair, axis=0)
            rows = pl.ds((piece + 1) * places - LANES, LANES)
            out_ref[rows, :] = both.T.astype(out_ref.dtype)
            pair = (empty, empty)
    early.wait()


def pick_rows(tokens, table, weight, pieces=8):
    width = table.shape[0]
    rows = tokens.size * width // LANES
    early = (weight.shape[0] * 3 // 4, weight.shape[1])
    return kernel_call(
        pick_rows_kernel,
        (array((rows, LANES), table.dtype), pltpu.VMEM(early, weight.dtype)),
        [VMEM, HBM, HBM],
        scratch=[
            pltpu.SMEM(tokens.shape, tokens.dtype),
            pltpu.VMEM((2, rows, width, LANES), table.dtype),
            pltpu.SemaphoreType.DMA((pieces,)),
            pltpu.SemaphoreType.DMA,
            pltpu.SemaphoreType.DMA,
        ],
        limit=24,
        name="pick_rows",
    )(tokens, in_hbm(table), in_hbm(weight))


def project_kernel(
    blocks_ref, gain_ref, early_ref, key_ref, value_ref, x_ref, query_ref, *rest
):
    parts = rest[:4]
    gained_ref, placed_ref, sums_ref, late_ref, keys_ref, sems = rest[4:]
    count, width = x_ref.shape
    kv_width = key_ref.shape[1] // 4
    tp = lax.axis_index("tp")
    early = early_ref.shape[0]
    chunk = width - early
    copies = [pltpu.make_async_copy(value_ref.at[pl.ds(early, chunk)], late_ref, sems.at[0])]
    for at in range(width // chunk):
        rows = pl.ds(at * chunk, chunk)
        copies.append(
            pltpu.make_async_copy(key_ref.at[rows], keys_ref.at[rows], sems.at[at + 1])
        )
    for copy in copies:
        copy.start()
    left = lax.broadcasted_iota(jnp.int32, (8, LANES), 1) < HALF
    squares = jnp.zeros((count, LANES), jnp.float32)
    for k in range(width // LANES):
        pair = blocks_ref[pl.ds(16 * k, 16), :].astype(jnp.float32)
        one, two = pair[:8], pair[8:]
        low = jnp.where(left, one, pltpu.roll(two, HALF, 1))
        high = jnp.where(left, pltpu.roll(one, HALF, 1), two)
        x = jnp.concatenate([low, high], axis=0)
        squares += x * x
        columns = pl.ds(k * LANES, LANES)
        x_ref[:, columns] = x.astype(x_ref.dtype)
        gained = x * gain_ref[k : k + 1, :].astype(jnp.float32)
        gained_ref[:, columns] = gained.astype(gained_ref.dtype)
        head, group = divmod(k, GROUP)
        for row in range(4):
            placed_ref[4 * head + row, pl.ds(4 * group, 4), :] = gained[4 * row : 4 * row + 4]
    query_ref[...] = (placed_ref[...] * shrink).astype(query_ref.dtype)
    total = jnp.broadcast_to(jnp.sum(squares, axis=1, keepdims=True), (count, LANES))

    def product(rows, weight):
        return jnp.dot(gained_ref[:, rows], weight, preferred_element_type=jnp.float32)

    values = product(pl.ds(0, early), early_ref[...])
    copies[0].wait()
    sums_ref[1] = values + product(pl.ds(early, chunk), late_ref[...])
    keys = None
    for at in range(width // chunk):
        rows = pl.ds(at * chunk, chunk)
        copies[at + 1].wait()
        partial = product(rows, keys_ref[rows, :])
        keys = partial if keys is None else keys + partial
    sums_ref[0] = keys
    head = total.astype(jnp.bfloat16)
    tail = jnp.where(total < 3e38, total - head.astype(jnp.float32), 0.0).astype(jnp.bfloat16)
    for by, part_ref in enumerate(parts):
        start = pl.multiple_of(jnp.bitwise_xor(tp, by) * kv_width, kv_width)
        peer = pl.ds(start, kv_width)
        part_ref[:, :kv_width] = sums_ref[0, :, peer].astype(part_ref.dtype)
        part_ref[:, kv_width : 2 * kv_width] = sums_ref[1, :, peer].astype(part_ref.dtype)
        if by == 0:
            part_ref[:, 2 * kv_width :] = total
        else:
            part_ref[:, 2 * kv_width : 2 * kv_width + LANES] = head
            part_ref[:, 2 * kv_width + LANES :] = tail


def project(blocks, gain, early_values, key_weight, value_weight):
    width, kv_all = key_weight.shape
    count = blocks.shape[0] * LANES // width
    early = early_values.shape[0]
    own = array((count, kv_all // 2 + LANES), jnp.float32)
    part = array((count, kv_all // 2 + 2 * LANES), jnp.bfloat16)
    heads = width // (GROUP * HEAD_DIM)
    queries = (4 * heads, 4 * GROUP, HEAD_DIM)
    x, query, *parts = kernel_call(
        project_kernel,
        (array((count, width), jnp.bfloat16), array(queries, jnp.bfloat16), own) + (part,) * 3,
        [VMEM] * 3 + [HBM] * 2,
        scratch=[
            pltpu.VMEM((count, width), jnp.bfloat16),
            pltpu.VMEM(queries, jnp.float32),
            pltpu.VMEM((2, count, kv_all), jnp.float32),
            pltpu.VMEM((width - early, kv_all), key_weight.dtype),
            pltpu.VMEM((width, kv_all), key_weight.dtype),
            pltpu.SemaphoreType.DMA((1 + width // (width - early),)),
        ],
        flops=4 * count * width * kv_all,
        moved=4 * width * kv_all,
        name="project",
    )(
        blocks,
        gain,
        early_values,
        in_hbm(key_weight),
        in_hbm(value_weight),
    )
    return x, query, parts


def masked_scores(query, keys, length, raw_ref, top_ref, at):
    raw = lax.dot_general(query, keys, NT, preferred_element_type=jnp.float32)
    visible = lax.broadcasted_iota(jnp.int32, raw.shape, 1) < length
    raw = jnp.where(visible, raw, masked)
    raw_ref[at] = raw
    top_ref[at] = jnp.broadcast_to(jnp.max(raw, axis=1, keepdims=True), top_ref.shape[1:])


def scores_kernel(length_ref, query_ref, keys_ref, raw_ref, top_ref):
    for at in range(query_ref.shape[0]):
        head, row = divmod(at, 4)
        keys = keys_ref[row, :, pl.ds(head * HEAD_DIM, HEAD_DIM)]
        masked_scores(query_ref[at], keys, length_ref[row], raw_ref, top_ref, at)


def policy_scores(lengths, query, keys):
    raw = array(query.shape[:2] + (keys.shape[1],), jnp.float32)
    return kernel_call(
        scores_kernel,
        (raw, array(query.shape, jnp.float32)),
        [SMEM, VMEM, VMEM],
        flops=2 * raw.size * HEAD_DIM,
        moved=2 * keys.size + 4 * raw.size,
        name="policy_scores",
    )(lengths, query, keys)


def spread_rows(inv, spread_ref):
    for row in range(4):
        for group in range(GROUP):
            spread_ref[row, pl.ds(4 * group, 4), :] = inv[4 * row : 4 * row + 4]


def widened(x, width):
    return jnp.concatenate([x] * (width // LANES), axis=1)


def masked_weights(raw, spread, highest):
    return jnp.where(raw > 0.5 * masked, jnp.exp2(raw * spread - highest), 0.0)


def policy_kernel(
    own_ref,
    one_ref,
    two_ref,
    three_ref,
    raw_ref,
    top_ref,
    query_ref,
    x_ref,
    values_ref,
    passed_ref,
    squares_ref,
    spread_ref,
    rows_ref,
):
    count, width = x_ref.shape
    kv_width = values_ref.shape[2]
    cache_size = values_ref.shape[1]
    total = own_ref[...]
    for part_ref in (one_ref, two_ref, three_ref):
        part = part_ref[...].astype(jnp.float32)
        squares = part[:, 2 * kv_width : 2 * kv_width + LANES] + part[:, 2 * kv_width + LANES :]
        total = total + jnp.concatenate([part[:, : 2 * kv_width], squares], axis=1)
    inv = lax.rsqrt(total[:, 2 * kv_width :] * (1.0 / D) + norm_eps)
    wide = widened(inv, kv_width)
    new_key = (wide * total[:, :kv_width]).astype(jnp.bfloat16)
    new_value = (wide * total[:, kv_width : 2 * kv_width]).astype(jnp.bfloat16)
    spread_rows(inv * (attn_scale * log2_e / shrink), spread_ref)
    queries = query_ref.shape[1]
    at_query = lax.broadcasted_iota(jnp.int32, (4 * queries, count), 0)
    at_fresh = lax.broadcasted_iota(jnp.int32, (4 * queries, count), 1)
    mine = jnp.logical_and(
        lax.div(at_query, queries) == lax.shift_right_logical(at_fresh, 2),
        jnp.bitwise_and(at_fresh, 3) <= jnp.bitwise_and(at_query, 3),
    )
    for head in range(query_ref.shape[0] // 4):
        columns = slice(head * HEAD_DIM, (head + 1) * HEAD_DIM)
        all_queries = query_ref[pl.ds(4 * head, 4)].reshape(4 * queries, HEAD_DIM)
        fresh = lax.dot_general(
            all_queries, new_key[:, columns], NT, preferred_element_type=jnp.float32
        )
        fresh = jnp.where(mine, fresh, masked)
        fresh_top = jnp.max(fresh, axis=1, keepdims=True)
        fresh_weights, attended, inverses = [], [], []
        for row in range(4):
            at = 4 * head + row
            part = slice(row * queries, (row + 1) * queries)
            spread = spread_ref[row]
            highest = jnp.maximum(top_ref[at], fresh_top[part]) * spread
            weights = masked_weights(
                raw_ref[at], widened(spread, cache_size), widened(highest, cache_size)
            )
            extra = masked_weights(fresh[part], spread[:, :count], highest[:, :count])
            inverses.append(
                1.0
                / (jnp.sum(weights, axis=1, keepdims=True) + jnp.sum(extra, axis=1, keepdims=True))
            )
            fresh_weights.append(extra)
            attended.append(
                jnp.dot(
                    weights.astype(jnp.bfloat16),
                    values_ref[row, :, columns],
                    preferred_element_type=jnp.float32,
                )
            )
        fresh_weights = jnp.concatenate(fresh_weights, axis=0).astype(jnp.bfloat16)
        fresh_sum = jnp.dot(
            fresh_weights, new_value[:, columns], preferred_element_type=jnp.float32
        )
        for row in range(4):
            part = slice(row * queries, (row + 1) * queries)
            both = (attended[row] + fresh_sum[part]) * inverses[row]
            for group in range(GROUP):
                rows_ref[head * GROUP + group, pl.ds(4 * row, 4), :] = both[
                    4 * group : 4 * group + 4
                ]
    squares = jnp.zeros((count, LANES), jnp.float32)
    for k in range(width // LANES):
        columns = pl.ds(k * LANES, LANES)
        hidden = (x_ref[:, columns].astype(jnp.float32) + rows_ref[k]).astype(passed_ref.dtype)
        passed_ref[:, columns] = hidden
        hidden = hidden.astype(jnp.float32)
        squares += hidden * hidden
    squares_ref[...] = jnp.broadcast_to(jnp.sum(squares, axis=1, keepdims=True), squares_ref.shape)


def policy(parts, raw, top, query, x, values):
    count, width = x.shape
    return kernel_call(
        policy_kernel,
        (array((count, width), jnp.bfloat16), array((count, LANES), jnp.float32)),
        [VMEM] * 9,
        scratch=[
            pltpu.VMEM((4, 4 * GROUP, LANES), jnp.float32),
            pltpu.VMEM((width // LANES, count, LANES), jnp.float32),
        ],
        flops=2 * raw.size * HEAD_DIM,
        moved=2 * values.size + 4 * raw.size,
        name="policy",
    )(*parts, raw, top, query, x, values)


def by_step_kernel(rows_ref, out_ref, wide_ref):
    for k in range(rows_ref.shape[1] // LANES):
        columns = pl.ds(k * LANES, LANES)
        wide_ref[k] = rows_ref[:, columns].astype(jnp.float32)
        for step in range(4):
            out_ref[step, :, columns] = wide_ref[k, pl.ds(step, 4, stride=4), :].astype(
                out_ref.dtype
            )


def by_step(rows):
    count, width = rows.shape
    return kernel_call(
        by_step_kernel,
        array((4, count // 4, width), rows.dtype),
        [VMEM],
        scratch=[pltpu.VMEM((width // LANES, count, LANES), jnp.float32)],
        moved=16 * rows.size,
        name="by_step",
    )(rows)


def squares_kernel(rows_ref, other_ref, _, out_ref):
    squares = jnp.zeros(out_ref.shape, jnp.float32)
    for k in range(rows_ref.shape[1] // LANES):
        part = rows_ref[:, pl.ds(k * LANES, LANES)].astype(jnp.float32)
        squares += part * part
    out_ref[...] = other_ref[...] + jnp.sum(squares, axis=1, keepdims=True)


def row_squares(rows, other, after):
    return kernel_call(
        squares_kernel,
        array(other.shape, jnp.float32),
        [VMEM, VMEM, pl.BlockSpec(memory_space=pl.ANY)],
        name="row_squares",
    )(rows, other, after)


def critic_scores_kernel(
    length_ref, rows_ref, gain_ref, keys_ref, raw_ref, top_ref, placed_ref
):
    for k in range(rows_ref.shape[1] // LANES):
        columns = pl.ds(k * LANES, LANES)
        gained = rows_ref[:, columns].astype(jnp.float32) * gain_ref[k : k + 1, :].astype(jnp.float32)
        head, group = divmod(k, GROUP)
        for row in range(4):
            placed_ref[4 * head + row, pl.ds(4 * group, 4), :] = gained[4 * row : 4 * row + 4]
    for at in range(placed_ref.shape[0]):
        head, row = divmod(at, 4)
        keys = keys_ref[row, :, pl.ds(head * HEAD_DIM, HEAD_DIM)]
        query = (placed_ref[at] * shrink).astype(jnp.bfloat16)
        masked_scores(query, keys, length_ref[row], raw_ref, top_ref, at)


def critic_scores(lengths, rows, gain, keys):
    heads = keys.shape[2] // HEAD_DIM
    placed = (4 * heads, 4 * GROUP, HEAD_DIM)
    raw = array(placed[:2] + (keys.shape[1],), jnp.float32)
    return kernel_call(
        critic_scores_kernel,
        (raw, array(placed, jnp.float32)),
        [SMEM] + [VMEM] * 3,
        scratch=[pltpu.VMEM(placed, jnp.float32)],
        flops=2 * raw.size * HEAD_DIM,
        moved=2 * keys.size + 4 * raw.size,
        name="critic_scores",
    )(lengths, rows, gain, keys)


def critic_kernel(
    near_ref,
    far_ref,
    raw_ref,
    top_ref,
    rows_ref,
    gain_ref,
    values_ref,
    head_ref,
    out_ref,
    spread_ref,
    attended_ref,
    scaled_ref,
):
    count, width = rows_ref.shape
    cache_size = values_ref.shape[1]
    inv = lax.rsqrt((near_ref[...] + far_ref[...]) * (1.0 / D) + norm_eps)
    spread_rows(inv * (attn_scale * log2_e / shrink), spread_ref)
    for at in range(raw_ref.shape[0]):
        head, row = divmod(at, 4)
        spread = spread_ref[row]
        weights = masked_weights(
            raw_ref[at],
            widened(spread, cache_size),
            widened(top_ref[at] * spread, cache_size),
        )
        inverse = 1.0 / jnp.sum(weights, axis=1, keepdims=True)
        attended = inverse * jnp.dot(
            weights.astype(jnp.bfloat16),
            values_ref[row, :, pl.ds(head * HEAD_DIM, HEAD_DIM)],
            preferred_element_type=jnp.float32,
        )
        for group in range(GROUP):
            attended_ref[head * GROUP + group, pl.ds(4 * row, 4), :] = attended[
                4 * group : 4 * group + 4
            ]
    squares = jnp.zeros((count, LANES), jnp.float32)
    for k in range(width // LANES):
        columns = pl.ds(k * LANES, LANES)
        combined = rows_ref[:, columns].astype(jnp.float32) + attended_ref[k]
        squares += combined * combined
        scaled_ref[:, columns] = (combined * gain_ref[k : k + 1, :].astype(jnp.float32)).astype(
            scaled_ref.dtype
        )
    logits = lax.dot_general(
        scaled_ref[...], head_ref[...], NT, preferred_element_type=jnp.float32
    )
    out_ref[...] = jnp.broadcast_to(jnp.sum(squares, axis=1, keepdims=True), (count, LANES))
    out_ref[:, :ATOMS] = logits


def critic(parts, raw, top, rows, gain, values, head):
    count, width = rows.shape
    return kernel_call(
        critic_kernel,
        array((count, LANES), jnp.float32),
        [VMEM] * 8,
        scratch=[
            pltpu.VMEM((4, 4 * GROUP, LANES), jnp.float32),
            pltpu.VMEM((width // LANES, count, LANES), jnp.float32),
            pltpu.VMEM((count, width), jnp.bfloat16),
        ],
        flops=2 * raw.size * HEAD_DIM,
        moved=2 * values.size + 4 * raw.size,
        name="critic",
    )(*parts, raw, top, rows, gain, values, head)


def expect_kernel(own_ref, one_ref, two_ref, three_ref, out_ref):
    total = own_ref[...] + (one_ref[...] + (two_ref[...] + three_ref[...]))
    lane = lax.broadcasted_iota(jnp.int32, total.shape, 1)
    at = lax.broadcasted_iota(jnp.int32, total.shape, 0)
    logits = lax.rsqrt(total[:, LANES - 1 :] * (1.0 / D) + norm_eps) * total
    real = lane < ATOMS
    logits = jnp.where(real, logits, masked)
    weights = jnp.exp(logits - jnp.max(logits, axis=1, keepdims=True))
    atoms = -atom_span + 2.0 * atom_span * lane.astype(jnp.float32) / (ATOMS - 1)
    value = jnp.sum(weights * atoms, axis=1, keepdims=True) / jnp.sum(
        weights, axis=1, keepdims=True
    )
    placed = jnp.where(lane == lax.shift_right_logical(at, 2), value, 0.0)
    rows = [
        jnp.sum(jnp.where(jnp.bitwise_and(at, 3) == step, placed, 0.0), axis=0, keepdims=True)
        for step in range(4)
    ]
    out_ref[...] = jnp.concatenate(rows, axis=0)[:, :4]


def expect(parts):
    return kernel_call(expect_kernel, array((4, 4), jnp.float32), [VMEM] * 4, name="expect")(*parts)


def swapped(shard, by):
    peers = lax.axis_size("tp")
    return lax.ppermute(shard, "tp", [(i, i ^ by) for i in range(peers)])


def passed_along(shard, axis, by):
    peers = lax.axis_size(axis)
    return lax.ppermute(shard, axis, [(i, (i + by) % peers) for i in range(peers)])


def crossed(shard, by_rows, by_tp):
    peers = lax.axis_size("tp")
    groups = lax.axis_size("rows")
    pairs = [
        (r * peers + t, (r + by_rows) % groups * peers + (t ^ by_tp))
        for r in range(groups)
        for t in range(peers)
    ]
    return lax.ppermute(shard, ("rows", "tp"), pairs)


def with_peers(shard):
    return [shard] + [swapped(shard, by) for by in (1, 2, 3)]


def on_device(
    tokens,
    lengths,
    embedding,
    attn_gain,
    key_weight,
    value_weight,
    policy_keys,
    policy_values,
    critic_lengths,
    critic_gain,
    critic_keys,
    critic_values,
    value_gain,
    value_head,
):
    row_groups = lax.axis_size("rows")

    def as_rows(gain):
        return gain.reshape(-1, LANES)

    table = embedding.transpose(1, 2, 0).reshape(embedding.shape[2], embedding.shape[0])
    all_tokens = lax.all_to_all(laid_out(tokens, row_groups), "rows", 0, 0)
    picked, early_values = pick_rows(all_tokens, table, value_weight)
    blocks = lax.all_to_all(picked.reshape(row_groups, -1, LANES), "rows", 0, 0)
    x, query, parts = project(
        blocks.reshape(picked.shape), as_rows(attn_gain), early_values, key_weight, value_weight
    )
    arrived = parts[:1] + [swapped(parts[by], by) for by in (1, 2, 3)]
    raw, top = policy_scores(lengths, query, policy_keys)
    passed, squares = policy(arrived, raw, top, query, x, policy_values)
    rows = passed_along(passed, "rows", row_groups // 2)
    squares = crossed(squares, row_groups // 2, 2)
    hidden = by_step(passed)

    raw, top = critic_scores(critic_lengths, rows, as_rows(critic_gain), critic_keys)
    near = row_squares(rows, squares, top)
    logits = critic(
        (near, swapped(near, 1)),
        raw,
        top,
        rows,
        as_rows(value_gain),
        critic_values,
        value_head.T,
    )
    values = expect(with_peers(logits))
    return hidden, values


def solution(mesh):
    placed = (
        P(None, "rows"),
        P("rows"),
        P(None, "rows", "tp"),
        P("tp"),
        P("tp", None),
        P("tp", None),
        P("rows", None, "tp"),
        P("rows", None, "tp"),
        P("rows"),
        P("tp"),
        P("rows", None, "tp"),
        P("rows", None, "tp"),
        P("tp"),
        P("tp", None),
    )
    return jax.shard_map(
        on_device,
        mesh=mesh,
        in_specs=placed,
        out_specs=(P(None, "rows", "tp"), P(None, "rows")),
        check_vma=False,
    )
```

```python
import functools
import math

import jax
import jax.numpy as jnp
from jax import lax
from jax.experimental import pallas as pl
from jax.experimental.pallas import tpu as pltpu
from jax.sharding import PartitionSpec as P

D = 8192
HEAD_DIM = 128
GROUP = 8
ATOMS = 51
LANES = 128
HALF = 64
MIB = 1024 * 1024

norm_eps = 1e-06
atom_span = 10.0
masked = -1e30
shrink = 2.0**-64
attn_scale = 1.0 / math.sqrt(HEAD_DIM)
log2_e = 1.0 / math.log(2.0)

SMEM = pl.BlockSpec(memory_space=pltpu.SMEM)
VMEM = pl.BlockSpec(memory_space=pltpu.VMEM)
HBM = pl.BlockSpec(memory_space=pltpu.HBM)
NT = (((1,), (1,)), ((), ()))


def kernel_call(body, outs, specs, scratch=(), limit=16, flops=0, moved=0, name=None):
    return pl.pallas_call(
        body,
        out_shape=outs,
        in_specs=specs,
        out_specs=tuple(VMEM for _ in outs) if isinstance(outs, tuple) else VMEM,
        scratch_shapes=scratch,
        compiler_params=pltpu.CompilerParams(vmem_limit_bytes=limit * MIB),
        cost_estimate=pl.CostEstimate(flops=flops, bytes_accessed=moved, transcendentals=0),
        name=name,
    )


def array(shape, dtype):
    return jax.ShapeDtypeStruct(shape, dtype)


def in_hbm(x):
    return pltpu.with_memory_space_constraint(x, pltpu.HBM)


def lay_out_kernel(token_ref, out_ref):
    row = jnp.concatenate([token_ref[step : step + 1, :] for step in range(4)], axis=1)
    out_ref[...] = jnp.broadcast_to(row[None], out_ref.shape)


def laid_out(tokens, copies):
    out = array((copies, 1, tokens.size), tokens.dtype)
    return kernel_call(lay_out_kernel, out, [VMEM], name="lay_out")(tokens)


def pick_rows_kernel(
    source_ref,
    table_ref,
    weight_ref,
    out_ref,
    early_ref,
    token_ref,
    tiles_ref,
    sems,
    early_sem,
    token_sem,
):
    early = pltpu.make_async_copy(
        weight_ref.at[pl.ds(0, early_ref.shape[0])], early_ref, early_sem
    )
    early.start()
    tokens = pltpu.make_async_copy(source_ref, token_ref, token_sem)
    tokens.start()
    tokens.wait()
    width = table_ref.shape[0]
    pieces = sems.shape[0]
    destinations = token_ref.shape[0] // pieces
    places = 8 * destinations
    lane = lax.broadcasted_iota(jnp.int32, (width, LANES), 1)

    def token_of(destination, i, half):
        m = 8 * half + i
        return token_ref[destination, 0, 4 * (m % 4) + m // 4]

    for piece in range(pieces):

        def fetch(at, carry):
            destination = piece * destinations + at
            for half in range(2):
                for i in range(8):
                    block = jnp.bitwise_and(token_of(destination, i, half), ~(LANES - 1))
                    pltpu.make_async_copy(
                        table_ref.at[:, pl.ds(pl.multiple_of(block, LANES), LANES)],
                        tiles_ref.at[half, 8 * destination + i],
                        sems.at[piece],
                    ).start()
            return carry

        lax.fori_loop(0, destinations, fetch, 0)

    empty = jnp.zeros((width, LANES), jnp.float32)
    pair = (empty, empty)
    for piece in range(pieces):
        part = tiles_ref.at[:, pl.ds(piece * places, places)]
        pltpu.make_async_copy(part, part, sems.at[piece]).wait()
        first_place = piece * places % LANES

        def step(at, carry):
            destination = piece * destinations + at
            pair = list(carry)
            for i in range(8):
                place = 8 * destination + i
                here = lane == first_place + 8 * at + i
                for half in range(2):
                    shift = jnp.bitwise_and(place - token_of(destination, i, half), LANES - 1)
                    tile = pltpu.roll(tiles_ref[half, place].astype(jnp.float32), shift, 1)
                    pair[half] = jnp.where(here, tile, pair[half])
            return tuple(pair)

        pair = lax.fori_loop(0, destinations, step, pair, unroll=min(destinations, 4))
        if first_place + places == LANES:
            both = jnp.concatenate(pair, axis=0)
            rows = pl.ds((piece + 1) * places - LANES, LANES)
            out_ref[rows, :] = both.T.astype(out_ref.dtype)
            pair = (empty, empty)
    early.wait()


def pick_rows(tokens, table, weight, pieces=8):
    width = table.shape[0]
    rows = tokens.size * width // LANES
    early = (weight.shape[0] * 3 // 4, weight.shape[1])
    return kernel_call(
        pick_rows_kernel,
        (array((rows, LANES), table.dtype), pltpu.VMEM(early, weight.dtype)),
        [VMEM, HBM, HBM],
        scratch=[
            pltpu.SMEM(tokens.shape, tokens.dtype),
            pltpu.VMEM((2, rows, width, LANES), table.dtype),
            pltpu.SemaphoreType.DMA((pieces,)),
            pltpu.SemaphoreType.DMA,
            pltpu.SemaphoreType.DMA,
        ],
        limit=24,
        name="pick_rows",
    )(tokens, in_hbm(table), in_hbm(weight))


def project_kernel(
    blocks_ref, gain_ref, early_ref, key_ref, value_ref, x_ref, query_ref, *rest
):
    parts = rest[:4]
    gained_ref, placed_ref, sums_ref, late_ref, keys_ref, sems = rest[4:]
    count, width = x_ref.shape
    kv_width = key_ref.shape[1] // 4
    tp = lax.axis_index("tp")
    early = early_ref.shape[0]
    chunk = width - early
    piece = chunk // 2
    copies = [pltpu.make_async_copy(value_ref.at[pl.ds(early, chunk)], late_ref, sems.at[0])]
    for at in range(width // piece):
        rows = pl.ds(at * piece, piece)
        copies.append(
            pltpu.make_async_copy(key_ref.at[rows], keys_ref.at[rows], sems.at[at + 1])
        )
    for copy in copies:
        copy.start(priority=1)
    left = lax.broadcasted_iota(jnp.int32, (8, LANES), 1) < HALF
    squares = jnp.zeros((count, LANES), jnp.float32)
    for k in range(width // LANES):
        pair = blocks_ref[pl.ds(16 * k, 16), :].astype(jnp.float32)
        one, two = pair[:8], pair[8:]
        low = jnp.where(left, one, pltpu.roll(two, HALF, 1))
        high = jnp.where(left, pltpu.roll(one, HALF, 1), two)
        x = jnp.concatenate([low, high], axis=0)
        squares += x * x
        columns = pl.ds(k * LANES, LANES)
        x_ref[:, columns] = x.astype(x_ref.dtype)
        gained = x * gain_ref[k : k + 1, :].astype(jnp.float32)
        gained_ref[:, columns] = gained.astype(gained_ref.dtype)
        head, group = divmod(k, GROUP)
        for row in range(4):
            placed_ref[4 * head + row, pl.ds(4 * group, 4), :] = gained[4 * row : 4 * row + 4]
    query_ref[...] = (placed_ref[...] * shrink).astype(query_ref.dtype)
    total = jnp.broadcast_to(jnp.sum(squares, axis=1, keepdims=True), (count, LANES))

    def product(rows, weight):
        return jnp.dot(gained_ref[:, rows], weight, preferred_element_type=jnp.float32)

    values = product(pl.ds(0, early), early_ref[...])
    copies[0].wait()
    sums_ref[1] = values + product(pl.ds(early, chunk), late_ref[...])
    keys = None
    for at in range(width // piece):
        rows = pl.ds(at * piece, piece)
        copies[at + 1].wait()
        partial = product(rows, keys_ref[rows, :])
        keys = partial if keys is None else keys + partial
    sums_ref[0] = keys
    head = total.astype(jnp.bfloat16)
    tail = jnp.where(total < 3e38, total - head.astype(jnp.float32), 0.0).astype(jnp.bfloat16)
    for by, part_ref in enumerate(parts):
        start = pl.multiple_of(jnp.bitwise_xor(tp, by) * kv_width, kv_width)
        peer = pl.ds(start, kv_width)
        part_ref[:, :kv_width] = sums_ref[0, :, peer].astype(part_ref.dtype)
        part_ref[:, kv_width : 2 * kv_width] = sums_ref[1, :, peer].astype(part_ref.dtype)
        if by == 0:
            part_ref[:, 2 * kv_width :] = total
        else:
            part_ref[:, 2 * kv_width : 2 * kv_width + LANES] = head
            part_ref[:, 2 * kv_width + LANES :] = tail


def project(blocks, gain, early_values, key_weight, value_weight):
    width, kv_all = key_weight.shape
    count = blocks.shape[0] * LANES // width
    early = early_values.shape[0]
    own = array((count, kv_all // 2 + LANES), jnp.float32)
    part = array((count, kv_all // 2 + 2 * LANES), jnp.bfloat16)
    heads = width // (GROUP * HEAD_DIM)
    queries = (4 * heads, 4 * GROUP, HEAD_DIM)
    x, query, *parts = kernel_call(
        project_kernel,
        (array((count, width), jnp.bfloat16), array(queries, jnp.bfloat16), own) + (part,) * 3,
        [VMEM] * 3 + [HBM] * 2,
        scratch=[
            pltpu.VMEM((count, width), jnp.bfloat16),
            pltpu.VMEM(queries, jnp.float32),
            pltpu.VMEM((2, count, kv_all), jnp.float32),
            pltpu.VMEM((width - early, kv_all), key_weight.dtype),
            pltpu.VMEM((width, kv_all), key_weight.dtype),
            pltpu.SemaphoreType.DMA((1 + 2 * width // (width - early),)),
        ],
        flops=4 * count * width * kv_all,
        moved=4 * width * kv_all,
        name="project",
    )(
        blocks,
        gain,
        early_values,
        in_hbm(key_weight),
        in_hbm(value_weight),
    )
    return x, query, parts


def masked_scores(query, keys, length, raw_ref, top_ref, at):
    raw = lax.dot_general(query, keys, NT, preferred_element_type=jnp.float32)
    visible = lax.broadcasted_iota(jnp.int32, raw.shape, 1) < length
    raw = jnp.where(visible, raw, masked)
    raw_ref[at] = raw
    top_ref[at] = jnp.broadcast_to(jnp.max(raw, axis=1, keepdims=True), top_ref.shape[1:])


def scores_kernel(length_ref, query_ref, keys_ref, raw_ref, top_ref):
    for at in range(query_ref.shape[0]):
        head, row = divmod(at, 4)
        keys = keys_ref[row, :, pl.ds(head * HEAD_DIM, HEAD_DIM)]
        masked_scores(query_ref[at], keys, length_ref[row], raw_ref, top_ref, at)


def policy_scores(lengths, query, keys):
    raw = array(query.shape[:2] + (keys.shape[1],), jnp.float32)
    return kernel_call(
        scores_kernel,
        (raw, array(query.shape, jnp.float32)),
        [SMEM, VMEM, VMEM],
        flops=2 * raw.size * HEAD_DIM,
        moved=2 * keys.size + 4 * raw.size,
        name="policy_scores",
    )(lengths, query, keys)


def spread_rows(inv, spread_ref):
    for row in range(4):
        for group in range(GROUP):
            spread_ref[row, pl.ds(4 * group, 4), :] = inv[4 * row : 4 * row + 4]


def widened(x, width):
    return jnp.concatenate([x] * (width // LANES), axis=1)


def masked_weights(raw, spread, highest):
    return jnp.where(raw > 0.5 * masked, jnp.exp2(raw * spread - highest), 0.0)


def policy_kernel(
    own_ref,
    one_ref,
    two_ref,
    three_ref,
    raw_ref,
    top_ref,
    query_ref,
    x_ref,
    values_ref,
    passed_ref,
    squares_ref,
    spread_ref,
    rows_ref,
):
    count, width = x_ref.shape
    kv_width = values_ref.shape[2]
    cache_size = values_ref.shape[1]
    total = own_ref[...]
    for part_ref in (one_ref, two_ref, three_ref):
        part = part_ref[...].astype(jnp.float32)
        squares = part[:, 2 * kv_width : 2 * kv_width + LANES] + part[:, 2 * kv_width + LANES :]
        total = total + jnp.concatenate([part[:, : 2 * kv_width], squares], axis=1)
    inv = lax.rsqrt(total[:, 2 * kv_width :] * (1.0 / D) + norm_eps)
    wide = widened(inv, kv_width)
    new_key = (wide * total[:, :kv_width]).astype(jnp.bfloat16)
    new_value = (wide * total[:, kv_width : 2 * kv_width]).astype(jnp.bfloat16)
    spread_rows(inv * (attn_scale * log2_e / shrink), spread_ref)
    queries = query_ref.shape[1]
    at_query = lax.broadcasted_iota(jnp.int32, (4 * queries, count), 0)
    at_fresh = lax.broadcasted_iota(jnp.int32, (4 * queries, count), 1)
    mine = jnp.logical_and(
        lax.div(at_query, queries) == lax.shift_right_logical(at_fresh, 2),
        jnp.bitwise_and(at_fresh, 3) <= jnp.bitwise_and(at_query, 3),
    )
    for head in range(query_ref.shape[0] // 4):
        columns = slice(head * HEAD_DIM, (head + 1) * HEAD_DIM)
        all_queries = query_ref[pl.ds(4 * head, 4)].reshape(4 * queries, HEAD_DIM)
        fresh = lax.dot_general(
            all_queries, new_key[:, columns], NT, preferred_element_type=jnp.float32
        )
        fresh = jnp.where(mine, fresh, masked)
        fresh_top = jnp.max(fresh, axis=1, keepdims=True)
        fresh_weights, attended, inverses = [], [], []
        for row in range(4):
            at = 4 * head + row
            part = slice(row * queries, (row + 1) * queries)
            spread = spread_ref[row]
            highest = jnp.maximum(top_ref[at], fresh_top[part]) * spread
            weights = masked_weights(
                raw_ref[at], widened(spread, cache_size), widened(highest, cache_size)
            )
            extra = masked_weights(fresh[part], spread[:, :count], highest[:, :count])
            inverses.append(
                1.0
                / (jnp.sum(weights, axis=1, keepdims=True) + jnp.sum(extra, axis=1, keepdims=True))
            )
            fresh_weights.append(extra)
            attended.append(
                jnp.dot(
                    weights.astype(jnp.bfloat16),
                    values_ref[row, :, columns],
                    preferred_element_type=jnp.float32,
                )
            )
        fresh_weights = jnp.concatenate(fresh_weights, axis=0).astype(jnp.bfloat16)
        fresh_sum = jnp.dot(
            fresh_weights, new_value[:, columns], preferred_element_type=jnp.float32
        )
        for row in range(4):
            part = slice(row * queries, (row + 1) * queries)
            both = (attended[row] + fresh_sum[part]) * inverses[row]
            for group in range(GROUP):
                rows_ref[head * GROUP + group, pl.ds(4 * row, 4), :] = both[
                    4 * group : 4 * group + 4
                ]
    squares = jnp.zeros((count, LANES), jnp.float32)
    for k in range(width // LANES):
        columns = pl.ds(k * LANES, LANES)
        hidden = (x_ref[:, columns].astype(jnp.float32) + rows_ref[k]).astype(passed_ref.dtype)
        passed_ref[:, columns] = hidden
        hidden = hidden.astype(jnp.float32)
        squares += hidden * hidden
    squares_ref[...] = jnp.broadcast_to(jnp.sum(squares, axis=1, keepdims=True), squares_ref.shape)


def policy(parts, raw, top, query, x, values):
    count, width = x.shape
    return kernel_call(
        policy_kernel,
        (array((count, width), jnp.bfloat16), array((count, LANES), jnp.float32)),
        [VMEM] * 9,
        scratch=[
            pltpu.VMEM((4, 4 * GROUP, LANES), jnp.float32),
            pltpu.VMEM((width // LANES, count, LANES), jnp.float32),
        ],
        flops=2 * raw.size * HEAD_DIM,
        moved=2 * values.size + 4 * raw.size,
        name="policy",
    )(*parts, raw, top, query, x, values)


def by_step_kernel(rows_ref, out_ref, wide_ref):
    for k in range(rows_ref.shape[1] // LANES):
        columns = pl.ds(k * LANES, LANES)
        wide_ref[k] = rows_ref[:, columns].astype(jnp.float32)
        for step in range(4):
            out_ref[step, :, columns] = wide_ref[k, pl.ds(step, 4, stride=4), :].astype(
                out_ref.dtype
            )


def by_step(rows):
    count, width = rows.shape
    return kernel_call(
        by_step_kernel,
        array((4, count // 4, width), rows.dtype),
        [VMEM],
        scratch=[pltpu.VMEM((width // LANES, count, LANES), jnp.float32)],
        moved=16 * rows.size,
        name="by_step",
    )(rows)


def squares_kernel(rows_ref, other_ref, _, out_ref):
    squares = jnp.zeros(out_ref.shape, jnp.float32)
    for k in range(rows_ref.shape[1] // LANES):
        part = rows_ref[:, pl.ds(k * LANES, LANES)].astype(jnp.float32)
        squares += part * part
    out_ref[...] = other_ref[...] + jnp.sum(squares, axis=1, keepdims=True)


def row_squares(rows, other, after):
    return kernel_call(
        squares_kernel,
        array(other.shape, jnp.float32),
        [VMEM, VMEM, pl.BlockSpec(memory_space=pl.ANY)],
        name="row_squares",
    )(rows, other, after)


def critic_scores_kernel(
    length_ref, rows_ref, gain_ref, keys_ref, raw_ref, top_ref, placed_ref
):
    for k in range(rows_ref.shape[1] // LANES):
        columns = pl.ds(k * LANES, LANES)
        gained = rows_ref[:, columns].astype(jnp.float32) * gain_ref[k : k + 1, :].astype(jnp.float32)
        head, group = divmod(k, GROUP)
        for row in range(4):
            placed_ref[4 * head + row, pl.ds(4 * group, 4), :] = gained[4 * row : 4 * row + 4]
    for at in range(placed_ref.shape[0]):
        head, row = divmod(at, 4)
        keys = keys_ref[row, :, pl.ds(head * HEAD_DIM, HEAD_DIM)]
        query = (placed_ref[at] * shrink).astype(jnp.bfloat16)
        masked_scores(query, keys, length_ref[row], raw_ref, top_ref, at)


def critic_scores(lengths, rows, gain, keys):
    heads = keys.shape[2] // HEAD_DIM
    placed = (4 * heads, 4 * GROUP, HEAD_DIM)
    raw = array(placed[:2] + (keys.shape[1],), jnp.float32)
    return kernel_call(
        critic_scores_kernel,
        (raw, array(placed, jnp.float32)),
        [SMEM] + [VMEM] * 3,
        scratch=[pltpu.VMEM(placed, jnp.float32)],
        flops=2 * raw.size * HEAD_DIM,
        moved=2 * keys.size + 4 * raw.size,
        name="critic_scores",
    )(lengths, rows, gain, keys)


def critic_kernel(
    near_ref,
    far_ref,
    raw_ref,
    top_ref,
    rows_ref,
    gain_ref,
    values_ref,
    head_ref,
    out_ref,
    spread_ref,
    attended_ref,
    scaled_ref,
):
    count, width = rows_ref.shape
    cache_size = values_ref.shape[1]
    inv = lax.rsqrt((near_ref[...] + far_ref[...]) * (1.0 / D) + norm_eps)
    spread_rows(inv * (attn_scale * log2_e / shrink), spread_ref)
    for at in range(raw_ref.shape[0]):
        head, row = divmod(at, 4)
        spread = spread_ref[row]
        weights = masked_weights(
            raw_ref[at],
            widened(spread, cache_size),
            widened(top_ref[at] * spread, cache_size),
        )
        inverse = 1.0 / jnp.sum(weights, axis=1, keepdims=True)
        attended = inverse * jnp.dot(
            weights.astype(jnp.bfloat16),
            values_ref[row, :, pl.ds(head * HEAD_DIM, HEAD_DIM)],
            preferred_element_type=jnp.float32,
        )
        for group in range(GROUP):
            attended_ref[head * GROUP + group, pl.ds(4 * row, 4), :] = attended[
                4 * group : 4 * group + 4
            ]
    squares = jnp.zeros((count, LANES), jnp.float32)
    for k in range(width // LANES):
        columns = pl.ds(k * LANES, LANES)
        combined = rows_ref[:, columns].astype(jnp.float32) + attended_ref[k]
        squares += combined * combined
        scaled_ref[:, columns] = (combined * gain_ref[k : k + 1, :].astype(jnp.float32)).astype(
            scaled_ref.dtype
        )
    logits = lax.dot_general(
        scaled_ref[...], head_ref[...], NT, preferred_element_type=jnp.float32
    )
    out_ref[...] = jnp.broadcast_to(jnp.sum(squares, axis=1, keepdims=True), (count, LANES))
    out_ref[:, :ATOMS] = logits


def critic(parts, raw, top, rows, gain, values, head):
    count, width = rows.shape
    return kernel_call(
        critic_kernel,
        array((count, LANES), jnp.float32),
        [VMEM] * 8,
        scratch=[
            pltpu.VMEM((4, 4 * GROUP, LANES), jnp.float32),
            pltpu.VMEM((width // LANES, count, LANES), jnp.float32),
            pltpu.VMEM((count, width), jnp.bfloat16),
        ],
        flops=2 * raw.size * HEAD_DIM,
        moved=2 * values.size + 4 * raw.size,
        name="critic",
    )(*parts, raw, top, rows, gain, values, head)


def expect_kernel(own_ref, one_ref, two_ref, three_ref, out_ref):
    total = own_ref[...] + (one_ref[...] + (two_ref[...] + three_ref[...]))
    lane = lax.broadcasted_iota(jnp.int32, total.shape, 1)
    at = lax.broadcasted_iota(jnp.int32, total.shape, 0)
    logits = lax.rsqrt(total[:, LANES - 1 :] * (1.0 / D) + norm_eps) * total
    real = lane < ATOMS
    logits = jnp.where(real, logits, masked)
    weights = jnp.exp(logits - jnp.max(logits, axis=1, keepdims=True))
    atoms = -atom_span + 2.0 * atom_span * lane.astype(jnp.float32) / (ATOMS - 1)
    value = jnp.sum(weights * atoms, axis=1, keepdims=True) / jnp.sum(
        weights, axis=1, keepdims=True
    )
    placed = jnp.where(lane == lax.shift_right_logical(at, 2), value, 0.0)
    rows = [
        jnp.sum(jnp.where(jnp.bitwise_and(at, 3) == step, placed, 0.0), axis=0, keepdims=True)
        for step in range(4)
    ]
    out_ref[...] = jnp.concatenate(rows, axis=0)[:, :4]


def expect(parts):
    return kernel_call(expect_kernel, array((4, 4), jnp.float32), [VMEM] * 4, name="expect")(*parts)


def swapped(shard, by):
    peers = lax.axis_size("tp")
    return lax.ppermute(shard, "tp", [(i, i ^ by) for i in range(peers)])


def passed_along(shard, axis, by):
    peers = lax.axis_size(axis)
    return lax.ppermute(shard, axis, [(i, (i + by) % peers) for i in range(peers)])


def crossed(shard, by_rows, by_tp):
    peers = lax.axis_size("tp")
    groups = lax.axis_size("rows")
    pairs = [
        (r * peers + t, (r + by_rows) % groups * peers + (t ^ by_tp))
        for r in range(groups)
        for t in range(peers)
    ]
    return lax.ppermute(shard, ("rows", "tp"), pairs)


def with_peers(shard):
    return [shard] + [swapped(shard, by) for by in (1, 2, 3)]


def on_device(
    tokens,
    lengths,
    embedding,
    attn_gain,
    key_weight,
    value_weight,
    policy_keys,
    policy_values,
    critic_lengths,
    critic_gain,
    critic_keys,
    critic_values,
    value_gain,
    value_head,
):
    row_groups = lax.axis_size("rows")

    def as_rows(gain):
        return gain.reshape(-1, LANES)

    table = embedding.transpose(1, 2, 0).reshape(embedding.shape[2], embedding.shape[0])
    all_tokens = lax.all_to_all(laid_out(tokens, row_groups), "rows", 0, 0)
    picked, early_values = pick_rows(all_tokens, table, value_weight)
    blocks = lax.all_to_all(picked.reshape(row_groups, -1, LANES), "rows", 0, 0)
    x, query, parts = project(
        blocks.reshape(picked.shape), as_rows(attn_gain), early_values, key_weight, value_weight
    )
    arrived = parts[:1] + [swapped(parts[by], by) for by in (1, 2, 3)]
    raw, top = policy_scores(lengths, query, policy_keys)
    passed, squares = policy(arrived, raw, top, query, x, policy_values)
    rows = passed_along(passed, "rows", row_groups // 2)
    squares = crossed(squares, row_groups // 2, 2)
    hidden = by_step(passed)

    raw, top = critic_scores(critic_lengths, rows, as_rows(critic_gain), critic_keys)
    near = row_squares(rows, squares, top)
    logits = critic(
        (near, swapped(near, 1)),
        raw,
        top,
        rows,
        as_rows(value_gain),
        critic_values,
        value_head.T,
    )
    values = expect(with_peers(logits))
    return hidden, values


def solution(mesh):
    placed = (
        P(None, "rows"),
        P("rows"),
        P(None, "rows", "tp"),
        P("tp"),
        P("tp", None),
        P("tp", None),
        P("rows", None, "tp"),
        P("rows", None, "tp"),
        P("rows"),
        P("tp"),
        P("rows", None, "tp"),
        P("rows", None, "tp"),
        P("tp"),
        P("tp", None),
    )
    return jax.shard_map(
        on_device,
        mesh=mesh,
        in_specs=placed,
        out_specs=(P(None, "rows", "tp"), P(None, "rows")),
        check_vma=False,
    )
```
